32 devices in a mesh: seq: 8 (over z, x), mp: 4 (over y, core).
Axes of the slice: x: 2, y: 2, z: 4, core: 2. Of those that a mesh axis runs over, the one named last changes fastest.
Arguments:
- tokens: bfloat16 [2, 4096, 512], P(None, 'seq'), may hold values from -6 to 6
- lengths: int32 [2], replicated, may hold values from 1024 to 4096, as said below
- norm_attn: bfloat16 [2, 512], P(None, 'seq'), may hold values from 0.5 to 1.5
- norm_ffn: bfloat16 [2, 512], P(None, 'seq'), may hold values from 0.5 to 1.5
- w_qkv: bfloat16 [2, 512, 3, 512], P(None, 'seq', None, 'mp'), may hold values from -0.25 to 0.25
- w_ctrl: bfloat16 [2, 512, 512], P(None, 'seq', 'mp'), may hold values from -1 to 1
- w_out: bfloat16 [2, 512, 512], P(None, 'seq', 'mp'), may hold values from -1 to 1
- w_up: bfloat16 [2, 512, 2048], P(None, 'seq', 'mp'), may hold values from -0.25 to 0.25
- w_down: bfloat16 [2, 512, 2048], P(None, 'seq', 'mp'), may hold values from -0.125 to 0.125
- cotangent: bfloat16 [2, 4096, 512], P(None, 'seq'), may hold values from -6 to 6
Outputs:
- mixed: bfloat16 [2, 4096, 512], P(None, 'seq')
- grad_tokens: float32 [2, 4096, 512], P(None, 'seq')
- grad_norm_attn: float32 [2, 512], P(None, 'seq')
- grad_norm_ffn: float32 [2, 512], P(None, 'seq')
- grad_qkv: float32 [2, 512, 3, 512], P(None, 'seq', None, 'mp')
- grad_ctrl: float32 [2, 512, 512], P(None, 'seq', 'mp')
- grad_out: float32 [2, 512, 512], P(None, 'seq', 'mp')
- grad_up: float32 [2, 512, 2048], P(None, 'seq', 'mp')
- grad_down: float32 [2, 512, 2048], P(None, 'seq', 'mp')
The draws below stay inside these ranges and needn't reach their ends.
Inputs may be any that keep to these rules, and one draw needn't show every extreme that they name: The valid tokens of sequence b are its first lengths[b]; one sequence, which one drawn from the seed, has exactly 4096.
All inputs are finite; a program needn't handle non-finite values.
Results may differ from the reference program's by a relative error of at most 0.018.
Values may be sent and summed in bfloat16 or wider, within the bound.
A program may use at most 192 MiB of HBM per device.

```python
import math
import jax
import jax.numpy as jnp
from jax import lax

D = 512
HEAD_DIM = 64
SLOTS = 64
FF = 2048
LAYERS = 2
SEQS = 2
LEN = 4096


def draw_lengths(key, part):
    length_key = jax.random.fold_in(key, 11)
    pick_key = jax.random.fold_in(key, 23)
    drawn_lengths = jax.random.randint(length_key, (SEQS,), LEN // 4, LEN + 1)
    chosen = jax.random.randint(pick_key, (), 0, SEQS)
    return jnp.where(jnp.arange(SEQS) == chosen, LEN, drawn_lengths).astype(jnp.int32)


def shard_levels(own_key, dims, pieces, smallest, largest):
    level, own = 1.0, jax.random.fold_in(own_key, 6)
    for axis_at, blocks in pieces:
        steps = jnp.exp(jax.random.uniform(jax.random.fold_in(own, axis_at), (blocks,), jnp.float32, smallest / len(pieces), largest / len(pieces)))
        level = level * jnp.repeat(steps, dims[axis_at] // blocks).reshape([-1 if axis == axis_at else 1 for axis in range(len(dims))])
    return level


def centred(own_key, extent, scale, most, shards=(), held_as=jnp.bfloat16):
    entries = jax.random.normal(own_key, extent, jnp.float32) * scale
    if len(shards) > 0:
        entries = shard_levels(own_key, extent, shards, -0.22, 0.18) * entries
    return jnp.clip(entries, min=-most, max=most).astype(held_as)


def setup_inputs(seed: int = 0) -> dict:
    key_of = jax.random.split(jax.random.key(seed), 11)
    tokens = centred(key_of[0], (SEQS, LEN, D), 1.0, 6.0, ((1, 8),))
    lengths = draw_lengths(jax.random.fold_in(key_of[10], 71), 0)
    norm_attn = jnp.clip(1.0 + 0.1 * jax.random.normal(key_of[2], (LAYERS, D), jnp.float32), 0.5, 1.5).astype(jnp.bfloat16)
    norm_ffn = jnp.clip(1.0 + 0.1 * jax.random.normal(key_of[3], (LAYERS, D), jnp.float32), 0.5, 1.5).astype(jnp.bfloat16)
    w_qkv = centred(key_of[4], (LAYERS, D, 3, D), D ** -0.5, 0.25, ((1, 8), (3, 4)))
    w_ctrl = centred(key_of[5], (LAYERS, D, D), (D // 16) ** -0.5, 1.0, ((1, 8), (2, 4)))
    w_out = centred(key_of[6], (LAYERS, D, D), (D // 16) ** -0.5, 1.0, ((1, 8), (2, 4)))
    w_up = centred(key_of[7], (LAYERS, D, FF), D ** -0.5, 0.25, ((1, 8), (2, 4)))
    w_down = centred(key_of[8], (LAYERS, D, FF), FF ** -0.5, 0.125, ((1, 8), (2, 4)))
    cotangent = centred(key_of[9], (SEQS, LEN, D), 1.0, 6.0, ((1, 8),))
    return dict(tokens=tokens, lengths=lengths, norm_attn=norm_attn, norm_ffn=norm_ffn, w_qkv=w_qkv, w_ctrl=w_ctrl, w_out=w_out, w_up=w_up, w_down=w_down, cotangent=cotangent)


precise = lax.Precision.HIGHEST
epsilon = 1e-05

@jax.custom_vjp
def low(v):
    return lax.optimization_barrier(v.astype(jnp.bfloat16)).astype(jnp.float32)

@jax.custom_vjp
def low_back(v):
    return v

def low_keep(v):
    return (low(v), None)

def low_pass(kept, grad):
    return (grad,)

def back_keep(v):
    return (v, None)

def back_low(kept, grad):
    return (low(grad),)
low.defvjp(low_keep, low_pass)
low_back.defvjp(back_keep, back_low)

def normed(stream):
    center = stream - lax.optimization_barrier(jnp.mean(stream, axis=-1, keepdims=True))
    spread = lax.optimization_barrier(jnp.mean(center * center, axis=-1, keepdims=True))
    return center * lax.rsqrt(spread + epsilon)

def smooth_gate(hidden):
    return 0.5 * hidden * (1.0 + jnp.tanh(0.7978845608 * (hidden + 0.044715 * hidden * hidden * hidden)))

def slot_block(carry, block):
    key_state, value_state, total_state = carry
    queries, key_rows, value_rows, writes = block
    block_size = queries.shape[1]
    causal = jnp.tril(jnp.ones((block_size, block_size), jnp.float32))
    totals = total_state[:, None] + jnp.cumsum(writes, axis=1)
    affinity = jnp.einsum('bthe,buhe->bhtu', queries, key_rows, precision=precise) * causal
    numerator = jnp.einsum('bhtu,buhs->bths', affinity, writes, precision=precise)
    numerator = numerator + jnp.einsum('bthe,bhse->bths', queries, key_state, precision=precise)
    scores = numerator / (totals * math.sqrt(queries.shape[-1]))
    shifted = jnp.exp(scores - lax.optimization_barrier(jnp.max(scores, axis=-1, keepdims=True)))
    attention = shifted / lax.optimization_barrier(jnp.sum(shifted, axis=-1, keepdims=True))
    scaled = attention / totals
    mixing = jnp.einsum('bths,buhs->bhtu', scaled, writes, precision=precise) * causal
    mixed_rows = jnp.einsum('bhtu,buhe->bthe', mixing, value_rows, precision=precise)
    mixed_rows = mixed_rows + jnp.einsum('bths,bhse->bthe', scaled, value_state, precision=precise)
    key_state = key_state + jnp.einsum('buhs,buhe->bhse', writes, key_rows, precision=precise)
    value_state = value_state + jnp.einsum('buhs,buhe->bhse', writes, value_rows, precision=precise)
    total_state = total_state + lax.optimization_barrier(jnp.sum(writes, axis=1))
    return ((key_state, value_state, total_state), mixed_rows)

def slot_mixer(queries, key_rows, value_rows, writes):
    batch_size, seq_length, head_count, head_width = queries.shape
    slot_count = writes.shape[-1]
    block_size = math.gcd(seq_length, 512)
    block_count = seq_length // block_size

    def blocks(array):
        return jnp.swapaxes(array.reshape(batch_size, block_count, block_size, head_count, array.shape[-1]), 0, 1)
    initial = (jnp.zeros((batch_size, head_count, slot_count, head_width), jnp.float32), jnp.zeros((batch_size, head_count, slot_count, head_width), jnp.float32), jnp.zeros((batch_size, head_count, slot_count), jnp.float32))
    final_state, mixed_rows = lax.scan(jax.checkpoint(slot_block), initial, (blocks(queries), blocks(key_rows), blocks(value_rows), blocks(writes)))
    return jnp.swapaxes(mixed_rows, 0, 1).reshape(batch_size, seq_length, head_count, head_width)

def block_layer(stream, gain_attn, gain_ffn, mat_qkv, mat_ctrl, mat_out, mat_up, mat_down):
    batch_size, seq_length, model_width = stream.shape
    head_count = model_width // HEAD_DIM
    attn_in = low(normed(stream) * gain_attn)
    projected = low_back(jnp.einsum('btd,dkc->btkc', attn_in, mat_qkv, precision=precise))
    queries = low(projected[:, :, 0]).reshape(batch_size, seq_length, head_count, HEAD_DIM)
    key_rows = low(projected[:, :, 1]).reshape(batch_size, seq_length, head_count, HEAD_DIM)
    value_rows = low(projected[:, :, 2]).reshape(batch_size, seq_length, head_count, HEAD_DIM)
    control = low_back(jnp.einsum('btd,dc->btc', attn_in, mat_ctrl, precision=precise))
    writes = jnp.exp(16.0 * jnp.tanh(control / 16.0)).reshape(batch_size, seq_length, head_count, SLOTS)
    mixed_rows = low(slot_mixer(queries, key_rows, value_rows, writes).reshape(batch_size, seq_length, model_width))
    middle = stream + low_back(jnp.einsum('btc,dc->btd', mixed_rows, mat_out, precision=precise))
    ffn_in = low(normed(middle) * gain_ffn)
    hidden = low_back(jnp.einsum('btd,df->btf', ffn_in, mat_up, precision=precise))
    gated = low(smooth_gate(hidden))
    return middle + low_back(jnp.einsum('btf,df->btd', gated, mat_down, precision=precise))

def reference(tokens, lengths, norm_attn, norm_ffn, w_qkv, w_ctrl, w_out, w_up, w_down, cotangent):
    positions = jnp.arange(LEN, dtype=jnp.int32)
    valid_rows = (positions[None, :] < lengths[:, None].astype(jnp.int32)).astype(jnp.float32)[:, :, None]

    def forward(stream, gains_attn, gains_ffn, mats_qkv, mats_ctrl, mats_out, mats_up, mats_down):
        for layer_index in range(LAYERS):
            stream = jax.checkpoint(block_layer)(stream, gains_attn[layer_index], gains_ffn[layer_index], mats_qkv[layer_index], mats_ctrl[layer_index], mats_out[layer_index], mats_up[layer_index], mats_down[layer_index])
        return stream * valid_rows
    outputs, pullback = jax.vjp(forward, tokens.astype(jnp.float32), norm_attn.astype(jnp.float32), norm_ffn.astype(jnp.float32), w_qkv.astype(jnp.float32), w_ctrl.astype(jnp.float32), w_out.astype(jnp.float32), w_up.astype(jnp.float32), w_down.astype(jnp.float32))
    grads = pullback(cotangent.astype(jnp.float32))
    return (outputs.astype(jnp.bfloat16), grads[0], grads[1], grads[2], grads[3], grads[4], grads[5], grads[6], grads[7])
```

```python
import functools

import jax
import jax.numpy as jnp
from jax import lax
from jax.experimental import pallas as pl
from jax.experimental.pallas import tpu as pltpu
from jax.sharding import PartitionSpec as P

F32 = jnp.float32
BF = jnp.bfloat16
MESH = pl.DeviceIdType.MESH
GROUPS = 8
HEAD = 64
EPS = 1e-05
TILE = 256


def nn(a, b):
    return lax.dot_general(a, b, (((1,), (0,)), ((), ())), preferred_element_type=F32)


def nt(a, b):
    return lax.dot_general(a, b, (((1,), (1,)), ((), ())), preferred_element_type=F32)


def tn(a, b):
    return lax.dot_general(a, b, (((0,), (0,)), ((), ())), preferred_element_type=F32)


def norm_parts(x):
    center = x - jnp.mean(x, axis=-1, keepdims=True)
    spread = jnp.mean(center * center, axis=-1, keepdims=True)
    rstd = lax.rsqrt(spread + EPS)
    return center * rstd, rstd


def gate_and_slope(u):
    t = jnp.tanh(0.7978845608 * (u + 0.044715 * u * u * u))
    half = 0.5 * (1.0 + t)
    slope = half + 0.5 * u * (1.0 - t * t) * (0.7978845608 * (1.0 + 3.0 * 0.044715 * u * u))
    return u * half, slope


def kernel(
    n_seq,
    layers,
    tok_hbm,
    cot_hbm,
    len_ref,
    wa_hbm,
    wf_hbm,
    gain_ref,
    mixed_hbm,
    gt_hbm,
    ga_hbm,
    gf_hbm,
    gn_hbm,
    H,
    MID,
    AB,
    FB,
    QKV,
    WB,
    S2,
    ZS,
    PS,
    XS,
    AST,
    MST,
    OB,
    GU,
    GG,
    KP,
    VP,
    LOC,
    TOKB,
    GBF,
    DOB,
    DU,
    DMID,
    YST,
    DNB,
    RB,
    DZ,
    DWF,
    WA,
    WF,
    GAIN,
    GFULL,
    ARS,
    ARR,
    SCS,
    SCR1,
    SCR2,
    SCP,
    GA,
    GF,
    GAX,
    GAZ,
    GAY,
    GFY,
    GFX,
    GFZ,
    GAO,
    GFO,
    GN,
    GNY,
    GNR,
    GNO,
    OUTB,
    send_sems,
    recv_sems,
    local_sems,
):
    T, D = TOKB.shape[1], TOKB.shape[2]
    tiles = T // TILE
    R = D // GROUPS
    stride = n_seq // GROUPS
    s = lax.axis_index("seq")
    m = lax.axis_index("mp")
    y, core = m // 2, m % 2
    g, lo = s // stride, s % stride
    x, z = g % 2, g // 2
    z1, z0 = z // 2, z % 2

    def flip_z(d):
        d1, d0 = d // 2, d % 2
        return 2 * (1 - z1 if d1 else z1) + (1 - z0 if d0 else z0)

    def seq_of(gx, gz):
        return (gz * 2 + gx) * stride + lo

    def group_of(gx, gz):
        return gz * 2 + gx

    core_peer = (s, 2 * y + (1 - core))
    y_peer = (s, 2 * (1 - y) + core)
    x_peer = (seq_of(1 - x, z), m)
    z_peer = {d: (seq_of(x, flip_z(d)), m) for d in (1, 2, 3)}
    pairs = n_seq // 2
    low, high = s % 2, s // 2
    pair_peer = (s - low + (1 - low), m)

    used = [0, 0]

    def remote(src, dst, peer):
        k = used[0]
        used[0] += 1
        return pltpu.make_async_remote_copy(
            src_ref=src,
            dst_ref=dst,
            send_sem=send_sems.at[k],
            recv_sem=recv_sems.at[k],
            device_id=peer,
            device_id_type=MESH,
        )

    def local(src, dst):
        k = used[1]
        used[1] += 1
        c = pltpu.make_async_copy(src, dst, local_sems.at[k])
        c.start()
        return c

    sent = []

    barrier = pltpu.get_barrier_semaphore()

    def hello(peer):
        pl.semaphore_signal(barrier, inc=1, device_id=peer, device_id_type=MESH)

    hello(core_peer)
    hello(y_peer)
    hello(pair_peer)
    count = 3
    for d in range(1, pairs):
        other = lax.rem(high + d, pairs) * 2
        hello((other + low, m))
        count += 1
        if stride == 1:
            hello((other + 1 - low, m))
            count += 1

    tok_copy = local(tok_hbm.at[y], TOKB.at[0])
    cot_copy = local(cot_hbm.at[y], TOKB.at[1])
    own = []
    rows_own = pl.ds(pl.multiple_of(g * R, R), R)
    for l in range(layers):
        own.append(local(wa_hbm.at[l], WA.at[l, y, rows_own]))
        own.append(local(wf_hbm.at[l], WF.at[l, y, rows_own]))
    GAIN[0] = gain_ref[...]

    pl.semaphore_wait(barrier, count)

    def rows_at(gx, gz):
        return pl.ds(pl.multiple_of(group_of(gx, gz) * R, R), R)

    def region(buf, l, other_y, other_x, d):
        yy = 1 - y if other_y else y
        xx = 1 - x if other_x else x
        zz = flip_z(d)
        return buf.at[l, yy, rows_at(xx, zz)]

    class Shift:
        def __init__(self, buf, l):
            self.buf, self.l = buf, l
            self.arrivals = {}

        def push(self, mine, peer, key, arriving):
            src = region(self.buf, self.l, *mine)
            c = remote(src, src, peer)
            c.start()
            sent.append(c)
            self.arrivals[key] = (c, arriving)

        def take(self, key):
            c, arriving = self.arrivals[key]
            c.wait_recv()

    def mixer_start(l):
        f = Shift(WA, l)
        f.push((0, 0, 0), y_peer, ("y",), None)
        for d in (1, 2, 3):
            f.push((0, 0, d * 0), z_peer[d], ("z", 0, d), None)
        f.push((0, 0, 0), x_peer, ("x", 0, 0), None)
        return f

    def mixer_forward_1(f):
        f.take(("y",))
        for d in (1, 2, 3):
            f.push((1, 0, 0), z_peer[d], ("z", 1, d), None)
        f.push((1, 0, 0), x_peer, ("x", 1, 0), None)

    def mixer_forward_2(f):
        for d in (1, 2, 3):
            for o in (0, 1):
                f.take(("z", o, d))
                f.push((o, 0, d), x_peer, ("x", o, d), None)

    def mixer_done(f):
        for o in (0, 1):
            for d in range(4):
                f.take(("x", o, d))

    def ffn_start(l):
        f = Shift(WF, l)
        for d in (1, 2, 3):
            f.push((0, 0, 0), z_peer[d], ("z", d), None)
        f.push((0, 0, 0), x_peer, ("x", 0), None)
        f.push((0, 0, 0), y_peer, ("y", 0, 0), None)
        return f

    def ffn_forward_1(f):
        for d in (1, 2, 3):
            f.take(("z", d))
            f.push((0, 0, d), x_peer, ("x", d), None)
            f.push((0, 0, d), y_peer, ("y", 0, d), None)

    def ffn_forward_2(f):
        for d in range(4):
            f.take(("x", d))
            f.push((0, 1, d), y_peer, ("y", 1, d), None)

    def ffn_done(f):
        for o in (0, 1):
            for d in range(4):
                f.take(("y", o, d))

    gain_in = []
    for d in (0, 1, 2, 3):
        for o in (0, 1):
            if (d, o) == (0, 0):
                continue
            k = d * 2 + o
            peer = (seq_of(1 - x if o else x, flip_z(d)), m)
            c = remote(GAIN.at[0], GAIN.at[k], peer)
            c.start()
            sent.append(c)
            gain_in.append(c)
    for c in own:
        c.wait()
    mixer = [mixer_start(0)]
    ffn = [ffn_start(0)]

    lane = lax.broadcasted_iota(jnp.int32, (TILE, 128), 1)
    first = lane < HEAD
    head_rows = [
        (lax.broadcasted_iota(jnp.int32, (1, 128), 1) < HEAD).astype(F32).astype(BF),
        (lax.broadcasted_iota(jnp.int32, (1, 128), 1) >= HEAD).astype(F32).astype(BF),
    ]
    rr = lax.broadcasted_iota(jnp.int32, (TILE, TILE), 0)
    cc = lax.broadcasted_iota(jnp.int32, (TILE, TILE), 1)
    lower = rr >= cc
    lower_ones = lower.astype(F32).astype(BF)
    upper_ones = (rr <= cc).astype(F32).astype(BF)
    diag = (lax.broadcasted_iota(jnp.int32, (128, 128), 0) < HEAD) == (
        lax.broadcasted_iota(jnp.int32, (128, 128), 1) < HEAD
    )

    def per_head(value):
        a = jnp.sum(jnp.where(first, value, 0.0), axis=-1, keepdims=True)
        b = jnp.sum(jnp.where(first, 0.0, value), axis=-1, keepdims=True)
        return jnp.where(first, a, b)

    def per_head_max(value):
        a = jnp.max(jnp.where(first, value, -jnp.inf), axis=-1, keepdims=True)
        b = jnp.max(jnp.where(first, -jnp.inf, value), axis=-1, keepdims=True)
        return jnp.where(first, a, b)

    def heads(value):
        return value * head_rows[0], value * head_rows[1]

    def tile_rows(i):
        return pl.ds(i * TILE, TILE)

    ar_used = [0]
    ar_prev = {}

    def share_start(i, value):
        k = ar_used[0]
        ar_used[0] += 1
        slot = k % ARS.shape[0]
        if slot in ar_prev:
            ar_prev[slot].wait_send()
        ARS[slot] = value.astype(BF)
        k = k % ARR.shape[0]
        c = remote(ARS.at[slot], ARR.at[k], core_peer)
        c.start()
        ar_prev[slot] = c
        return c, slot, k

    def share_end(handle):
        c, slot, k = handle
        c.wait_recv()
        return ARS[slot].astype(F32) + ARR[k].astype(F32)

    def pack_state(which, k_states, v_states, z_rows):
        for p in range(2):
            SCS[which, pl.ds(p * 128, 128)] = (
                k_states[p] + pltpu.roll(v_states[p], HEAD, 1)
            ).astype(BF)
        pack_normalizer(which, z_rows)

    def pack_normalizer(which, z_rows):
        sub = lax.broadcasted_iota(jnp.int32, (16, 128), 0)
        rest = jnp.zeros((16, 128), F32)
        for p in range(2):
            part = z_rows[p]
            for k in range(3):
                piece = part.astype(BF).astype(F32)
                rest = jnp.where(sub == 3 * p + k, piece, rest)
                part = part - piece
        SCS[which, pl.ds(256, 16)] = rest.astype(BF)

    def scan_phase_1(call):
        c = remote(SCS.at[2 * call], SCR1.at[call], pair_peer)
        c.start()
        sent.append(c)
        return c

    def scan_phase_2(call, c, forward):
        c.wait_recv()
        both = SCS[2 * call].astype(F32) + SCR1[call].astype(F32)
        SCS[2 * call + 1, pl.ds(0, 256)] = both[:256].astype(BF)
        z_rows = [
            jnp.sum(both[256 + 3 * p : 256 + 3 * p + 3], axis=0, keepdims=True) for p in range(2)
        ]
        pack_normalizer(2 * call + 1, z_rows)
        links = []
        for d in range(1, pairs):
            to = high + d if forward else high - d
            frm = high - d if forward else high + d
            inside = to < pairs if forward else to >= 0
            comes = frm >= 0 if forward else frm < pairs
            target = jnp.where(inside, to, high)
            c2 = remote(SCS.at[2 * call + 1], SCR2.at[call, d - 1], (target * 2 + low, m))

            @pl.when(inside)
            def _(c2=c2):
                c2.start()

            links.append((c2, inside, comes))
        return links

    def scan_end(call, c, links, forward):
        mine = (low == 1) if forward else (low == 0)
        SCP[...] = jnp.where(mine, SCR1[call].astype(F32), 0.0)
        for d, (c2, inside, comes) in enumerate(links):

            @pl.when(comes)
            def _(c2=c2, d=d):
                c2.wait_recv()
                SCP[...] += SCR2[call, d].astype(F32)

        for c2, inside, comes in links:

            @pl.when(inside)
            def _(c2=c2):
                c2.wait_send()

        def unpack(p):
            block = SCP[pl.ds(p * 128, 128)]
            k_state = jnp.where(diag, block, 0.0)
            v_state = pltpu.roll(jnp.where(diag, 0.0, block), HEAD, 1)
            return k_state, v_state

        tail = SCP[pl.ds(256, 16)]
        z_rows = [jnp.sum(tail[3 * p : 3 * p + 3], axis=0, keepdims=True) for p in range(2)]
        return unpack, z_rows

    tok_copy.wait()
    cot_copy.wait()
    for c in gain_in:
        c.wait_recv()
    for gz in range(GROUPS // 2):
        total = jnp.zeros((8, 128), F32)
        for d in range(4):
            here = flip_z(d) == gz
            total = total + jnp.where(here, GAIN[2 * d] + GAIN[2 * d + 1], 0.0)
        GFULL[:, pl.ds(gz * 128, 128)] = total

    def gain_row(l, which):
        return GFULL[pl.ds(2 * l + which, 1), :]

    def stream(l, rows):
        return TOKB[0, rows].astype(F32) if l == 0 else H[l - 1, rows]

    def attn_norm(l, i):
        rows = tile_rows(i)
        y_hat, _ = norm_parts(stream(l, rows))
        AB[l, rows] = (y_hat * gain_row(l, 0)).astype(BF)

    for i in range(tiles):
        attn_norm(0, i)

    mixer_forward_1(mixer[0])
    mixer_forward_2(mixer[0])
    ffn_forward_1(ffn[0])
    mixer_done(mixer[0])

    for l in range(layers):
        if l + 1 < layers:
            mixer.append(mixer_start(l + 1))
        for p in range(2):

            def project(i, _, p=p, l=l):
                rows = pl.ds(pl.multiple_of(i * TILE, TILE), TILE)
                out = nn(AB[l, rows], WA[l, p, :, pl.ds(0, 512)])
                QKV[l, p, rows] = out[:, :384].astype(BF)
                th = jnp.tanh(out[:, 384:] * (1.0 / 16.0))
                WB[l, p, rows] = jnp.exp(16.0 * th).astype(BF)
                S2[l, p, rows] = (1.0 - th * th).astype(BF)
                return 0

            lax.fori_loop(0, tiles, project, 0)
        k_tot, v_tot, z_tot = [], [], []
        for p in range(2):
            ks, vs, zs = 0.0, 0.0, 0.0
            for j in range(tiles):
                rows = tile_rows(j)
                w = WB[l, p, rows]
                kv = tn(w, QKV[l, p, rows, pl.ds(128, 256)])
                k_j = jnp.where(diag, kv[:, :128], 0.0)
                v_j = jnp.where(diag, kv[:, 128:], 0.0)
                z_j = jnp.sum(w.astype(F32), axis=0, keepdims=True)
                LOC[p, j, 0] = k_j
                LOC[p, j, 1] = v_j
                ks, vs, zs = ks + k_j, vs + v_j, zs + z_j
            k_tot.append(ks)
            v_tot.append(vs)
            z_tot.append(zs)
        call = l
        pack_state(2 * call, k_tot, v_tot, z_tot)
        c1 = scan_phase_1(call)

        def inside(p, _, l=l):
            for j in range(tiles):
                rows = tile_rows(j)
                w = WB[l, p, rows]
                q = QKV[l, p, rows, pl.ds(0, 128)]
                k = QKV[l, p, rows, pl.ds(128, 128)]
                ZS[l, p, rows] = nn(lower_ones, w)
                num = jnp.zeros((TILE, 128), F32)
                for h, (qh, wh) in enumerate(zip(heads(q), heads(w))):
                    a = jnp.where(lower, nt(qh, k), 0.0).astype(BF)
                    AST[l, p, j, h] = a
                    num = num + nn(a, wh)
                XS[l, p, rows] = num
            return 0

        inside(0, 0)
        links = scan_phase_2(call, c1, True)
        inside(1, 0)
        if l == 0:
            ffn_forward_2(ffn[0])
        if l + 1 < layers:
            mixer_forward_1(mixer[l + 1])
        unpack, z_pre = scan_end(call, c1, links, True)

        for p in range(2):
            k_pre, v_pre = unpack(p)
            z_before = z_pre[p]
            for j in range(tiles):
                rows = tile_rows(j)
                if j > 0:
                    k_pre = k_pre + LOC[p, j - 1, 0]
                    v_pre = v_pre + LOC[p, j - 1, 1]
                    z_before = z_before + jnp.sum(
                        WB[l, p, tile_rows(j - 1)].astype(F32), axis=0, keepdims=True
                    )
                KP[l, p, j] = k_pre.astype(BF)
                VP[l, p, j] = v_pre.astype(BF)
                w = WB[l, p, rows]
                q = QKV[l, p, rows, pl.ds(0, 128)]
                v = QKV[l, p, rows, pl.ds(256, 128)]
                z_all = ZS[l, p, rows] + z_before
                num = XS[l, p, rows] + nt(q, KP[l, p, j])
                inv = 1.0 / z_all
                xs = num * inv * 0.125
                e = jnp.exp(xs - per_head_max(xs))
                prob = e / per_head(e)
                scaled = (prob * inv).astype(BF)
                ZS[l, p, rows] = inv
                XS[l, p, rows] = xs
                PS[l, p, rows] = prob
                out = nn(scaled, VP[l, p, j])
                for h, (rh, vh) in enumerate(zip(heads(scaled), heads(v))):
                    mm = jnp.where(lower, nt(rh, w), 0.0).astype(BF)
                    MST[l, p, j, h] = mm
                    out = out + nn(mm, vh)
                OB[l, rows, pl.ds(p * 128, 128)] = out.astype(BF)

        handles = []
        for i in range(tiles):
            rows = tile_rows(i)
            part = nt(OB[l, rows, pl.ds(0, 128)], WA[l, 0, :, pl.ds(512, 128)])
            part = part + nt(OB[l, rows, pl.ds(128, 128)], WA[l, 1, :, pl.ds(512, 128)])
            handles.append(share_start(i, part))
        if l + 1 < layers:
            mixer_forward_2(mixer[l + 1])
        ffn_done(ffn[l])
        if l + 1 < layers:
            ffn.append(ffn_start(l + 1))
        more = []
        for i in range(tiles):
            rows = tile_rows(i)
            mid = stream(l, rows) + share_end(handles[i])
            MID[l, rows] = mid
            y_hat, _ = norm_parts(mid)
            FB[l, rows] = (y_hat * gain_row(l, 1)).astype(BF)
            part = jnp.zeros((TILE, D), F32)
            for p in range(2):
                u = nn(FB[l, rows], WF[l, p, :, pl.ds(0, 512)])
                gate, slope = gate_and_slope(u)
                GG[l, p, rows] = gate.astype(BF)
                GU[l, p, rows] = slope.astype(BF)
                part = part + nt(GG[l, p, rows], WF[l, p, :, pl.ds(512, 512)])
            more.append(share_start(i, part))
        if l + 1 < layers:
            mixer_done(mixer[l + 1])
            ffn_forward_1(ffn[l + 1])
        if l + 1 < layers:
            for i in range(tiles):
                rows = tile_rows(i)
                H[l, rows] = MID[l, rows] + share_end(more[i])
                attn_norm(l + 1, i)
            ffn_forward_2(ffn[l + 1])

    length = len_ref[y]
    last = layers - 1

    def valid_rows(i):
        row = lax.broadcasted_iota(jnp.int32, (TILE, 1), 0)
        return jnp.where(s * T + i * TILE + row < length, 1.0, 0.0)

    def spread(buf_at, slot):
        rows = pl.ds(pl.multiple_of(core * (T // 2), T // 2), T // 2)
        src = buf_at.at[y, rows]
        c = remote(src, src, y_peer)
        c.start()
        sent.append(c)
        return c

    def spread_on(buf_at, c):
        c.wait_recv()
        rows = pl.ds(pl.multiple_of(core * (T // 2), T // 2), T // 2)
        src = buf_at.at[1 - y, rows]
        c2 = remote(src, src, core_peer)
        c2.start()
        sent.append(c2)
        return c2

    for i in range(tiles):
        rows = tile_rows(i)
        out = MID[last, rows] + share_end(more[i])
        keep = valid_rows(i)
        OUTB[0, y, rows] = (out * keep).astype(BF)
        DMID[rows] = TOKB[1, rows].astype(F32) * keep
    mixed_hop = spread(OUTB.at[0], 0)

    def add_bf(a, b):
        return (a.astype(F32) + b.astype(F32)).astype(BF)

    grad_norm = [None] * (2 * layers)
    waiting = {}

    def gf_start(l):
        c = remote(GF.at[l, 1 - y], GFY.at[l], y_peer)
        c.start()
        sent.append(c)
        waiting["fy", l] = c

    def gf_next_1(l):
        waiting["fy", l].wait_recv()

        def one(k, _):
            rows = pl.ds(pl.multiple_of(k * R, R), R)
            GF[l, y, rows] = add_bf(GF[l, y, rows], GFY[l, rows])
            return 0

        lax.fori_loop(0, GROUPS, one, 0)
        for d in range(4):
            c = remote(GF.at[l, y, rows_at(1 - x, flip_z(d))], GFX.at[l, d], x_peer)
            c.start()
            sent.append(c)
            waiting["fx", l, d] = c

    def gf_next_2(l):
        for d in (1, 2, 3, 0):
            waiting["fx", l, d].wait_recv()
            rows = rows_at(x, flip_z(d))
            GF[l, y, rows] = add_bf(GF[l, y, rows], GFX[l, d])
            if d:
                c = remote(GF.at[l, y, rows], GFZ.at[l, d - 1], z_peer[d])
                c.start()
                sent.append(c)
                waiting["fz", l, d] = c

    def gf_end(l):
        total = GF[l, y, rows_own].astype(F32)
        for d in (1, 2, 3):
            waiting["fz", l, d].wait_recv()
            total = total + GFZ[l, d - 1].astype(F32)
        GFO[l] = total
        return local(GFO.at[l], gf_hbm.at[l])

    def ga_start(l):
        for o in range(2):
            for d in range(4):
                yy = 1 - y if o else y
                c = remote(
                    GA.at[l, yy, rows_at(1 - x, flip_z(d))], GAX.at[l, o, d], x_peer
                )
                c.start()
                sent.append(c)
                waiting["ax", l, o, d] = c

    def ga_next_1(l):
        for d in (1, 2, 3, 0):
            for o in range(2):
                yy = 1 - y if o else y
                waiting["ax", l, o, d].wait_recv()
                rows = rows_at(x, flip_z(d))
                GA[l, yy, rows] = add_bf(GA[l, yy, rows], GAX[l, o, d])
                if d:
                    c = remote(GA.at[l, yy, rows], GAZ.at[l, o, d - 1], z_peer[d])
                    c.start()
                    sent.append(c)
                    waiting["az", l, o, d] = c

    def ga_next_2(l):
        for o in (1, 0):
            yy = 1 - y if o else y
            total = GA[l, yy, rows_own].astype(F32)
            for d in (1, 2, 3):
                waiting["az", l, o, d].wait_recv()
                total = total + GAZ[l, o, d - 1].astype(F32)
            GA[l, yy, rows_own] = total.astype(BF)
            if o:
                c = remote(GA.at[l, yy, rows_own], GAY.at[l], y_peer)
                c.start()
                sent.append(c)
                waiting["ay", l] = c

    def ga_end(l):
        waiting["ay", l].wait_recv()
        GAO[l] = GA[l, y, rows_own].astype(F32) + GAY[l].astype(F32)
        return local(GAO.at[l], ga_hbm.at[l])

    finals = []
    for l in range(layers - 1, -1, -1):
        handles = []
        for i in range(tiles):
            rows = tile_rows(i)
            GBF[rows] = DMID[rows].astype(BF)
            part = jnp.zeros((TILE, D), F32)
            for p in range(2):
                dg = nn(GBF[rows], WF[l, p, :, pl.ds(512, 512)])
                DU[p, rows] = (dg * GU[l, p, rows].astype(F32)).astype(BF)
                part = part + nt(DU[p, rows], WF[l, p, :, pl.ds(0, 512)])
            handles.append(share_start(i, part))
        for o in (1, 0):
            yy = 1 - y if o else y
            GF[l, yy, :, pl.ds(0, 512)] = tn(FB[l], DU[yy]).astype(BF)
            GF[l, yy, :, pl.ds(512, 512)] = tn(GBF[...], GG[l, yy]).astype(BF)
            if o:
                gf_start(l)
        gsum = jnp.zeros((1, D), F32)
        for i in range(tiles):
            rows = tile_rows(i)
            df = share_end(handles[i])
            y_hat, rstd = norm_parts(MID[l, rows])
            gsum = gsum + jnp.sum(df * y_hat, axis=0, keepdims=True)
            df = df * gain_row(l, 1)
            dm = DMID[rows] + (
                df
                - jnp.mean(df, axis=-1, keepdims=True)
                - y_hat * jnp.mean(df * y_hat, axis=-1, keepdims=True)
            ) * rstd
            DMID[rows] = dm
            GBF[rows] = dm.astype(BF)
            for p in range(2):
                DOB[p, rows] = nn(GBF[rows], WA[l, p, :, pl.ds(512, 128)]).astype(BF)
        grad_norm[2 * l + 1] = gsum
        if l == last:
            mixed_hop_2 = spread_on(OUTB.at[0], mixed_hop)
        dk_tot, dv_tot, dz_tot = [], [], []
        for p in range(2):
            dks, dvs, dzs = 0.0, 0.0, 0.0
            for j in range(tiles - 1, -1, -1):
                rows = tile_rows(j)
                w = WB[l, p, rows]
                q = QKV[l, p, rows, pl.ds(0, 128)]
                v = QKV[l, p, rows, pl.ds(256, 128)]
                do = DOB[p, rows]
                inv = ZS[l, p, rows]
                prob = PS[l, p, rows]
                dr = nt(do, VP[l, p, j])
                for h, (dh_, wh) in enumerate(zip(heads(do), heads(w))):
                    yy_ = jnp.where(lower, nt(dh_, v), 0.0).astype(BF)
                    YST[p, j, h] = yy_
                    dr = dr + nn(yy_, wh)
                dp = dr * inv
                dx = prob * (dp - per_head(dp * prob))
                dn = (dx * inv * 0.125).astype(BF)
                r = (prob * inv).astype(BF)
                DNB[p, rows] = dn
                RB[p, rows] = r
                dz = -(r.astype(F32) * dp) - 8.0 * dn.astype(F32) * XS[l, p, rows]
                DZ[p, rows] = dz
                dk_j = jnp.where(diag, tn(dn, q), 0.0)
                dv_j = jnp.where(diag, tn(r, do), 0.0)
                LOC[p, j, 0] = dk_j
                LOC[p, j, 1] = dv_j
                dks, dvs = dks + dk_j, dvs + dv_j
                dzs = dzs + jnp.sum(dz, axis=0, keepdims=True)
            dk_tot.append(dks)
            dv_tot.append(dvs)
            dz_tot.append(dzs)
        call = 2 * layers - 1 - l
        pack_state(2 * call, dk_tot, dv_tot, dz_tot)
        c1 = scan_phase_1(call)
        gf_next_1(l)

        def within(p, _, l=l):
            for j in range(tiles):
                rows = tile_rows(j)
                w = WB[l, p, rows]
                q = QKV[l, p, rows, pl.ds(0, 128)]
                k = QKV[l, p, rows, pl.ds(128, 128)]
                do = DOB[p, rows]
                dn = DNB[p, rows]
                r = RB[p, rows]
                dz = DZ[p, rows]
                dz_hi = dz.astype(BF)
                dz_lo = (dz - dz_hi.astype(F32)).astype(BF)
                dw = nn(upper_ones, dz_hi) + nn(upper_ones, dz_lo)
                dq = nn(dn, KP[l, p, j])
                dk = jnp.zeros((TILE, 128), F32)
                dv = jnp.zeros((TILE, 128), F32)
                parts = zip(heads(do), heads(dn), heads(r), heads(q), heads(k))
                for h, (doh, dnh, rh, qh, kh) in enumerate(parts):
                    da = jnp.where(lower, nt(dnh, w), 0.0).astype(BF)
                    dq = dq + nn(da, kh)
                    dk = dk + tn(da, qh)
                    dv = dv + tn(MST[l, p, j, h], doh)
                    dw = dw + tn(YST[p, j, h], rh) + tn(AST[l, p, j, h], dnh)
                DU[p, rows, pl.ds(0, 128)] = dq.astype(BF)
                DWF[p, rows, pl.ds(0, 128)] = dk
                DWF[p, rows, pl.ds(128, 128)] = dv
                DWF[p, rows, pl.ds(256, 128)] = dw
            return 0

        within(0, 0)
        links = scan_phase_2(call, c1, False)
        within(1, 0)
        for p in range(2):
            GA[l, p, :, pl.ds(512, 128)] = tn(GBF[...], OB[l, :, pl.ds(p * 128, 128)]).astype(BF)
        gf_next_2(l)
        unpack, z_post = scan_end(call, c1, links, False)
        for p in range(2):
            k_post, v_post = unpack(p)
            z_after = z_post[p]
            for j in range(tiles - 1, -1, -1):
                rows = tile_rows(j)
                if j < tiles - 1:
                    k_post = k_post + LOC[p, j + 1, 0]
                    v_post = v_post + LOC[p, j + 1, 1]
                    z_after = z_after + jnp.sum(DZ[p, tile_rows(j + 1)], axis=0, keepdims=True)
                kb, vb = k_post.astype(BF), v_post.astype(BF)
                w = WB[l, p, rows]
                k = QKV[l, p, rows, pl.ds(128, 128)]
                v = QKV[l, p, rows, pl.ds(256, 128)]
                dk = DWF[p, rows, pl.ds(0, 128)] + nn(w, kb)
                dv = DWF[p, rows, pl.ds(128, 128)] + nn(w, vb)
                dw = DWF[p, rows, pl.ds(256, 128)] + nt(k, kb) + nt(v, vb) + z_after
                dc = dw * w.astype(F32) * S2[l, p, rows].astype(F32)
                DU[p, rows, pl.ds(128, 128)] = dk.astype(BF)
                DU[p, rows, pl.ds(256, 128)] = dv.astype(BF)
                DU[p, rows, pl.ds(384, 128)] = dc.astype(BF)
        handles = []
        for i in range(tiles):
            rows = tile_rows(i)
            part = nt(DU[0, rows], WA[l, 0, :, pl.ds(0, 512)])
            part = part + nt(DU[1, rows], WA[l, 1, :, pl.ds(0, 512)])
            handles.append(share_start(i, part))
        for p in range(2):
            GA[l, p, :, pl.ds(0, 512)] = tn(AB[l], DU[p]).astype(BF)
        ga_start(l)
        gsum = jnp.zeros((1, D), F32)
        for i in range(tiles):
            rows = tile_rows(i)
            da = share_end(handles[i])
            y_hat, rstd = norm_parts(stream(l, rows))
            gsum = gsum + jnp.sum(da * y_hat, axis=0, keepdims=True)
            da = da * gain_row(l, 0)
            dh = DMID[rows] + (
                da
                - jnp.mean(da, axis=-1, keepdims=True)
                - y_hat * jnp.mean(da * y_hat, axis=-1, keepdims=True)
            ) * rstd
            DMID[rows] = dh
            if l == 0:
                OUTB[1, y, rows] = dh.astype(BF)
        grad_norm[2 * l] = gsum
        if l == last:
            mixed_hop_2.wait_recv()
            finals.append(local(OUTB.at[0], mixed_hbm))
        if l > 0:
            ga_next_1(l)
            finals.append(gf_end(l))
            ga_next_2(l)
            finals.append(ga_end(l))

    tokens_hop = spread(OUTB.at[1], 1)
    sub = lax.broadcasted_iota(jnp.int32, (8, D), 0)
    rows8 = jnp.zeros((8, D), F32)
    for k in range(2 * layers):
        rows8 = jnp.where(sub == k, grad_norm[k], rows8)
    GN[...] = rows8
    cn = remote(GN, GNY, y_peer)
    cn.start()
    sent.append(cn)
    ga_next_1(0)
    cn.wait_recv()
    both = rows8 + GNY[...]
    for gz in range(GROUPS // 2):
        GNR[0, gz] = both[:, gz * 128 : (gz + 1) * 128]
    gn_in = []
    for d in range(4):
        for o in range(2):
            if (d, o) == (0, 0):
                continue
            c = remote(
                GNR.at[0, flip_z(d)],
                GNR.at[1, 2 * d + o],
                (seq_of(1 - x if o else x, flip_z(d)), m),
            )
            c.start()
            sent.append(c)
            gn_in.append((c, 2 * d + o))
    finals.append(gf_end(0))
    tokens_hop_2 = spread_on(OUTB.at[1], tokens_hop)
    ga_next_2(0)
    total = GNR[0, z]
    for c, k in gn_in:
        c.wait_recv()
        total = total + GNR[1, k]
    GNO[...] = total
    finals.append(local(GNO, gn_hbm))
    tokens_hop_2.wait_recv()
    finals.append(local(OUTB.at[1], gt_hbm))
    finals.append(ga_end(0))
    for c in finals:
        c.wait()
    for c in sent:
        c.wait_send()
    for c in ar_prev.values():
        c.wait_send()


def shards(tokens, lengths, norm_attn, norm_ffn, w_qkv, w_ctrl, w_out, w_up, w_down, cotangent):
    layers = w_qkv.shape[0]
    n_seq = lax.axis_size("seq")
    stride = n_seq // GROUPS
    _, T, D = tokens.shape
    rows = w_qkv.shape[1]
    wa = jnp.concatenate([w_qkv.reshape(layers, rows, -1), w_ctrl, w_out], axis=-1)
    wf = jnp.concatenate([w_up, w_down], axis=-1)
    gains = jnp.stack([norm_attn, norm_ffn], axis=1).reshape(2 * layers, rows)
    blocks = [[k * stride + j for j in range(stride)] for k in range(GROUPS)]
    if stride > 1:

        def fill(a, dim):
            return lax.all_gather(a, "seq", axis=dim, tiled=True, axis_index_groups=blocks)

        wa, wf, gains = fill(wa, 1), fill(wf, 1), fill(gains, 1)
    R = D // GROUPS
    odd = (lax.axis_index("seq") // stride) % 2
    gains = gains.astype(F32)
    none = jnp.zeros_like(gains)
    gains = jnp.concatenate(
        [jnp.where(odd == 0, gains, none), jnp.where(odd == 0, none, gains)], axis=1
    )
    gains = jnp.pad(gains, ((0, 8 - 2 * layers), (0, 0)))
    A, F = wa.shape[-1], wf.shape[-1]
    pairs = n_seq // 2
    tiles = T // TILE
    bf, f32 = BF, F32
    v = pltpu.VMEM
    scratch = [
        v((max(layers - 1, 1), T, D), f32),
        v((layers, T, D), f32),
        v((layers, T, D), bf),
        v((layers, T, D), bf),
        v((layers, 2, T, 384), bf),
        v((layers, 2, T, 128), bf),
        v((layers, 2, T, 128), bf),
        v((layers, 2, T, 128), f32),
        v((layers, 2, T, 128), f32),
        v((layers, 2, T, 128), f32),
        v((layers, 2, tiles, 2, TILE, TILE), bf),
        v((layers, 2, tiles, 2, TILE, TILE), bf),
        v((layers, T, 256), bf),
        v((layers, 2, T, F // 2), bf),
        v((layers, 2, T, F // 2), bf),
        v((layers, 2, tiles, 128, 128), bf),
        v((layers, 2, tiles, 128, 128), bf),
        v((2, tiles, 2, 128, 128), f32),
        v((2, T, D), bf),
        v((T, D), bf),
        v((2, T, 128), bf),
        v((2, T, F // 2), bf),
        v((T, D), f32),
        v((2, tiles, 2, TILE, TILE), bf),
        v((2, T, 128), bf),
        v((2, T, 128), bf),
        v((2, T, 128), f32),
        v((2, T, 384), f32),
        v((layers, 2, D, A), bf),
        v((layers, 2, D, F), bf),
        v((8, 8, 128), f32),
        v((8, D), f32),
        v((tiles, TILE, D), bf),
        v((2 * tiles, TILE, D), bf),
        v((4 * layers, 272, 128), bf),
        v((2 * layers, 272, 128), bf),
        v((2 * layers, pairs - 1, 272, 128), bf),
        v((272, 128), f32),
        v((layers, 2, D, A), bf),
        v((layers, 2, D, F), bf),
        v((layers, 2, 4, R, A), bf),
        v((layers, 2, 3, R, A), bf),
        v((layers, R, A), bf),
        v((layers, D, F), bf),
        v((layers, 4, R, F), bf),
        v((layers, 3, R, F), bf),
        v((layers, R, A), f32),
        v((layers, R, F), f32),
        v((8, D), f32),
        v((8, D), f32),
        v((2, 8, 8, 128), f32),
        v((8, 128), f32),
        v((2, 2, T, D), bf),
        pltpu.SemaphoreType.DMA((N_REMOTE + 2 * layers * pairs,)),
        pltpu.SemaphoreType.DMA((N_REMOTE + 2 * layers * pairs,)),
        pltpu.SemaphoreType.DMA((32,)),
    ]
    any_spec = pl.BlockSpec(memory_space=pl.ANY)
    out_shape = (
        jax.ShapeDtypeStruct((2, T, D), bf),
        jax.ShapeDtypeStruct((2, T, D), bf),
        jax.ShapeDtypeStruct((layers, R, A), f32),
        jax.ShapeDtypeStruct((layers, R, F), f32),
        jax.ShapeDtypeStruct((8, 128), f32),
    )
    mixed, grad_tokens, ga, gf, gn = pl.pallas_call(
        functools.partial(kernel, n_seq, layers),
        out_shape=out_shape,
        in_specs=[
            any_spec,
            any_spec,
            pl.BlockSpec(memory_space=pltpu.SMEM),
            any_spec,
            any_spec,
            pl.BlockSpec(memory_space=pltpu.VMEM),
        ],
        out_specs=(any_spec,) * 5,
        scratch_shapes=scratch,
        compiler_params=pltpu.CompilerParams(
            collective_id=0, has_side_effects=True, vmem_limit_bytes=VMEM_BYTES
        ),
    )(tokens, cotangent, lengths, wa, wf, gains)
    gn = jnp.where(odd == 0, gn[: 2 * layers, :R], gn[: 2 * layers, R : 2 * R])
    if stride > 1:

        def empty(a, dim):
            return lax.psum_scatter(
                a, "seq", scatter_dimension=dim, tiled=True, axis_index_groups=blocks
            )

        ga, gf, gn = empty(ga, 1), empty(gf, 1), empty(gn, 1)
    gn = gn.reshape(layers, 2, rows)
    half = F // 2
    qkv_width = 3 * 128
    return (
        mixed,
        grad_tokens.astype(F32),
        gn[:, 0],
        gn[:, 1],
        ga[:, :, :qkv_width].reshape(w_qkv.shape),
        ga[:, :, qkv_width : qkv_width + 128],
        ga[:, :, qkv_width + 128 :],
        gf[:, :, :half],
        gf[:, :, half:],
    )


N_REMOTE = 256
VMEM_BYTES = 62 << 20


def solution(mesh):
    in_specs = (
        P(None, "seq", None),
        P(),
        P(None, "seq"),
        P(None, "seq"),
        P(None, "seq", None, "mp"),
        P(None, "seq", "mp"),
        P(None, "seq", "mp"),
        P(None, "seq", "mp"),
        P(None, "seq", "mp"),
        P(None, "seq", None),
    )
    out_specs = (
        P(None, "seq", None),
        P(None, "seq", None),
        P(None, "seq"),
        P(None, "seq"),
        P(None, "seq", None, "mp"),
        P(None, "seq", "mp"),
        P(None, "seq", "mp"),
        P(None, "seq", "mp"),
        P(None, "seq", "mp"),
    )
    return jax.shard_map(shards, mesh=mesh, in_specs=in_specs, out_specs=out_specs, check_vma=False)
```

```python
import functools

import jax
import jax.numpy as jnp
from jax import lax
from jax.experimental import pallas as pl
from jax.experimental.pallas import tpu as pltpu
from jax.sharding import PartitionSpec as P

F32 = jnp.float32
BF = jnp.bfloat16
MESH = pl.DeviceIdType.MESH
GROUPS = 8
HEAD = 64
EPS = 1e-05
TILE = 256


def nn(a, b):
    return lax.dot_general(a, b, (((1,), (0,)), ((), ())), preferred_element_type=F32)


def nt(a, b):
    return lax.dot_general(a, b, (((1,), (1,)), ((), ())), preferred_element_type=F32)


def tn(a, b):
    return lax.dot_general(a, b, (((0,), (0,)), ((), ())), preferred_element_type=F32)


def norm_parts(x):
    center = x - jnp.mean(x, axis=-1, keepdims=True)
    spread = jnp.mean(center * center, axis=-1, keepdims=True)
    rstd = lax.rsqrt(spread + EPS)
    return center * rstd, rstd


def gate_and_slope(u):
    t = jnp.tanh(0.7978845608 * (u + 0.044715 * u * u * u))
    half = 0.5 * (1.0 + t)
    slope = half + 0.5 * u * (1.0 - t * t) * (0.7978845608 * (1.0 + 3.0 * 0.044715 * u * u))
    return u * half, slope


def kernel(
    n_seq,
    layers,
    tok_hbm,
    cot_hbm,
    len_ref,
    qkv_hbm,
    ctrl_hbm,
    up_hbm,
    down_hbm,
    out_hbm,
    norm_attn_ref,
    norm_ffn_ref,
    mixed_hbm,
    gt_hbm,
    gqkv_hbm,
    gctrl_hbm,
    gout_hbm,
    gup_hbm,
    gdown_hbm,
    gn_hbm,
    H,
    MID,
    AB,
    FB,
    QKV,
    WB,
    S2,
    ZS,
    PS,
    XS,
    AST,
    MST,
    OB,
    GU,
    GG,
    KP,
    VP,
    LOC,
    TOKB,
    GBF,
    DOB,
    DU,
    DMID,
    YST,
    DNB,
    DZ,
    DWF,
    WA,
    WF,
    GAIN,
    GFULL,
    ARS,
    ARR,
    SCS,
    SCR1,
    SCR2,
    SCP,
    RQK,
    RVC,
    ROUT,
    RUP,
    RDN,
    LQK,
    LVC,
    LOUT,
    LUP,
    LDN,
    OQKV,
    OCTRL,
    OOUT,
    OUP,
    ODN,
    GN,
    GNY,
    GNR,
    GNO,
    OUTB,
    send_sems,
    recv_sems,
    local_sems,
):
    T, D = TOKB.shape[1], TOKB.shape[2]
    tiles = T // TILE
    R = D // GROUPS
    stride = n_seq // GROUPS
    s = lax.axis_index("seq")
    m = lax.axis_index("mp")
    y, core = m // 2, m % 2
    g, lo = s // stride, s % stride
    x, z = g % 2, g // 2
    z1, z0 = z // 2, z % 2
    last = layers - 1

    def flip_z(d):
        d1, d0 = d // 2, d % 2
        return 2 * (1 - z1 if d1 else z1) + (1 - z0 if d0 else z0)

    def seq_of(gx, gz):
        return (gz * 2 + gx) * stride + lo

    core_peer = (s, 2 * y + (1 - core))
    y_peer = (s, 2 * (1 - y) + core)
    x_peer = (seq_of(1 - x, z), m)
    z_peer = {d: (seq_of(x, flip_z(d)), m) for d in (1, 2, 3)}
    pairs = n_seq // 2
    low, high = s % 2, s // 2
    pair_peer = (s - low + (1 - low), m)

    used = [0, 0]
    sent = []

    def remote(src, dst, peer):
        k = used[0]
        used[0] += 1
        return pltpu.make_async_remote_copy(
            src_ref=src,
            dst_ref=dst,
            send_sem=send_sems.at[k],
            recv_sem=recv_sems.at[k],
            device_id=peer,
            device_id_type=MESH,
        )

    def send(src, dst, peer):
        c = remote(src, dst, peer)
        c.start()
        sent.append(c)
        return c

    def local(src, dst):
        k = used[1]
        used[1] += 1
        c = pltpu.make_async_copy(src, dst, local_sems.at[k])
        c.start()
        return c

    barrier = pltpu.get_barrier_semaphore()

    def hello(peer):
        pl.semaphore_signal(barrier, inc=1, device_id=peer, device_id_type=MESH)

    hello(core_peer)
    hello(y_peer)
    hello(pair_peer)
    count = 3
    for d in range(1, pairs):
        other = lax.rem(high + d, pairs) * 2
        hello((other + low, m))
        count += 1
        if stride == 1:
            hello((other + 1 - low, m))
            count += 1

    own = []
    for l in range(layers):
        lanes = 0
        for src in (qkv_hbm, ctrl_hbm):
            at = pl.ds(lanes, src.shape[-1])
            own.append(local(src.at[l], WA.at[l, y, z, x, slice(None), at]))
            lanes += src.shape[-1]
        lanes = 0
        for src in (up_hbm, down_hbm, out_hbm):
            at = pl.ds(lanes, src.shape[-1])
            own.append(local(src.at[l], WF.at[l, y, z, x, slice(None), at]))
            lanes += src.shape[-1]
    tok_copy = local(tok_hbm.at[y], TOKB.at[0])
    cot_copy = local(cot_hbm.at[y], TOKB.at[1])
    gain_sub = lax.broadcasted_iota(jnp.int32, (8, R), 0)
    own_gains = jnp.zeros((8, R), F32)
    for l in range(layers):
        for k, ref in enumerate((norm_attn_ref, norm_ffn_ref)):
            row = ref[pl.ds(l, 1), :].astype(F32)
            own_gains = jnp.where(gain_sub == 2 * l + k, row, own_gains)
    GAIN[0, :, pl.ds(0, R)] = jnp.where(x == 0, own_gains, 0.0)
    GAIN[0, :, pl.ds(R, R)] = jnp.where(x == 0, 0.0, own_gains)

    pl.semaphore_wait(barrier, count)

    class Gather:
        def __init__(self, buf, l, low_end, cut, high_end):
            self.buf, self.l, self.c = buf, l, {}
            self.all = pl.ds(low_end, high_end - low_end)
            self.halves = (pl.ds(low_end, cut - low_end), pl.ds(cut, high_end - cut))

        def push(self, key, region, peer, lanes=None):
            src = self.buf.at[(self.l,) + region + (slice(None), lanes or self.all)]
            self.c[key] = send(src, src, peer)

        def start(self):
            mine = (y, z, x)
            for d in (1, 2, 3):
                self.push(("z", d), mine, z_peer[d])

        def step_1_own(self):
            mine = (y, z, x)
            self.push(("x", 0), mine, x_peer)
            self.push(("y", 0), mine, y_peer)

        def step_1(self):
            for d in (1, 2, 3):
                self.c["z", d].wait_recv()
                self.push(("x", d), (y, flip_z(d), x), x_peer)
                self.push(("y", d), (y, flip_z(d), x), y_peer)

        def step_2(self):
            first, second = self.halves
            for d in range(4):
                self.c["x", d].wait_recv()
                self.push(("xy", d), (y, flip_z(d), 1 - x), y_peer, first)
                self.c["y", d].wait_recv()
                self.push(("yx", d), (1 - y, flip_z(d), x), x_peer, second)

        def end(self):
            for d in range(4):
                self.c["xy", d].wait_recv()
                self.c["yx", d].wait_recv()

    gain_in = []
    for d in (0, 1, 2, 3):
        for o in (0, 1):
            if (d, o) == (0, 0):
                continue
            peer = (seq_of(1 - x if o else x, flip_z(d)), m)
            gain_in.append(send(GAIN.at[0], GAIN.at[d * 2 + o], peer))
    for c in own:
        c.wait()
    mixer = [Gather(WA, l, 0, 256, 512) for l in range(layers)]
    upper = [Gather(WF, l, 0, 256, 512) for l in range(layers)]
    lower_part = [Gather(WF, l, 512, 896, 1152) for l in range(layers)]
    for f in (mixer[0], upper[0], lower_part[0]):
        f.start()
        f.step_1_own()

    lane = lax.broadcasted_iota(jnp.int32, (TILE, 128), 1)
    first = lane < HEAD
    head_rows = [
        (lax.broadcasted_iota(jnp.int32, (1, 128), 1) < HEAD).astype(F32).astype(BF),
        (lax.broadcasted_iota(jnp.int32, (1, 128), 1) >= HEAD).astype(F32).astype(BF),
    ]
    rr = lax.broadcasted_iota(jnp.int32, (TILE, TILE), 0)
    cc = lax.broadcasted_iota(jnp.int32, (TILE, TILE), 1)
    lower = rr >= cc
    lower_ones = lower.astype(F32).astype(BF)
    upper_ones = (rr <= cc).astype(F32).astype(BF)
    diag = (lax.broadcasted_iota(jnp.int32, (128, 128), 0) < HEAD) == (
        lax.broadcasted_iota(jnp.int32, (128, 128), 1) < HEAD
    )

    def per_head(value):
        a = jnp.sum(jnp.where(first, value, 0.0), axis=-1, keepdims=True)
        b = jnp.sum(jnp.where(first, 0.0, value), axis=-1, keepdims=True)
        return jnp.where(first, a, b)

    def per_head_max(value):
        a = jnp.max(jnp.where(first, value, -jnp.inf), axis=-1, keepdims=True)
        b = jnp.max(jnp.where(first, -jnp.inf, value), axis=-1, keepdims=True)
        return jnp.where(first, a, b)

    def heads(value):
        return value * head_rows[0], value * head_rows[1]

    def tile_rows(i):
        return pl.ds(i * TILE, TILE)

    def weight(buf, l, p, start, width):
        return buf[l, p, :, :, :, pl.ds(start, width)].reshape(D, width)

    def mixer_weight(l, p):
        return weight(WA, l, p, 0, 512)

    def up_weight(l, p):
        return weight(WF, l, p, 0, 512)

    def down_weight(l, p):
        return weight(WF, l, p, 512, 512)

    def out_weight(l, p):
        return weight(WF, l, p, 1024, 128)

    ar_used = [0]
    ar_prev = {}

    def share_start(value):
        k = ar_used[0]
        ar_used[0] += 1
        slot = k % ARS.shape[0]
        if slot in ar_prev:
            ar_prev[slot].wait_send()
        ARS[slot] = value.astype(BF)
        k = k % ARR.shape[0]
        c = remote(ARS.at[slot], ARR.at[k], core_peer)
        c.start()
        ar_prev[slot] = c
        return c, slot, k

    def share_end(handle):
        c, slot, k = handle
        c.wait_recv()
        return ARS[slot].astype(F32) + ARR[k].astype(F32)

    class Scan:
        def __init__(self, call, forward):
            self.call, self.forward = call, forward

        def pack_normalizer(self, which, part):
            sub = lax.broadcasted_iota(jnp.int32, (16, 128), 0)
            rest = jnp.zeros((16, 128), F32)
            for k in range(3):
                piece = part.astype(BF).astype(F32)
                rest = jnp.where(sub == k, piece, rest)
                part = part - piece
            SCS[which, pl.ds(128, 16)] = rest.astype(BF)

        def start(self, k_state, v_state, z_row):
            which = self.call
            SCS[which, pl.ds(0, 128)] = (k_state + pltpu.roll(v_state, HEAD, 1)).astype(BF)
            self.pack_normalizer(which, z_row)
            self.near = remote(SCS.at[which], SCR1.at[self.call], pair_peer)
            self.near.start()

        def step(self):
            self.near.wait()
            which = self.call
            both = SCS[which].astype(F32) + SCR1[self.call].astype(F32)
            SCS[which, pl.ds(0, 128)] = both[:128].astype(BF)
            self.pack_normalizer(which, jnp.sum(both[128:131], axis=0, keepdims=True))
            self.links = []
            for d in range(1, pairs):
                to = high + d if self.forward else high - d
                frm = high - d if self.forward else high + d
                inside = to < pairs if self.forward else to >= 0
                comes = frm >= 0 if self.forward else frm < pairs
                target = jnp.where(inside, to, high)
                c = remote(SCS.at[which], SCR2.at[self.call, d - 1], (target * 2 + low, m))

                @pl.when(inside)
                def _(c=c):
                    c.start()

                self.links.append((c, inside, comes))

        def end(self):
            acc = SCP.at[self.call % 2]
            mine = (low == 1) if self.forward else (low == 0)
            acc[...] = jnp.where(mine, SCR1[self.call].astype(F32), 0.0)
            for d, (c, inside, comes) in enumerate(self.links):

                @pl.when(comes)
                def _(c=c, d=d):
                    c.wait_recv()
                    acc[...] += SCR2[self.call, d].astype(F32)

            for c, inside, comes in self.links:

                @pl.when(inside)
                def _(c=c):
                    c.wait_send()

            block = acc[pl.ds(0, 128)]
            k_state = jnp.where(diag, block, 0.0)
            v_state = pltpu.roll(jnp.where(diag, 0.0, block), HEAD, 1)
            return k_state, v_state, jnp.sum(acc[pl.ds(128, 3)], axis=0, keepdims=True)

    every = slice(None)

    def add_to(buf, at, more):
        buf[at] = (buf[at].astype(F32) + more.astype(F32)).astype(BF)

    class Scatter:
        def __init__(self, buf, land, l, x_first):
            self.buf, self.land, self.l, self.x_first = buf, land, l, x_first
            self.first_peer = x_peer if x_first else y_peer
            self.next_peer = y_peer if x_first else x_peer

        def block(self, first_other, next_other):
            ox, oy = (first_other, next_other) if self.x_first else (next_other, first_other)
            return (self.l, 1 - y if oy else y, every, 1 - x if ox else x)

        c1 = None

        def start(self, halves=(1, 0)):
            self.c1 = self.c1 or {}
            for o in halves:
                src = self.buf.at[self.block(1, o)]
                self.c1[o] = send(src, self.land.at[self.l, pl.ds(4 * o, 4)], self.first_peer)

        def step_1(self, halves=(1, 0)):
            for o in halves:
                self.c1[o].wait_recv()
                at = self.block(0, o)
                add_to(self.buf, at, self.land[self.l, pl.ds(4 * o, 4)])
                if o:
                    self.c2 = send(self.buf.at[at], self.land.at[self.l, pl.ds(8, 4)], self.next_peer)

        def step_2(self):
            self.c2.wait_recv()
            self.c3 = {}
            for d in (1, 2, 3, 0):
                at = (self.l, y, flip_z(d), x)
                add_to(self.buf, at, self.land[self.l, 8 + flip_z(d)])
                if d:
                    self.c3[d] = send(self.buf.at[at], self.land.at[self.l, 11 + d], z_peer[d])

        def end(self):
            total = self.buf[self.l, y, z, x].astype(F32)
            for d in (1, 2, 3):
                self.c3[d].wait_recv()
                total = total + self.land[self.l, 11 + d].astype(F32)
            return total

    finals = []
    jobs = []
    for l in range(layers):
        jobs.append(
            dict(
                qk=Scatter(RQK, LQK, l, True),
                vc=Scatter(RVC, LVC, l, False),
                out=Scatter(ROUT, LOUT, l, False),
                up=Scatter(RUP, LUP, l, False),
                down=Scatter(RDN, LDN, l, True),
            )
        )

    def finish(l, name):
        total = jobs[l][name].end()
        if name == "up":
            OUP[l] = total
            finals.append(local(OUP.at[l], gup_hbm.at[l]))
        elif name == "down":
            ODN[l] = total
            finals.append(local(ODN.at[l], gdown_hbm.at[l]))
        elif name == "out":
            OOUT[l] = total
            finals.append(local(OOUT.at[l], gout_hbm.at[l]))
        elif name == "qk":
            OQKV[l, :, pl.ds(0, 256)] = total
        else:
            OQKV[l, :, pl.ds(256, 128)] = total[:, :128]
            OCTRL[l] = total[:, 128:]
            finals.append(local(OQKV.at[l], gqkv_hbm.at[l]))
            finals.append(local(OCTRL.at[l], gctrl_hbm.at[l]))

    tok_copy.wait()
    cot_copy.wait()
    for c in gain_in:
        c.wait_recv()
    for gz in range(GROUPS // 2):
        total = jnp.zeros((8, 128), F32)
        for d in range(4):
            here = flip_z(d) == gz
            total = total + jnp.where(here, GAIN[2 * d] + GAIN[2 * d + 1], 0.0)
        GFULL[:, pl.ds(gz * 128, 128)] = total

    def gain_row(l, which):
        return GFULL[pl.ds(2 * l + which, 1), :]

    def stream(l, rows):
        return TOKB[0, rows].astype(F32) if l == 0 else H[l - 1, rows]

    def attn_norm(l, i):
        rows = tile_rows(i)
        y_hat, _ = norm_parts(stream(l, rows))
        AB[l, rows] = (y_hat * gain_row(l, 0)).astype(BF)

    for i in range(tiles):
        attn_norm(0, i)

    mixer[0].step_1()
    mixer[0].step_2()
    upper[0].step_1()
    mixer[0].end()

    for l in range(layers):
        more_layers = l + 1 < layers
        if more_layers:
            mixer[l + 1].start()
        scans = [Scan(2 * l + p, True) for p in range(2)]

        def project_pair(p, l=l):
            def project(i, _):
                rows = pl.ds(pl.multiple_of(i * TILE, TILE), TILE)
                out = nn(AB[l, rows], mixer_weight(l, p))
                QKV[l, p, rows] = out[:, :384].astype(BF)
                th = jnp.tanh(out[:, 384:] * (1.0 / 16.0))
                WB[l, p, rows] = jnp.exp(16.0 * th).astype(BF)
                S2[l, p, rows] = (1.0 - th * th).astype(BF)
                return 0

            lax.fori_loop(0, tiles, project, 0)

        def local_states(p, l=l):
            ks, vs, zs = 0.0, 0.0, 0.0
            for j in range(tiles):
                rows = tile_rows(j)
                w = WB[l, p, rows]
                kv = tn(w, QKV[l, p, rows, pl.ds(128, 256)])
                k_j = jnp.where(diag, kv[:, :128], 0.0)
                v_j = jnp.where(diag, kv[:, 128:], 0.0)
                if j < tiles - 1:
                    LOC[p, j, 0] = k_j
                    LOC[p, j, 1] = v_j
                ks, vs = ks + k_j, vs + v_j
                zs = zs + jnp.sum(w.astype(F32), axis=0, keepdims=True)
            return ks, vs, zs

        def inside_block(p, l=l):
            for j in range(tiles):
                rows = tile_rows(j)
                w = WB[l, p, rows]
                q = QKV[l, p, rows, pl.ds(0, 128)]
                k = QKV[l, p, rows, pl.ds(128, 128)]
                ZS[l, p, rows] = nn(lower_ones, w)
                num = jnp.zeros((TILE, 128), F32)
                for h, (qh, wh) in enumerate(zip(heads(q), heads(w))):
                    a = jnp.where(lower, nt(qh, k), 0.0).astype(BF)
                    AST[l, p, j, h] = a
                    num = num + nn(a, wh)
                XS[l, p, rows] = num

        def with_earlier(p, l=l):
            k_pre, v_pre, z_before = scans[p].end()
            for j in range(tiles):
                rows = tile_rows(j)
                if j > 0:
                    k_pre = k_pre + LOC[p, j - 1, 0]
                    v_pre = v_pre + LOC[p, j - 1, 1]
                    z_before = z_before + jnp.sum(
                        WB[l, p, tile_rows(j - 1)].astype(F32), axis=0, keepdims=True
                    )
                KP[l, p, j] = k_pre.astype(BF)
                VP[l, p, j] = v_pre.astype(BF)
                w = WB[l, p, rows]
                q = QKV[l, p, rows, pl.ds(0, 128)]
                v = QKV[l, p, rows, pl.ds(256, 128)]
                inv = 1.0 / (ZS[l, p, rows] + z_before)
                xs = (XS[l, p, rows] + nt(q, KP[l, p, j])) * inv * 0.125
                e = jnp.exp(xs - per_head_max(xs))
                prob = e / per_head(e)
                scaled = (prob * inv).astype(BF)
                ZS[l, p, rows] = inv
                XS[l, p, rows] = xs
                PS[l, p, rows] = prob
                out = nn(scaled, VP[l, p, j])
                for h, (rh, vh) in enumerate(zip(heads(scaled), heads(v))):
                    mm = jnp.where(lower, nt(rh, w), 0.0).astype(BF)
                    MST[l, p, j, h] = mm
                    out = out + nn(mm, vh)
                OB[l, rows, pl.ds(p * 128, 128)] = out.astype(BF)

        for p in range(2):
            project_pair(p)
            scans[p].start(*local_states(p))
        if l > 0:
            lower_part[l].step_1_own()
        inside_block(0)
        lower_part[l].step_1()
        scans[0].step()
        inside_block(1)
        scans[1].step()
        upper[l].step_2()
        lower_part[l].step_2()
        if more_layers:
            mixer[l + 1].step_1_own()
            mixer[l + 1].step_1()
            upper[l + 1].start()
            lower_part[l + 1].start()
        with_earlier(0)
        with_earlier(1)
        lower_part[l].end()
        upper[l].end()

        handles = []
        for i in range(tiles):
            rows = tile_rows(i)
            part = nt(OB[l, rows, pl.ds(0, 128)], out_weight(l, 0))
            part = part + nt(OB[l, rows, pl.ds(128, 128)], out_weight(l, 1))
            handles.append(share_start(part))
        if more_layers:
            mixer[l + 1].step_2()
            upper[l + 1].step_1_own()
            upper[l + 1].step_1()
        more = []
        for i in range(tiles):
            rows = tile_rows(i)
            mid = stream(l, rows) + share_end(handles[i])
            MID[l, rows] = mid
            y_hat, _ = norm_parts(mid)
            FB[l, rows] = (y_hat * gain_row(l, 1)).astype(BF)
            part = jnp.zeros((TILE, D), F32)
            for p in range(2):
                gate, slope = gate_and_slope(nn(FB[l, rows], up_weight(l, p)))
                GG[l, p, rows] = gate.astype(BF)
                GU[l, p, rows] = slope.astype(BF)
                part = part + nt(GG[l, p, rows], down_weight(l, p))
            more.append(share_start(part))
        if more_layers:
            for i in range(tiles):
                rows = tile_rows(i)
                H[l, rows] = MID[l, rows] + share_end(more[i])
                attn_norm(l + 1, i)
            mixer[l + 1].end()

    length = len_ref[y]

    def valid_rows(i):
        row = lax.broadcasted_iota(jnp.int32, (TILE, 1), 0)
        return jnp.where(s * T + i * TILE + row < length, 1.0, 0.0)

    half_rows = pl.ds(pl.multiple_of(core * (T // 2), T // 2), T // 2)

    def spread(k):
        src = OUTB.at[k, y, half_rows]
        return send(src, src, y_peer)

    def spread_on(k, c):
        c.wait_recv()
        src = OUTB.at[k, 1 - y, half_rows]
        return send(src, src, core_peer)

    for i in range(tiles):
        rows = tile_rows(i)
        out = MID[last, rows] + share_end(more[i])
        keep = valid_rows(i)
        OUTB[0, y, rows] = (out * keep).astype(BF)
        DMID[rows] = TOKB[1, rows].astype(F32) * keep

    grad_norm = [None] * (2 * layers)

    def split_rows(value):
        return value.astype(BF).reshape(4, 2, R, value.shape[-1])

    for l in range(last, -1, -1):
        job = jobs[l]
        before = jobs[l + 1] if l < last else None
        for i in range(tiles):
            GBF[tile_rows(i)] = DMID[tile_rows(i)].astype(BF)
        RDN[l, 1 - y] = split_rows(tn(GBF[...], GG[l, 1 - y]))
        job["down"].start((1,))
        handles = []
        for i in range(tiles):
            rows = tile_rows(i)
            part = jnp.zeros((TILE, D), F32)
            for p in range(2):
                dg = nn(GBF[rows], down_weight(l, p))
                DU[p, rows] = (dg * GU[l, p, rows].astype(F32)).astype(BF)
                part = part + nt(DU[p, rows], up_weight(l, p))
            handles.append(share_start(part))
        if before:
            for name in ("qk", "vc"):
                before[name].step_1()
        RUP[l, 1 - y] = split_rows(tn(FB[l], DU[1 - y]))
        job["up"].start()
        RDN[l, y] = split_rows(tn(GBF[...], GG[l, y]))
        gsum = jnp.zeros((1, D), F32)
        for i in range(tiles):
            rows = tile_rows(i)
            df = share_end(handles[i])
            y_hat, rstd = norm_parts(MID[l, rows])
            gsum = gsum + jnp.sum(df * y_hat, axis=0, keepdims=True)
            df = df * gain_row(l, 1)
            dm = DMID[rows] + (
                df
                - jnp.mean(df, axis=-1, keepdims=True)
                - y_hat * jnp.mean(df * y_hat, axis=-1, keepdims=True)
            ) * rstd
            DMID[rows] = dm
            GBF[rows] = dm.astype(BF)
            for p in range(2):
                DOB[p, rows] = nn(GBF[rows], out_weight(l, p)).astype(BF)
        grad_norm[2 * l + 1] = gsum

        scans = [Scan(2 * layers + 2 * (last - l) + k, False) for k in range(2)]
        order = (1 - y, y)

        def to_states(p, l=l):
            dks, dvs, dzs = 0.0, 0.0, 0.0
            for j in range(tiles - 1, -1, -1):
                rows = tile_rows(j)
                w = WB[l, p, rows]
                q = QKV[l, p, rows, pl.ds(0, 128)]
                v = QKV[l, p, rows, pl.ds(256, 128)]
                do = DOB[p, rows]
                inv = ZS[l, p, rows]
                prob = PS[l, p, rows]
                dr = nt(do, VP[l, p, j])
                for h, (doh, wh) in enumerate(zip(heads(do), heads(w))):
                    pair = jnp.where(lower, nt(doh, v), 0.0).astype(BF)
                    YST[p, j, h] = pair
                    dr = dr + nn(pair, wh)
                dp = dr * inv
                dx = prob * (dp - per_head(dp * prob))
                dn = (dx * inv * 0.125).astype(BF)
                r = (prob * inv).astype(BF)
                DNB[p, rows] = dn
                dz = -(r.astype(F32) * dp) - 8.0 * dn.astype(F32) * XS[l, p, rows]
                DZ[p, rows] = dz
                dk_j = jnp.where(diag, tn(dn, q), 0.0)
                dv_j = jnp.where(diag, tn(r, do), 0.0)
                if j > 0:
                    LOC[p, j - 1, 0] = dk_j
                    LOC[p, j - 1, 1] = dv_j
                dks, dvs = dks + dk_j, dvs + dv_j
                dzs = dzs + jnp.sum(dz, axis=0, keepdims=True)
            return dks, dvs, dzs

        def within(p, l=l):
            for j in range(tiles):
                rows = tile_rows(j)
                w = WB[l, p, rows]
                q = QKV[l, p, rows, pl.ds(0, 128)]
                k = QKV[l, p, rows, pl.ds(128, 128)]
                do = DOB[p, rows]
                dn = DNB[p, rows]
                r = (PS[l, p, rows] * ZS[l, p, rows]).astype(BF)
                dz = DZ[p, rows]
                dz_hi = dz.astype(BF)
                dz_lo = (dz - dz_hi.astype(F32)).astype(BF)
                dw = nn(upper_ones, dz_hi) + nn(upper_ones, dz_lo)
                dq = nn(dn, KP[l, p, j])
                dk = jnp.zeros((TILE, 128), F32)
                dv = jnp.zeros((TILE, 128), F32)
                parts = zip(heads(do), heads(dn), heads(r), heads(q), heads(k))
                for h, (doh, dnh, rh, qh, kh) in enumerate(parts):
                    da = jnp.where(lower, nt(dnh, w), 0.0).astype(BF)
                    dq = dq + nn(da, kh)
                    dk = dk + tn(da, qh)
                    dv = dv + tn(MST[l, p, j, h], doh)
                    dw = dw + tn(YST[p, j, h], rh) + tn(AST[l, p, j, h], dnh)
                DU[p, rows, pl.ds(0, 128)] = dq.astype(BF)
                DWF[p, rows, pl.ds(0, 128)] = dk
                DWF[p, rows, pl.ds(128, 128)] = dv
                DWF[p, rows, pl.ds(256, 128)] = dw

        def with_later(k, p, l=l):
            k_post, v_post, z_after = scans[k].end()
            for j in range(tiles - 1, -1, -1):
                rows = tile_rows(j)
                if j < tiles - 1:
                    k_post = k_post + LOC[p, j, 0]
                    v_post = v_post + LOC[p, j, 1]
                    z_after = z_after + jnp.sum(DZ[p, tile_rows(j + 1)], axis=0, keepdims=True)
                kb, vb = k_post.astype(BF), v_post.astype(BF)
                w = WB[l, p, rows]
                key = QKV[l, p, rows, pl.ds(128, 128)]
                v = QKV[l, p, rows, pl.ds(256, 128)]
                dk = DWF[p, rows, pl.ds(0, 128)] + nn(w, kb)
                dv = DWF[p, rows, pl.ds(128, 128)] + nn(w, vb)
                dw = DWF[p, rows, pl.ds(256, 128)] + nt(key, kb) + nt(v, vb) + z_after
                dc = dw * w.astype(F32) * S2[l, p, rows].astype(F32)
                DU[p, rows, pl.ds(128, 128)] = dk.astype(BF)
                DU[p, rows, pl.ds(256, 128)] = dv.astype(BF)
                DU[p, rows, pl.ds(384, 128)] = dc.astype(BF)

        for k in range(2):
            scans[k].start(*to_states(order[k]))
        RUP[l, y] = split_rows(tn(FB[l], DU[y]))
        for p in range(2):
            ROUT[l, p] = split_rows(tn(GBF[...], OB[l, :, pl.ds(p * 128, 128)]))
        scans[0].step()
        scans[1].step()
        job["up"].step_1((1,))
        job["down"].start((0,))
        job["down"].step_1((1,))
        job["out"].start()
        within(order[0])
        within(order[1])
        if before:
            for name in ("qk", "vc", "out"):
                before[name].step_2()
            mixed_hop_2 = spread_on(0, mixed_hop)
        job["up"].step_1((0,))
        for k in range(2):
            p = order[k]
            with_later(k, p)
            grads = split_rows(tn(AB[l], DU[p]))
            RQK[l, p] = grads[..., :256]
            RVC[l, p] = grads[..., 256:]
            if k == 0:
                job["vc"].start()
                job["qk"].start((1,))
            else:
                job["qk"].start((0,))
        handles = []
        for i in range(tiles):
            rows = tile_rows(i)
            part = nt(DU[0, rows], mixer_weight(l, 0))
            part = part + nt(DU[1, rows], mixer_weight(l, 1))
            handles.append(share_start(part))
        job["up"].step_2()
        job["down"].step_1((0,))
        job["down"].step_2()
        job["out"].step_1()
        if l == last:
            mixed_hop = spread(0)
        gsum = jnp.zeros((1, D), F32)
        for i in range(tiles):
            rows = tile_rows(i)
            da = share_end(handles[i])
            y_hat, rstd = norm_parts(stream(l, rows))
            gsum = gsum + jnp.sum(da * y_hat, axis=0, keepdims=True)
            da = da * gain_row(l, 0)
            dh = DMID[rows] + (
                da
                - jnp.mean(da, axis=-1, keepdims=True)
                - y_hat * jnp.mean(da * y_hat, axis=-1, keepdims=True)
            ) * rstd
            DMID[rows] = dh
            if l == 0:
                OUTB[1, y, rows] = dh.astype(BF)
        grad_norm[2 * l] = gsum

    mixed_hop_2.wait_recv()
    finals.append(local(OUTB.at[0], mixed_hbm))
    sub = lax.broadcasted_iota(jnp.int32, (8, D), 0)
    rows8 = jnp.zeros((8, D), F32)
    for k in range(2 * layers):
        rows8 = jnp.where(sub == k, grad_norm[k], rows8)
    GN[...] = rows8
    cn = send(GN, GNY, y_peer)
    job = jobs[0]
    job["qk"].step_1()
    job["vc"].step_1()
    tokens_hop = spread(1)
    job["out"].step_2()
    for l in range(1, layers):
        for name in ("up", "down", "out", "qk", "vc"):
            finish(l, name)
    cn.wait_recv()
    both = rows8 + GNY[...]
    for gz in range(GROUPS // 2):
        GNR[0, gz] = both[:, gz * 128 : (gz + 1) * 128]
    gn_in = []
    for d in range(4):
        for o in range(2):
            if (d, o) == (0, 0):
                continue
            peer = (seq_of(1 - x if o else x, flip_z(d)), m)
            gn_in.append((send(GNR.at[0, flip_z(d)], GNR.at[1, 2 * d + o], peer), 2 * d + o))
    job["vc"].step_2()
    job["qk"].step_2()
    finish(0, "up")
    finish(0, "down")
    finish(0, "out")
    tokens_hop_2 = spread_on(1, tokens_hop)
    total = GNR[0, z]
    for c, k in gn_in:
        c.wait_recv()
        total = total + GNR[1, k]
    GNO[...] = total
    finals.append(local(GNO, gn_hbm))
    tokens_hop_2.wait_recv()
    finals.append(local(OUTB.at[1], gt_hbm))
    finish(0, "qk")
    finish(0, "vc")
    for c in finals:
        c.wait()
    for c in sent:
        c.wait_send()
    for c in ar_prev.values():
        c.wait_send()


def shards(tokens, lengths, norm_attn, norm_ffn, w_qkv, w_ctrl, w_out, w_up, w_down, cotangent):
    layers = w_qkv.shape[0]
    n_seq = lax.axis_size("seq")
    stride = n_seq // GROUPS
    _, T, D = tokens.shape
    rows = w_qkv.shape[1]
    weights = [w_qkv.reshape(layers, rows, -1), w_ctrl, w_up, w_down, w_out]
    gains = [norm_attn, norm_ffn]
    blocks = [[k * stride + j for j in range(stride)] for k in range(GROUPS)]
    if stride > 1:

        def fill(a):
            return lax.all_gather(a, "seq", axis=1, tiled=True, axis_index_groups=blocks)

        weights, gains = [fill(a) for a in weights], [fill(a) for a in gains]
    R = D // GROUPS
    odd = (lax.axis_index("seq") // stride) % 2
    A = weights[0].shape[-1] + w_ctrl.shape[-1]
    U = w_up.shape[-1]
    F = 2 * U + w_out.shape[-1]
    pairs = n_seq // 2
    tiles = T // TILE
    bf, f32 = BF, F32
    v = pltpu.VMEM
    remote_copies = 256
    scratch = [
        v((max(layers - 1, 1), T, D), f32),
        v((layers, T, D), f32),
        v((layers, T, D), bf),
        v((layers, T, D), bf),
        v((layers, 2, T, 384), bf),
        v((layers, 2, T, 128), bf),
        v((layers, 2, T, 128), bf),
        v((layers, 2, T, 128), f32),
        v((layers, 2, T, 128), f32),
        v((layers, 2, T, 128), f32),
        v((layers, 2, tiles, 2, TILE, TILE), bf),
        v((layers, 2, tiles, 2, TILE, TILE), bf),
        v((layers, T, 256), bf),
        v((layers, 2, T, U), bf),
        v((layers, 2, T, U), bf),
        v((layers, 2, tiles, 128, 128), bf),
        v((layers, 2, tiles, 128, 128), bf),
        v((2, max(tiles - 1, 1), 2, 128, 128), f32),
        v((2, T, D), bf),
        v((T, D), bf),
        v((2, T, 128), bf),
        v((2, T, U), bf),
        v((T, D), f32),
        v((2, tiles, 2, TILE, TILE), bf),
        v((2, T, 128), bf),
        v((2, T, 128), f32),
        v((2, T, 384), f32),
        v((layers, 2, 4, 2, R, A), bf),
        v((layers, 2, 4, 2, R, F), bf),
        v((8, 8, 128), f32),
        v((8, D), f32),
        v((tiles, TILE, D), bf),
        v((2 * tiles, TILE, D), bf),
        v((4 * layers, 144, 128), bf),
        v((4 * layers, 144, 128), bf),
        v((4 * layers, pairs - 1, 144, 128), bf),
        v((2, 144, 128), f32),
        v((layers, 2, 4, 2, R, 256), bf),
        v((layers, 2, 4, 2, R, 256), bf),
        v((layers, 2, 4, 2, R, 128), bf),
        v((layers, 2, 4, 2, R, U), bf),
        v((layers, 2, 4, 2, R, U), bf),
        v((layers, 15, R, 256), bf),
        v((layers, 15, R, 256), bf),
        v((layers, 15, R, 128), bf),
        v((layers, 15, R, U), bf),
        v((layers, 15, R, U), bf),
        v((layers, R, 384), f32),
        v((layers, R, 128), f32),
        v((layers, R, 128), f32),
        v((layers, R, U), f32),
        v((layers, R, U), f32),
        v((8, D), f32),
        v((8, D), f32),
        v((2, 8, 8, 128), f32),
        v((8, 128), f32),
        v((2, 2, T, D), bf),
        pltpu.SemaphoreType.DMA((remote_copies + 4 * layers * pairs,)),
        pltpu.SemaphoreType.DMA((remote_copies + 4 * layers * pairs,)),
        pltpu.SemaphoreType.DMA((32,)),
    ]
    any_spec = pl.BlockSpec(memory_space=pl.ANY)
    out_shape = (
        jax.ShapeDtypeStruct((2, T, D), bf),
        jax.ShapeDtypeStruct((2, T, D), bf),
        jax.ShapeDtypeStruct((layers, R, 384), f32),
        jax.ShapeDtypeStruct((layers, R, 128), f32),
        jax.ShapeDtypeStruct((layers, R, 128), f32),
        jax.ShapeDtypeStruct((layers, R, U), f32),
        jax.ShapeDtypeStruct((layers, R, U), f32),
        jax.ShapeDtypeStruct((8, 128), f32),
    )
    mixed, grad_tokens, *grads, gn = pl.pallas_call(
        functools.partial(kernel, n_seq, layers),
        out_shape=out_shape,
        in_specs=[
            any_spec,
            any_spec,
            pl.BlockSpec(memory_space=pltpu.SMEM),
            *[any_spec] * 5,
            *[pl.BlockSpec(memory_space=pltpu.VMEM)] * 2,
        ],
        out_specs=(any_spec,) * len(out_shape),
        scratch_shapes=scratch,
        compiler_params=pltpu.CompilerParams(
            collective_id=0, has_side_effects=True, vmem_limit_bytes=VMEM_BYTES
        ),
    )(tokens, cotangent, lengths, *weights, *gains)
    gn = jnp.where(odd == 0, gn[: 2 * layers, :R], gn[: 2 * layers, R : 2 * R])
    if stride > 1:

        def empty(a, dim):
            return lax.psum_scatter(
                a, "seq", scatter_dimension=dim, tiled=True, axis_index_groups=blocks
            )

        grads = [empty(a, 1) for a in grads]
        gn = empty(gn, 1)
    gn = gn.reshape(layers, 2, rows)
    return (
        mixed,
        grad_tokens.astype(F32),
        gn[:, 0],
        gn[:, 1],
        grads[0].reshape(w_qkv.shape),
        *grads[1:],
    )


VMEM_BYTES = 62 << 20


def solution(mesh):
    in_specs = (
        P(None, "seq", None),
        P(),
        P(None, "seq"),
        P(None, "seq"),
        P(None, "seq", None, "mp"),
        P(None, "seq", "mp"),
        P(None, "seq", "mp"),
        P(None, "seq", "mp"),
        P(None, "seq", "mp"),
        P(None, "seq", None),
    )
    out_specs = (
        P(None, "seq", None),
        P(None, "seq", None),
        P(None, "seq"),
        P(None, "seq"),
        P(None, "seq", None, "mp"),
        P(None, "seq", "mp"),
        P(None, "seq", "mp"),
        P(None, "seq", "mp"),
        P(None, "seq", "mp"),
    )
    return jax.shard_map(shards, mesh=mesh, in_specs=in_specs, out_specs=out_specs, check_vma=False)
```

```python
import functools

import jax
import jax.numpy as jnp
from jax import lax
from jax.experimental import pallas as pl
from jax.experimental.pallas import tpu as pltpu
from jax.sharding import PartitionSpec as P

F32 = jnp.float32
BF = jnp.bfloat16
MESH = pl.DeviceIdType.MESH
GROUPS = 8
HEAD = 64
EPS = 1e-05
TILE = 256


def nn(a, b):
    return lax.dot_general(a, b, (((1,), (0,)), ((), ())), preferred_element_type=F32)


def nt(a, b):
    return lax.dot_general(a, b, (((1,), (1,)), ((), ())), preferred_element_type=F32)


def tn(a, b):
    return lax.dot_general(a, b, (((0,), (0,)), ((), ())), preferred_element_type=F32)


def near_size(n_seq):
    return 1 << ((n_seq.bit_length() - 1) // 2)


def norm_parts(x):
    center = x - jnp.mean(x, axis=-1, keepdims=True)
    spread = jnp.mean(center * center, axis=-1, keepdims=True)
    rstd = lax.rsqrt(spread + EPS)
    return center * rstd, rstd


def gate_and_slope(u):
    u2 = u * u
    t = jnp.tanh(u * (0.7978845608 + (0.7978845608 * 0.044715) * u2))
    half = 0.5 + 0.5 * t
    gate = u * half
    slope = half + gate * (1.0 - half) * (1.5957691216 + (1.5957691216 * 0.134145) * u2)
    return gate, slope


X_FIRST = {("q", 1), ("kv", 0), ("out", 0), ("out", 1), ("down", 0), ("down", 1)}


PLAN = {
    "s0": (
        ("A", 1, "own"),
        ("A", 0, "start"),
        ("D", 0, "own"),
        ("A", 0, "own"),
        ("U", 0, "start"),
        ("U", 1, "own"),
        ("A", 0, "on"),
        ("U", 0, "own"),
        ("D", 0, "start"),
        ("A", 0, "across"),
    ),
    "s1": (
        ("U", 0, "on"),
        ("A", 0, "end"),
    ),
    "f0.1": (
        ("A", 1, "start"),
    ),
    "f0.3": (
        ("D", 0, "on"),
    ),
    "f0.4": (
        ("U", 0, "across"),
    ),
    "f0.5": (
        ("D", 0, "across"),
    ),
    "f0.6": (
        ("U", 0, "end"),
        ("U", 1, "start"),
        ("A", 1, "on"),
    ),
    "f0.7": (
        ("D", 1, "own"),
        ("D", 0, "end"),
    ),
    "f0.8": (
        ("A", 1, "across"),
    ),
    "f0.9": (
        ("D", 1, "start"),
        ("U", 1, "on"),
    ),
    "f0.10": (
        ("A", 1, "end"),
    ),
    "f1.3": (
        ("D", 1, "on"),
    ),
    "f1.4": (
        ("U", 1, "across"),
    ),
    "f1.6": (
        ("D", 1, "across"),
    ),
    "f1.7": (
        ("D", 1, "end"),
        ("U", 1, "end"),
    ),
    "b1.0": (
        ("mixed", 0, "start"),
        ("down", 1, "grad1"),
        ("down", 1, "start1"),
    ),
    "b1.1": (
        ("up", 1, "grad1"),
        ("up", 1, "start1"),
        ("down", 1, "grad0"),
    ),
    "b1.3": (
        ("up", 1, "start0"),
        ("down", 1, "start0"),
    ),
    "b1.4": (
        ("out", 1, "grad"),
    ),
    "b1.5": (
        ("up", 1, "grad0"),
    ),
    "b1.6": (
        ("up", 1, "add1"),
        ("out", 1, "start1"),
        ("out", 1, "start0"),
    ),
    "b1.7": (
        ("down", 1, "add1"),
        ("down", 1, "add0"),
    ),
    "b1.8": (
        ("c", 1, "start1"),
        ("c", 1, "start0"),
    ),
    "b1.9": (
        ("mixed", 0, "hop"),
        ("q", 1, "start1"),
        ("up", 1, "add0"),
    ),
    "b1.10": (
        ("up", 1, "turn"),
        ("q", 1, "start0"),
        ("kv", 1, "start1"),
    ),
    "b0.0": (
        ("down", 0, "grad1"),
    ),
    "b0.1": (
        ("down", 0, "start1"),
        ("down", 0, "grad0"),
        ("up", 0, "grad1"),
        ("kv", 1, "start0"),
    ),
    "b0.2": (
        ("down", 1, "turn"),
        ("q", 1, "add1"),
        ("q", 1, "add0"),
        ("out", 1, "add1"),
        ("up", 0, "start1"),
    ),
    "b0.3": (
        ("up", 0, "grad0"),
        ("c", 1, "add1"),
        ("c", 1, "add0"),
        ("kv", 1, "add1"),
    ),
    "b0.4": (
        ("up", 0, "start0"),
        ("out", 1, "add0"),
        ("kv", 1, "add0"),
        ("c", 1, "turn"),
    ),
    "b0.5": (
        ("down", 0, "start0"),
        ("out", 0, "grad"),
    ),
    "b0.6": (
        ("kv", 1, "turn"),
        ("up", 0, "add1"),
    ),
    "b0.7": (
        ("out", 0, "start0"),
        ("out", 1, "turn"),
    ),
    "b0.8": (
        ("up", 1, "end"),
        ("q", 1, "turn"),
        ("down", 0, "add1"),
    ),
    "b0.9": (
        ("up", 0, "add0"),
        ("mixed", 0, "end"),
        ("out", 0, "start1"),
        ("up", 0, "turn"),
        ("out", 1, "end"),
    ),
    "b0.10": (
        ("c", 1, "end"),
        ("kv", 0, "start1"),
        ("out", 0, "add0"),
        ("c", 0, "start1"),
        ("c", 0, "start0"),
        ("q", 0, "start1"),
        ("q", 0, "start0"),
        ("down", 0, "add0"),
    ),
    "b0.11": (
        ("down", 0, "turn"),
        ("out", 0, "add1"),
        ("kv", 0, "start0"),
        ("q", 1, "end"),
        ("kv", 0, "add1"),
        ("kv", 1, "end"),
        ("down", 1, "end"),
    ),
    "t": (
        ("c", 0, "add1"),
        ("gains", 0, "start"),
        ("out", 0, "turn"),
        ("c", 0, "add0"),
        ("q", 0, "add1"),
        ("q", 0, "add0"),
        ("up", 0, "end"),
        ("c", 0, "turn"),
        ("tokens", 0, "start"),
        ("kv", 0, "add0"),
        ("kv", 0, "turn"),
        ("q", 0, "turn"),
        ("gains", 0, "hop"),
        ("tokens", 0, "hop"),
        ("q", 0, "end"),
        ("c", 0, "end"),
        ("out", 0, "end"),
        ("kv", 0, "end"),
        ("tokens", 0, "end"),
        ("gains", 0, "end"),
        ("down", 0, "end"),
    ),
}


def kernel(
    n_seq,
    layers,
    tok_hbm,
    cot_hbm,
    len_ref,
    qkv_hbm,
    ctrl_hbm,
    up_hbm,
    down_hbm,
    out_hbm,
    norm_attn_hbm,
    norm_ffn_hbm,
    mixed_hbm,
    gt_hbm,
    gqkv_hbm,
    gctrl_hbm,
    gout_hbm,
    gup_hbm,
    gdown_hbm,
    gn_hbm,
    H,
    MID,
    AB,
    FB,
    QKV,
    WB,
    S2,
    ZS,
    PS,
    XS,
    AST,
    MST,
    OB,
    GU,
    GG,
    KP,
    VP,
    LOC,
    TOKB,
    GBF,
    DOB,
    DU,
    DMID,
    YST,
    DNB,
    DZ,
    DWF,
    WA,
    WF,
    GAIN,
    GROW,
    GFULL,
    ARS,
    ARR,
    SCS,
    SCR1,
    SCR2,
    SCP,
    RQ,
    RKV,
    RC,
    ROUT,
    RUP,
    RDN,
    LQ,
    LKV,
    LC,
    LOUT,
    LUP,
    LDN,
    OQKV,
    OCTRL,
    OOUT,
    OUP,
    ODN,
    GN,
    GNY,
    GNR,
    GNO,
    OUTB,
    send_sems,
    recv_sems,
    local_sems,
):
    T, D = TOKB.shape[1], TOKB.shape[2]
    tiles = T // TILE
    R = D // GROUPS
    stride = n_seq // GROUPS
    s = lax.axis_index("seq")
    m = lax.axis_index("mp")
    y, core = m // 2, m % 2
    g, lo = s // stride, s % stride
    x, z = g % 2, g // 2
    z1, z0 = z // 2, z % 2
    last = layers - 1

    def flip_z(d):
        d1, d0 = d // 2, d % 2
        return 2 * (1 - z1 if d1 else z1) + (1 - z0 if d0 else z0)

    def seq_of(gx, gz):
        return (gz * 2 + gx) * stride + lo

    core_peer = (s, 2 * y + (1 - core))
    y_peer = (s, 2 * (1 - y) + core)
    x_peer = (seq_of(1 - x, z), m)
    z_peer = {d: (seq_of(x, flip_z(d)), m) for d in (1, 2, 3)}
    near = near_size(n_seq)
    blocks = n_seq // near
    low, high = s % near, s // near

    used = [0, 0]
    sent = []

    def remote(src, dst, peer):
        k = used[0]
        used[0] += 1
        return pltpu.make_async_remote_copy(
            src_ref=src,
            dst_ref=dst,
            send_sem=send_sems.at[k],
            recv_sem=recv_sems.at[k],
            device_id=peer,
            device_id_type=MESH,
        )

    def send(src, dst, peer):
        c = remote(src, dst, peer)
        c.start()
        sent.append(c)
        return c

    def local(src, dst):
        k = used[1]
        used[1] += 1
        c = pltpu.make_async_copy(src, dst, local_sems.at[k])
        c.start()
        return c

    barrier = pltpu.get_barrier_semaphore()

    def hello(peer):
        pl.semaphore_signal(barrier, inc=1, device_id=peer, device_id_type=MESH)

    hello(core_peer)
    hello(y_peer)
    count = 2
    for d in range(1, near):
        hello((high * near + lax.rem(low + d, near), m))
        count += 1
    for d in range(1, blocks):
        other = lax.rem(high + d, blocks) * near
        hello((other + low, m))
        count += 1
        if stride == 1:
            hello((other + 1 - low, m))
            count += 1

    rows_in = [local(norm_attn_hbm, GROW.at[0]), local(norm_ffn_hbm, GROW.at[1])]
    own = []
    for l in range(layers):
        for k in range(4):
            src = qkv_hbm.at[l, k] if k < 3 else ctrl_hbm.at[l]
            own.append(local(src, WA.at[l, y, z, x, slice(None), pl.ds(k * 128, 128)]))
        lanes = 0
        for src in (up_hbm, down_hbm, out_hbm):
            at = pl.ds(lanes, src.shape[-1])
            own.append(local(src.at[l], WF.at[l, y, z, x, slice(None), at]))
            lanes += src.shape[-1]
    tok_copy = local(tok_hbm.at[y], TOKB.at[0])
    cot_copy = local(cot_hbm.at[y], TOKB.at[1])
    gain_sub = lax.broadcasted_iota(jnp.int32, (8, R), 0)
    own_gains = jnp.zeros((8, R), F32)
    for c in rows_in:
        c.wait()
    for l in range(layers):
        for k in range(2):
            row = GROW[k].astype(F32)[l : l + 1]
            own_gains = jnp.where(gain_sub == 2 * l + k, row, own_gains)
    GAIN[0, :, pl.ds(0, R)] = jnp.where(x == 0, own_gains, 0.0)
    GAIN[0, :, pl.ds(R, R)] = jnp.where(x == 0, 0.0, own_gains)

    pl.semaphore_wait(barrier, count)

    class Gather:
        def __init__(self, buf, l, low_end, cut, high_end):
            self.buf, self.l, self.c = buf, l, {}
            self.all = pl.ds(low_end, high_end - low_end)
            self.halves = (pl.ds(low_end, cut - low_end), pl.ds(cut, high_end - cut))

        def push(self, key, region, peer, lanes=None):
            src = self.buf.at[(self.l,) + region + (slice(None), lanes or self.all)]
            self.c[key] = send(src, src, peer)

        def start(self):
            mine = (y, z, x)
            for d in (1, 2, 3):
                self.push(("z", d), mine, z_peer[d])

        def own(self):
            mine = (y, z, x)
            self.push(("x", 0), mine, x_peer)
            self.push(("y", 0), mine, y_peer)

        def on(self):
            for d in (1, 2, 3):
                self.c["z", d].wait_recv()
                self.push(("x", d), (y, flip_z(d), x), x_peer)
                self.push(("y", d), (y, flip_z(d), x), y_peer)

        def across(self):
            first, second = self.halves
            for d in range(4):
                self.c["x", d].wait_recv()
                self.push(("xy", d), (y, flip_z(d), 1 - x), y_peer, first)
                self.c["y", d].wait_recv()
                self.push(("yx", d), (1 - y, flip_z(d), x), x_peer, second)

        def end(self):
            for d in range(4):
                self.c["xy", d].wait_recv()
                self.c["yx", d].wait_recv()

    gain_in = []
    for d in (0, 1, 2, 3):
        for o in (0, 1):
            if (d, o) == (0, 0):
                continue
            peer = (seq_of(1 - x if o else x, flip_z(d)), m)
            gain_in.append(send(GAIN.at[0], GAIN.at[d * 2 + o], peer))
    for c in own:
        c.wait()
    gathers = {}
    for l in range(layers):
        gathers["A", l] = Gather(WA, l, 0, 256, 512)
        gathers["U", l] = Gather(WF, l, 0, 256, 512)
        gathers["D", l] = Gather(WF, l, 512, 896, 1152)
    jobs = {}

    def at(slot):
        for name, l, what in PLAN.get(slot, ()):
            if (name, l) in gathers:
                getattr(gathers[name, l], what)()
            else:
                jobs[name, l][what]()

    at("s0")

    lane = lax.broadcasted_iota(jnp.int32, (TILE, 128), 1)
    first = lane < HEAD
    head_rows = [
        (lax.broadcasted_iota(jnp.int32, (1, 128), 1) < HEAD).astype(F32).astype(BF),
        (lax.broadcasted_iota(jnp.int32, (1, 128), 1) >= HEAD).astype(F32).astype(BF),
    ]
    rr = lax.broadcasted_iota(jnp.int32, (TILE, TILE), 0)
    cc = lax.broadcasted_iota(jnp.int32, (TILE, TILE), 1)
    lower = rr >= cc
    lower_ones = lower.astype(F32).astype(BF)
    upper_ones = (rr <= cc).astype(F32).astype(BF)
    diag = (lax.broadcasted_iota(jnp.int32, (128, 128), 0) < HEAD) == (
        lax.broadcasted_iota(jnp.int32, (128, 128), 1) < HEAD
    )

    def per_head(value):
        a = jnp.sum(jnp.where(first, value, 0.0), axis=-1, keepdims=True)
        b = jnp.sum(jnp.where(first, 0.0, value), axis=-1, keepdims=True)
        return jnp.where(first, a, b)

    def per_head_max(value):
        a = jnp.max(jnp.where(first, value, -jnp.inf), axis=-1, keepdims=True)
        b = jnp.max(jnp.where(first, -jnp.inf, value), axis=-1, keepdims=True)
        return jnp.where(first, a, b)

    def heads(value):
        return value * head_rows[0], value * head_rows[1]

    def tile_rows(i):
        return pl.ds(i * TILE, TILE)

    def weight(buf, l, p, start, width):
        return buf[l, p, :, :, :, pl.ds(start, width)].reshape(D, width)

    def mixer_weight(l, p):
        return weight(WA, l, p, 0, 512)

    def up_weight(l, p):
        return weight(WF, l, p, 0, 512)

    def down_weight(l, p):
        return weight(WF, l, p, 512, 512)

    def out_weight(l, p):
        return weight(WF, l, p, 1024, 128)

    ar_used = [0]
    ar_prev = {}

    def share_start(value):
        k = ar_used[0]
        ar_used[0] += 1
        slot = k % ARS.shape[0]
        if slot in ar_prev:
            ar_prev[slot].wait_send()
        ARS[slot] = value.astype(BF)
        k = k % ARR.shape[0]
        c = remote(ARS.at[slot], ARR.at[k], core_peer)
        c.start()
        ar_prev[slot] = c
        return c, slot, k

    def share_end(handle):
        c, slot, k = handle
        c.wait_recv()
        return ARS[slot].astype(F32) + ARR[k].astype(F32)

    class Scan:
        def __init__(self, call, forward):
            self.call, self.forward = call, forward

        def pack_normalizer(self, which, part):
            sub = lax.broadcasted_iota(jnp.int32, (16, 128), 0)
            rest = jnp.zeros((16, 128), F32)
            for k in range(3):
                piece = part.astype(BF).astype(F32)
                rest = jnp.where(sub == k, piece, rest)
                part = part - piece
            SCS[which, pl.ds(128, 16)] = rest.astype(BF)

        def start(self, k_state, v_state, z_row):
            which = self.call
            SCS[which, pl.ds(0, 128)] = (k_state + pltpu.roll(v_state, HEAD, 1)).astype(BF)
            self.pack_normalizer(which, z_row)
            self.near = []
            for d in range(1, near):
                peer = (high * near + lax.rem(low + d, near), m)
                c = remote(SCS.at[which], SCR1.at[self.call, d - 1], peer)
                c.start()
                self.near.append(c)

        def step(self):
            for c in self.near:
                c.wait()
            which = self.call
            both = SCS[which].astype(F32)
            for d in range(1, near):
                both = both + SCR1[self.call, d - 1].astype(F32)
            SCS[which, pl.ds(0, 128)] = both[:128].astype(BF)
            self.pack_normalizer(which, jnp.sum(both[128:131], axis=0, keepdims=True))
            self.links = []
            for d in range(1, blocks):
                to = high + d if self.forward else high - d
                frm = high - d if self.forward else high + d
                inside = to < blocks if self.forward else to >= 0
                comes = frm >= 0 if self.forward else frm < blocks
                target = jnp.where(inside, to, high)
                c = remote(SCS.at[which], SCR2.at[self.call, d - 1], (target * near + low, m))

                @pl.when(inside)
                def _(c=c):
                    c.start()

                self.links.append((c, inside, comes))

        def end(self):
            acc = SCP.at[self.call % 2]
            before = jnp.zeros(acc.shape, F32)
            for d in range(1, near):
                mine = low >= d if self.forward else low < d
                before = before + jnp.where(mine, SCR1[self.call, d - 1].astype(F32), 0.0)
            acc[...] = before
            for d, (c, inside, comes) in enumerate(self.links):

                @pl.when(comes)
                def _(c=c, d=d):
                    c.wait_recv()
                    acc[...] += SCR2[self.call, d].astype(F32)

            for c, inside, comes in self.links:

                @pl.when(inside)
                def _(c=c):
                    c.wait_send()

            block = acc[pl.ds(0, 128)]
            k_state = jnp.where(diag, block, 0.0)
            v_state = pltpu.roll(jnp.where(diag, 0.0, block), HEAD, 1)
            return k_state, v_state, jnp.sum(acc[pl.ds(128, 3)], axis=0, keepdims=True)

    every = slice(None)

    def add_to(buf, at, more):
        buf[at] = (buf[at].astype(F32) + more.astype(F32)).astype(BF)

    class Scatter:
        def __init__(self, buf, land, l, x_first):
            self.buf, self.land, self.l, self.x_first = buf, land, l, x_first
            self.first_peer = x_peer if x_first else y_peer
            self.next_peer = y_peer if x_first else x_peer

        def block(self, first_other, next_other):
            ox, oy = (first_other, next_other) if self.x_first else (next_other, first_other)
            return (self.l, 1 - y if oy else y, every, 1 - x if ox else x)

        c1 = None

        def start(self, o):
            self.c1 = self.c1 or {}
            src = self.buf.at[self.block(1, o)]
            self.c1[o] = send(src, self.land.at[self.l, pl.ds(4 * o, 4)], self.first_peer)

        def add(self, o):
            self.c1[o].wait_recv()
            at_ = self.block(0, o)
            add_to(self.buf, at_, self.land[self.l, pl.ds(4 * o, 4)])
            if o:
                self.c2 = send(self.buf.at[at_], self.land.at[self.l, pl.ds(8, 4)], self.next_peer)

        def turn(self):
            self.c2.wait_recv()
            self.c3 = {}
            for d in (1, 2, 3, 0):
                at = (self.l, y, flip_z(d), x)
                add_to(self.buf, at, self.land[self.l, 8 + flip_z(d)])
                if d:
                    self.c3[d] = send(self.buf.at[at], self.land.at[self.l, 11 + d], z_peer[d])

        def end(self):
            total = self.buf[self.l, y, z, x].astype(F32)
            for d in (1, 2, 3):
                self.c3[d].wait_recv()
                total = total + self.land[self.l, 11 + d].astype(F32)
            return total

    finals = []

    def finish(l, name):
        total = scatters[name, l].end()
        if name == "up":
            OUP[l] = total
            finals.append(local(OUP.at[l], gup_hbm.at[l]))
        elif name == "down":
            ODN[l] = total
            finals.append(local(ODN.at[l], gdown_hbm.at[l]))
        elif name == "out":
            OOUT[l] = total
            finals.append(local(OOUT.at[l], gout_hbm.at[l]))
        elif name == "q":
            OQKV[l, 0] = total
        elif name == "kv":
            OQKV[l, 1] = total[:, :128]
            OQKV[l, 2] = total[:, 128:]
            finals.append(local(OQKV.at[l], gqkv_hbm.at[l]))
        else:
            OCTRL[l] = total
            finals.append(local(OCTRL.at[l], gctrl_hbm.at[l]))

    def split_rows(value):
        return value.astype(BF).reshape(4, 2, R, value.shape[-1])

    def grad_up(l, o):
        yy = 1 - y if o else y
        RUP[l, yy] = split_rows(tn(FB[l], DU[yy]))

    def grad_down(l, o):
        yy = 1 - y if o else y
        RDN[l, yy] = split_rows(tn(GBF[...], GG[l, yy]))

    def grad_out(l):
        grads = tn(GBF[...], OB[l])
        for p in range(2):
            ROUT[l, p] = split_rows(grads[:, p * 128 : (p + 1) * 128])

    scatters = {}
    for l in range(layers):
        for name, buf, land in (
            ("q", RQ, LQ),
            ("kv", RKV, LKV),
            ("c", RC, LC),
            ("out", ROUT, LOUT),
            ("up", RUP, LUP),
            ("down", RDN, LDN),
        ):
            f = Scatter(buf, land, l, (name, l) in X_FIRST)
            scatters[name, l] = f
            jobs[name, l] = dict(
                start1=functools.partial(f.start, 1),
                start0=functools.partial(f.start, 0),
                add1=functools.partial(f.add, 1),
                add0=functools.partial(f.add, 0),
                turn=f.turn,
                end=functools.partial(finish, l, name),
            )
        for name, f in (("up", grad_up), ("down", grad_down)):
            jobs[name, l]["grad1"] = functools.partial(f, l, 1)
            jobs[name, l]["grad0"] = functools.partial(f, l, 0)
        jobs["out", l]["grad"] = functools.partial(grad_out, l)

    tok_copy.wait()
    cot_copy.wait()
    for c in gain_in:
        c.wait_recv()
    for gz in range(GROUPS // 2):
        total = jnp.zeros((8, 128), F32)
        for d in range(4):
            here = flip_z(d) == gz
            total = total + jnp.where(here, GAIN[2 * d] + GAIN[2 * d + 1], 0.0)
        GFULL[:, pl.ds(gz * 128, 128)] = total

    def gain_row(l, which):
        return GFULL[pl.ds(2 * l + which, 1), :]

    def stream(l, rows):
        return TOKB[0, rows].astype(F32) if l == 0 else H[l - 1, rows]

    def attn_norm(l, i):
        rows = tile_rows(i)
        y_hat, _ = norm_parts(stream(l, rows))
        AB[l, rows] = (y_hat * gain_row(l, 0)).astype(BF)

    for i in range(tiles):
        attn_norm(0, i)

    at("s1")

    for l in range(layers):
        more_layers = l + 1 < layers
        at(f"f{l}.0")
        scans = [Scan(2 * l + p, True) for p in range(2)]

        def project_pair(p, l=l):
            out = nn(AB[l], mixer_weight(l, p))
            kv = out[:, 128:384].astype(BF)
            th = jnp.tanh(out[:, 384:] * (1.0 / 16.0))
            w = jnp.exp(16.0 * th).astype(BF)
            sums = [
                (
                    tn(w[j * TILE : (j + 1) * TILE], kv[j * TILE : (j + 1) * TILE]),
                    jnp.sum(w[j * TILE : (j + 1) * TILE].astype(F32), axis=0, keepdims=True),
                )
                for j in range(tiles)
            ]
            ks, vs, zs = 0.0, 0.0, 0.0
            for j, (both, z_j) in enumerate(sums):
                k_j = jnp.where(diag, both[:, :128], 0.0)
                v_j = jnp.where(diag, both[:, 128:], 0.0)
                if j < tiles - 1:
                    LOC[p, j, 0] = k_j
                    LOC[p, j, 1] = v_j
                ks, vs, zs = ks + k_j, vs + v_j, zs + z_j
            QKV[l, p, :, pl.ds(0, 128)] = out[:, :128].astype(BF)
            QKV[l, p, :, pl.ds(128, 256)] = kv
            WB[l, p] = w
            S2[l, p] = (1.0 - th * th).astype(BF)
            return ks, vs, zs

        def inside_block(p, l=l):
            units = range(tiles)
            w = [WB[l, p, tile_rows(j)] for j in units]
            q = [QKV[l, p, tile_rows(j), pl.ds(0, 128)] for j in units]
            k = [QKV[l, p, tile_rows(j), pl.ds(128, 128)] for j in units]
            qs = [heads(q[j]) for j in units]
            a = [[jnp.where(lower, nt(qs[j][h], k[j]), 0.0).astype(BF) for h in (0, 1)] for j in units]
            sums = [nn(lower_ones, w[j]) for j in units]
            ws = [heads(w[j]) for j in units]
            num = [nn(a[j][0], ws[j][0]) + nn(a[j][1], ws[j][1]) for j in units]
            for j in units:
                for h in (0, 1):
                    AST[l, p, j, h] = a[j][h]
                ZS[l, p, tile_rows(j)] = sums[j]
                XS[l, p, tile_rows(j)] = num[j]

        def with_earlier(states, l=l):
            units = [(p, j) for p in range(2) for j in range(tiles)]
            ks, vs, z_before = {}, {}, {}
            for p, j in units:
                if j == 0:
                    k_pre, v_pre, z_pre = states[p]
                else:
                    k_pre = k_pre + LOC[p, j - 1, 0]
                    v_pre = v_pre + LOC[p, j - 1, 1]
                    z_pre = z_pre + jnp.sum(
                        WB[l, p, tile_rows(j - 1)].astype(F32), axis=0, keepdims=True
                    )
                ks[p, j], vs[p, j], z_before[p, j] = k_pre.astype(BF), v_pre.astype(BF), z_pre
            w = {(p, j): WB[l, p, tile_rows(j)] for p, j in units}
            q = {(p, j): QKV[l, p, tile_rows(j), pl.ds(0, 128)] for p, j in units}
            v = {(p, j): QKV[l, p, tile_rows(j), pl.ds(256, 128)] for p, j in units}
            inv = {(p, j): 1.0 / (ZS[l, p, tile_rows(j)] + z_before[p, j]) for p, j in units}
            num = {(p, j): XS[l, p, tile_rows(j)] for p, j in units}
            xs = {u: (num[u] + nt(q[u], ks[u])) * inv[u] * 0.125 for u in units}
            e = {u: jnp.exp(xs[u] - per_head_max(xs[u])) for u in units}
            prob = {u: e[u] / per_head(e[u]) for u in units}
            scaled = {u: (prob[u] * inv[u]).astype(BF) for u in units}
            rs = {u: heads(scaled[u]) for u in units}
            mm = {
                u: [jnp.where(lower, nt(rs[u][h], w[u]), 0.0).astype(BF) for h in (0, 1)]
                for u in units
            }
            vh = {u: heads(v[u]) for u in units}
            out = {
                u: nn(scaled[u], vs[u]) + nn(mm[u][0], vh[u][0]) + nn(mm[u][1], vh[u][1])
                for u in units
            }
            for p, j in units:
                rows = tile_rows(j)
                KP[l, p, j] = ks[p, j]
                VP[l, p, j] = vs[p, j]
                ZS[l, p, rows] = inv[p, j]
                XS[l, p, rows] = xs[p, j]
                PS[l, p, rows] = prob[p, j]
                for h in (0, 1):
                    MST[l, p, j, h] = mm[p, j][h]
                OB[l, rows, pl.ds(p * 128, 128)] = out[p, j].astype(BF)

        for p in range(2):
            scans[p].start(*project_pair(p))
            at(f"f{l}.{1 + p}")
        for p in range(2):
            inside_block(p)
            at(f"f{l}.{3 + 2 * p}")
            scans[p].step()
            at(f"f{l}.{4 + 2 * p}")
        with_earlier([scans[0].end(), scans[1].end()])
        at(f"f{l}.7")

        handles = []
        for i in range(tiles):
            rows = tile_rows(i)
            part = nt(OB[l, rows, pl.ds(0, 128)], out_weight(l, 0))
            part = part + nt(OB[l, rows, pl.ds(128, 128)], out_weight(l, 1))
            handles.append(share_start(part))
        at(f"f{l}.8")
        more = []
        for i in range(tiles):
            rows = tile_rows(i)
            mid = stream(l, rows) + share_end(handles[i])
            y_hat, _ = norm_parts(mid)
            f = (y_hat * gain_row(l, 1)).astype(BF)
            hidden = [nn(f, up_weight(l, p)) for p in range(2)]
            gates = [gate_and_slope(u) for u in hidden]
            low_gates = [gate.astype(BF) for gate, _ in gates]
            part = nt(low_gates[0], down_weight(l, 0)) + nt(low_gates[1], down_weight(l, 1))
            more.append(share_start(part))
            MID[l, rows] = mid
            FB[l, rows] = f
            for p in range(2):
                GG[l, p, rows] = low_gates[p]
                GU[l, p, rows] = gates[p][1].astype(BF)
            at(f"f{l}.{9 + i}")
        if more_layers:
            for i in range(tiles):
                rows = tile_rows(i)
                H[l, rows] = MID[l, rows] + share_end(more[i])
                attn_norm(l + 1, i)
            at(f"f{l}.11")

    length = len_ref[y]

    def valid_rows(i):
        row = lax.broadcasted_iota(jnp.int32, (TILE, 1), 0)
        return jnp.where(s * T + i * TILE + row < length, 1.0, 0.0)

    half_rows = pl.ds(pl.multiple_of(core * (T // 2), T // 2), T // 2)

    class Spread:
        def __init__(self, k, out):
            self.k, self.out = k, out

        def start(self):
            src = OUTB.at[self.k, y, half_rows]
            self.c = send(src, src, y_peer)

        def hop(self):
            self.c.wait_recv()
            src = OUTB.at[self.k, 1 - y, half_rows]
            self.c = send(src, src, core_peer)

        def end(self):
            self.c.wait_recv()
            finals.append(local(OUTB.at[self.k], self.out))

    for name, f in (("mixed", Spread(0, mixed_hbm)), ("tokens", Spread(1, gt_hbm))):
        jobs[name, 0] = dict(start=f.start, hop=f.hop, end=f.end)

    for i in range(tiles):
        rows = tile_rows(i)
        out = MID[last, rows] + share_end(more[i])
        keep = valid_rows(i)
        OUTB[0, y, rows] = (out * keep).astype(BF)
        DMID[rows] = TOKB[1, rows].astype(F32) * keep

    grad_norm = [None] * (2 * layers)

    for l in range(last, -1, -1):
        for i in range(tiles):
            GBF[tile_rows(i)] = DMID[tile_rows(i)].astype(BF)
        at(f"b{l}.0")
        handles = []
        for i in range(tiles):
            rows = tile_rows(i)
            gb = GBF[rows]
            du = [
                (nn(gb, down_weight(l, p)) * GU[l, p, rows].astype(F32)).astype(BF)
                for p in range(2)
            ]
            part = nt(du[0], up_weight(l, 0)) + nt(du[1], up_weight(l, 1))
            handles.append(share_start(part))
            for p in range(2):
                DU[p, rows] = du[p]
        at(f"b{l}.1")
        gsum = jnp.zeros((1, D), F32)
        for i in range(tiles):
            rows = tile_rows(i)
            df = share_end(handles[i])
            y_hat, rstd = norm_parts(MID[l, rows])
            gsum = gsum + jnp.sum(df * y_hat, axis=0, keepdims=True)
            df = df * gain_row(l, 1)
            dm = DMID[rows] + (
                df
                - jnp.mean(df, axis=-1, keepdims=True)
                - y_hat * jnp.mean(df * y_hat, axis=-1, keepdims=True)
            ) * rstd
            DMID[rows] = dm
            GBF[rows] = dm.astype(BF)
            for p in range(2):
                DOB[p, rows] = nn(GBF[rows], out_weight(l, p)).astype(BF)
        grad_norm[2 * l + 1] = gsum
        at(f"b{l}.2")

        scans = [Scan(2 * layers + 2 * (last - l) + k, False) for k in range(2)]
        order = (1 - y, y)

        def to_states(l=l):
            units = [(k, j) for k in range(2) for j in range(tiles - 1, -1, -1)]
            rows = {u: tile_rows(u[1]) for u in units}
            w = {(k, j): WB[l, order[k], rows[k, j]] for k, j in units}
            q = {(k, j): QKV[l, order[k], rows[k, j], pl.ds(0, 128)] for k, j in units}
            v = {(k, j): QKV[l, order[k], rows[k, j], pl.ds(256, 128)] for k, j in units}
            do = {(k, j): DOB[order[k], rows[k, j]] for k, j in units}
            inv = {(k, j): ZS[l, order[k], rows[k, j]] for k, j in units}
            prob = {(k, j): PS[l, order[k], rows[k, j]] for k, j in units}
            xs = {(k, j): XS[l, order[k], rows[k, j]] for k, j in units}
            v_pre = {(k, j): VP[l, order[k], j] for k, j in units}
            ws = {u: heads(w[u]) for u in units}
            dos = {u: heads(do[u]) for u in units}
            pair = {
                u: [jnp.where(lower, nt(dos[u][h], v[u]), 0.0).astype(BF) for h in (0, 1)]
                for u in units
            }
            dr = {
                u: nt(do[u], v_pre[u]) + nn(pair[u][0], ws[u][0]) + nn(pair[u][1], ws[u][1])
                for u in units
            }
            dp = {u: dr[u] * inv[u] for u in units}
            dx = {u: prob[u] * (dp[u] - per_head(dp[u] * prob[u])) for u in units}
            dn = {u: (dx[u] * inv[u] * 0.125).astype(BF) for u in units}
            r = {u: (prob[u] * inv[u]).astype(BF) for u in units}
            dz = {
                u: -(r[u].astype(F32) * dp[u]) - 8.0 * dn[u].astype(F32) * xs[u] for u in units
            }
            dk = {u: jnp.where(diag, tn(dn[u], q[u]), 0.0) for u in units}
            dv = {u: jnp.where(diag, tn(r[u], do[u]), 0.0) for u in units}
            totals = []
            for k in range(2):
                total = [0.0, 0.0, 0.0]
                for j in range(tiles):
                    dzs = jnp.sum(dz[k, j], axis=0, keepdims=True)
                    total = [a + b for a, b in zip(total, (dk[k, j], dv[k, j], dzs))]
                totals.append(total)
            for k, j in units:
                p = order[k]
                for h in (0, 1):
                    YST[p, j, h] = pair[k, j][h]
                DNB[p, rows[k, j]] = dn[k, j]
                DZ[p, rows[k, j]] = dz[k, j]
                if j > 0:
                    LOC[p, j - 1, 0] = dk[k, j]
                    LOC[p, j - 1, 1] = dv[k, j]
            return totals

        def within(p, l=l):
            units = range(tiles)
            rows = [tile_rows(j) for j in units]
            w = [WB[l, p, rows[j]] for j in units]
            q = [QKV[l, p, rows[j], pl.ds(0, 128)] for j in units]
            k = [QKV[l, p, rows[j], pl.ds(128, 128)] for j in units]
            do = [DOB[p, rows[j]] for j in units]
            dn = [DNB[p, rows[j]] for j in units]
            r = [(PS[l, p, rows[j]] * ZS[l, p, rows[j]]).astype(BF) for j in units]
            dz = [DZ[p, rows[j]] for j in units]
            k_pre = [KP[l, p, j] for j in units]
            dz_hi = [dz[j].astype(BF) for j in units]
            dz_lo = [(dz[j] - dz_hi[j].astype(F32)).astype(BF) for j in units]
            dns, rs, dos, qs, ks = ([heads(a[j]) for j in units] for a in (dn, r, do, q, k))
            da = [
                [jnp.where(lower, nt(dns[j][h], w[j]), 0.0).astype(BF) for h in (0, 1)]
                for j in units
            ]
            dq = [
                nn(dn[j], k_pre[j]) + nn(da[j][0], ks[j][0]) + nn(da[j][1], ks[j][1]) for j in units
            ]
            dk = [tn(da[j][0], qs[j][0]) + tn(da[j][1], qs[j][1]) for j in units]
            dv = [
                tn(MST[l, p, j, 0], dos[j][0]) + tn(MST[l, p, j, 1], dos[j][1]) for j in units
            ]
            dw = [
                nn(upper_ones, dz_hi[j])
                + nn(upper_ones, dz_lo[j])
                + tn(YST[p, j, 0], rs[j][0])
                + tn(AST[l, p, j, 0], dns[j][0])
                + tn(YST[p, j, 1], rs[j][1])
                + tn(AST[l, p, j, 1], dns[j][1])
                for j in units
            ]
            for j in units:
                DU[p, rows[j], pl.ds(0, 128)] = dq[j].astype(BF)
                DWF[p, rows[j], pl.ds(0, 128)] = dk[j]
                DWF[p, rows[j], pl.ds(128, 128)] = dv[j]
                DWF[p, rows[j], pl.ds(256, 128)] = dw[j]

        def with_later(k, p, l=l):
            k_post, v_post, z_after = scans[k].end()
            for j in range(tiles - 1, -1, -1):
                rows = tile_rows(j)
                if j < tiles - 1:
                    k_post = k_post + LOC[p, j, 0]
                    v_post = v_post + LOC[p, j, 1]
                    z_after = z_after + jnp.sum(DZ[p, tile_rows(j + 1)], axis=0, keepdims=True)
                kb, vb = k_post.astype(BF), v_post.astype(BF)
                w = WB[l, p, rows]
                key = QKV[l, p, rows, pl.ds(128, 128)]
                v = QKV[l, p, rows, pl.ds(256, 128)]
                dk = DWF[p, rows, pl.ds(0, 128)] + nn(w, kb)
                dv = DWF[p, rows, pl.ds(128, 128)] + nn(w, vb)
                dw = DWF[p, rows, pl.ds(256, 128)] + nt(key, kb) + nt(v, vb) + z_after
                dc = dw * w.astype(F32) * S2[l, p, rows].astype(F32)
                DU[p, rows, pl.ds(128, 128)] = dk.astype(BF)
                DU[p, rows, pl.ds(256, 128)] = dv.astype(BF)
                DU[p, rows, pl.ds(384, 128)] = dc.astype(BF)

        totals = to_states()
        for k in range(2):
            scans[k].start(*totals[k])
        at(f"b{l}.3")
        for k in range(2):
            scans[k].step()
            at(f"b{l}.{4 + k}")
        for k in range(2):
            p = order[k]
            within(p)
            RQ[l, p] = split_rows(tn(AB[l], DU[p, :, pl.ds(0, 128)]))
            at(f"b{l}.{6 + k}")
        for k in range(2):
            p = order[k]
            with_later(k, p)
            grads = split_rows(tn(AB[l], DU[p, :, pl.ds(128, 384)]))
            RKV[l, p] = grads[..., :256]
            RC[l, p] = grads[..., 256:]
            at(f"b{l}.{8 + k}")
        handles = []
        for i in range(tiles):
            rows = tile_rows(i)
            part = nt(DU[0, rows], mixer_weight(l, 0))
            part = part + nt(DU[1, rows], mixer_weight(l, 1))
            handles.append(share_start(part))
        at(f"b{l}.10")
        gsum = jnp.zeros((1, D), F32)
        for i in range(tiles):
            rows = tile_rows(i)
            da = share_end(handles[i])
            y_hat, rstd = norm_parts(stream(l, rows))
            gsum = gsum + jnp.sum(da * y_hat, axis=0, keepdims=True)
            da = da * gain_row(l, 0)
            dh = DMID[rows] + (
                da
                - jnp.mean(da, axis=-1, keepdims=True)
                - y_hat * jnp.mean(da * y_hat, axis=-1, keepdims=True)
            ) * rstd
            DMID[rows] = dh
            if l == 0:
                OUTB[1, y, rows] = dh.astype(BF)
        grad_norm[2 * l] = gsum
        at(f"b{l}.11")

    class Gains:
        def start(self):
            sub = lax.broadcasted_iota(jnp.int32, (8, D), 0)
            self.rows = jnp.zeros((8, D), F32)
            for k in range(2 * layers):
                self.rows = jnp.where(sub == k, grad_norm[k], self.rows)
            GN[...] = self.rows
            self.c = send(GN, GNY, y_peer)

        def hop(self):
            self.c.wait_recv()
            both = self.rows + GNY[...]
            for gz in range(GROUPS // 2):
                GNR[0, gz] = both[:, gz * 128 : (gz + 1) * 128]
            self.c = []
            for d in range(4):
                for o in range(2):
                    if (d, o) == (0, 0):
                        continue
                    peer = (seq_of(1 - x if o else x, flip_z(d)), m)
                    k = 2 * d + o
                    self.c.append((send(GNR.at[0, flip_z(d)], GNR.at[1, k], peer), k))

        def end(self):
            total = GNR[0, z]
            for c, k in self.c:
                c.wait_recv()
                total = total + GNR[1, k]
            GNO[...] = total
            finals.append(local(GNO, gn_hbm))

    f = Gains()
    jobs["gains", 0] = dict(start=f.start, hop=f.hop, end=f.end)
    at("t")
    for c in finals:
        c.wait()
    for c in sent:
        c.wait_send()
    for c in ar_prev.values():
        c.wait_send()


def lay_out(stride, *refs):
    mixed, tokens, qkv, ctrl, out, up, down, gains = refs[:8]
    mixed_out, tokens_out, attn_out, ffn_out, *weights_out = refs[8:17]
    wide, sems, *held = refs[17:]
    arrays = (tokens, mixed, up, down, qkv, ctrl, out)
    results = (None, mixed_out, weights_out[3], weights_out[4], *weights_out[:3])
    parts = [(k, b) for k in range(len(arrays)) for b in range(2)]
    ins = {
        (k, b): pltpu.make_async_copy(arrays[k].at[b], held[k].at[b], sems.at[0, k, b])
        for k, b in parts
    }
    for c in ins.values():
        c.start()
    x = (lax.axis_index("seq") // stride) % 2
    R = attn_out.shape[1]
    rows = jnp.where(x == 0, gains[:, pl.ds(0, R)], gains[:, pl.ds(R, R)])
    for l in range(attn_out.shape[0]):
        attn_out[pl.ds(l, 1), :] = rows[2 * l : 2 * l + 1]
        ffn_out[pl.ds(l, 1), :] = rows[2 * l + 1 : 2 * l + 2]
    outs = []
    for k, b in parts:
        ins[k, b].wait()
        if k == 0:
            wide[b] = held[0][b].astype(F32)
            c = pltpu.make_async_copy(wide.at[b], tokens_out.at[b], sems.at[1, k, b])
        else:
            c = pltpu.make_async_copy(held[k].at[b], results[k].at[b], sems.at[1, k, b])
        c.start()
        outs.append(c)
    for c in outs:
        c.wait()


def shards(tokens, lengths, norm_attn, norm_ffn, w_qkv, w_ctrl, w_out, w_up, w_down, cotangent):
    layers = w_qkv.shape[0]
    n_seq = lax.axis_size("seq")
    stride = n_seq // GROUPS
    _, T, D = tokens.shape
    rows = w_qkv.shape[1]
    weights = [w_qkv.transpose(0, 2, 1, 3), w_ctrl, w_up, w_down, w_out]
    gains = [norm_attn, norm_ffn]
    blocks = [[k * stride + j for j in range(stride)] for k in range(GROUPS)]
    if stride > 1:

        def fill(a, dim=1):
            return lax.all_gather(a, "seq", axis=dim, tiled=True, axis_index_groups=blocks)

        weights = [fill(a, a.ndim - 2) for a in weights]
        gains = [fill(a) for a in gains]
    R = D // GROUPS
    A = 3 * w_qkv.shape[-1] + w_ctrl.shape[-1]
    U = w_up.shape[-1]
    F = 2 * U + w_out.shape[-1]
    near = near_size(n_seq)
    far = n_seq // near
    tiles = T // TILE
    bf, f32 = BF, F32
    v = pltpu.VMEM
    remote_copies = 256
    scratch = [
        v((max(layers - 1, 1), T, D), f32),
        v((layers, T, D), f32),
        v((layers, T, D), bf),
        v((layers, T, D), bf),
        v((layers, 2, T, 384), bf),
        v((layers, 2, T, 128), bf),
        v((layers, 2, T, 128), bf),
        v((layers, 2, T, 128), f32),
        v((layers, 2, T, 128), f32),
        v((layers, 2, T, 128), f32),
        v((layers, 2, tiles, 2, TILE, TILE), bf),
        v((layers, 2, tiles, 2, TILE, TILE), bf),
        v((layers, T, 256), bf),
        v((layers, 2, T, U), bf),
        v((layers, 2, T, U), bf),
        v((layers, 2, tiles, 128, 128), bf),
        v((layers, 2, tiles, 128, 128), bf),
        v((2, max(tiles - 1, 1), 2, 128, 128), f32),
        v((2, T, D), bf),
        v((T, D), bf),
        v((2, T, 128), bf),
        v((2, T, U), bf),
        v((T, D), f32),
        v((2, tiles, 2, TILE, TILE), bf),
        v((2, T, 128), bf),
        v((2, T, 128), f32),
        v((2, T, 384), f32),
        v((layers, 2, 4, 2, R, A), bf),
        v((layers, 2, 4, 2, R, F), bf),
        v((8, 8, 128), f32),
        v((2, layers, R), bf),
        v((8, D), f32),
        v((tiles, TILE, D), bf),
        v((2 * tiles, TILE, D), bf),
        v((4 * layers, 144, 128), bf),
        v((4 * layers, near - 1, 144, 128), bf),
        v((4 * layers, far - 1, 144, 128), bf),
        v((2, 144, 128), f32),
        v((layers, 2, 4, 2, R, 128), bf),
        v((layers, 2, 4, 2, R, 256), bf),
        v((layers, 2, 4, 2, R, 128), bf),
        v((layers, 2, 4, 2, R, 128), bf),
        v((layers, 2, 4, 2, R, U), bf),
        v((layers, 2, 4, 2, R, U), bf),
        v((layers, 15, R, 128), bf),
        v((layers, 15, R, 256), bf),
        v((layers, 15, R, 128), bf),
        v((layers, 15, R, 128), bf),
        v((layers, 15, R, U), bf),
        v((layers, 15, R, U), bf),
        v((layers, 3, R, 128), f32),
        v((layers, R, 128), f32),
        v((layers, R, 128), f32),
        v((layers, R, U), f32),
        v((layers, R, U), f32),
        v((8, D), f32),
        v((8, D), f32),
        v((2, 8, 8, 128), f32),
        v((8, 128), f32),
        v((2, 2, T, D), bf),
        pltpu.SemaphoreType.DMA((remote_copies + 4 * layers * (near + far),)),
        pltpu.SemaphoreType.DMA((remote_copies + 4 * layers * (near + far),)),
        pltpu.SemaphoreType.DMA((32,)),
    ]
    any_spec = pl.BlockSpec(memory_space=pl.ANY)
    out_shape = (
        jax.ShapeDtypeStruct((2, T, D), bf),
        jax.ShapeDtypeStruct((2, T, D), bf),
        jax.ShapeDtypeStruct((layers, 3, R, 128), f32),
        jax.ShapeDtypeStruct((layers, R, 128), f32),
        jax.ShapeDtypeStruct((layers, R, 128), f32),
        jax.ShapeDtypeStruct((layers, R, U), f32),
        jax.ShapeDtypeStruct((layers, R, U), f32),
        jax.ShapeDtypeStruct((8, 128), f32),
    )
    mixed, grad_tokens, *grads, gn = pl.pallas_call(
        functools.partial(kernel, n_seq, layers),
        out_shape=out_shape,
        in_specs=[
            any_spec,
            any_spec,
            pl.BlockSpec(memory_space=pltpu.SMEM),
            *[any_spec] * 7,
        ],
        out_specs=(any_spec,) * len(out_shape),
        scratch_shapes=scratch,
        compiler_params=pltpu.CompilerParams(
            collective_id=0, has_side_effects=True, vmem_limit_bytes=VMEM_BYTES
        ),
    )(tokens, cotangent, lengths, *weights, *gains)
    out_shape = (
        jax.ShapeDtypeStruct((2, T, D), bf),
        jax.ShapeDtypeStruct((2, T, D), f32),
        jax.ShapeDtypeStruct((layers, R), f32),
        jax.ShapeDtypeStruct((layers, R), f32),
        *[jax.ShapeDtypeStruct(a.shape, f32) for a in grads],
    )
    vmem_spec = pl.BlockSpec(memory_space=pltpu.VMEM)
    mixed, grad_tokens, *grads = pl.pallas_call(
        functools.partial(lay_out, stride),
        out_shape=out_shape,
        in_specs=[any_spec] * 7 + [vmem_spec],
        out_specs=(any_spec, any_spec, vmem_spec, vmem_spec) + (any_spec,) * 5,
        scratch_shapes=[
            v((2, T, D), f32),
            pltpu.SemaphoreType.DMA((2, 7, 2)),
            *[v(a.shape, a.dtype) for a in (grad_tokens, mixed, *grads[3:], *grads[:3])],
        ],
        compiler_params=pltpu.CompilerParams(vmem_limit_bytes=VMEM_BYTES),
    )(mixed, grad_tokens, *grads, gn)
    if stride > 1:

        def empty(a):
            return lax.psum_scatter(
                a, "seq", scatter_dimension=max(a.ndim - 2, 1), tiled=True, axis_index_groups=blocks
            )

        grads = [empty(a) for a in grads]
    grads[2] = grads[2].transpose(0, 2, 1, 3)
    return (mixed, grad_tokens, *grads)


VMEM_BYTES = 62 << 20


def solution(mesh):
    in_specs = (
        P(None, "seq", None),
        P(),
        P(None, "seq"),
        P(None, "seq"),
        P(None, "seq", None, "mp"),
        P(None, "seq", "mp"),
        P(None, "seq", "mp"),
        P(None, "seq", "mp"),
        P(None, "seq", "mp"),
        P(None, "seq", None),
    )
    out_specs = (
        P(None, "seq", None),
        P(None, "seq", None),
        P(None, "seq"),
        P(None, "seq"),
        P(None, "seq", None, "mp"),
        P(None, "seq", "mp"),
        P(None, "seq", "mp"),
        P(None, "seq", "mp"),
        P(None, "seq", "mp"),
    )
    return jax.shard_map(shards, mesh=mesh, in_specs=in_specs, out_specs=out_specs, check_vma=False)
```

```python
import functools

import jax
import jax.numpy as jnp
from jax import lax
from jax.experimental import pallas as pl
from jax.experimental.pallas import tpu as pltpu
from jax.sharding import PartitionSpec as P

F32 = jnp.float32
BF = jnp.bfloat16
MESH = pl.DeviceIdType.MESH
GROUPS = 8
HEAD = 64
EPS = 1e-05
TILE = 256


def nn(a, b):
    return lax.dot_general(a, b, (((1,), (0,)), ((), ())), preferred_element_type=F32)


def nt(a, b):
    return lax.dot_general(a, b, (((1,), (1,)), ((), ())), preferred_element_type=F32)


def tn(a, b):
    return lax.dot_general(a, b, (((0,), (0,)), ((), ())), preferred_element_type=F32)


def near_size(n_seq):
    return 1 << ((n_seq.bit_length() - 1) // 2)


def norm_parts(x):
    center = x - jnp.mean(x, axis=-1, keepdims=True)
    spread = jnp.mean(center * center, axis=-1, keepdims=True)
    rstd = lax.rsqrt(spread + EPS)
    return center * rstd, rstd


def gate_and_slope(u):
    u2 = u * u
    t = jnp.tanh(u * (0.7978845608 + (0.7978845608 * 0.044715) * u2))
    half = 0.5 + 0.5 * t
    gate = u * half
    slope = half + gate * (1.0 - half) * (1.5957691216 + (1.5957691216 * 0.134145) * u2)
    return gate, slope


MIXER, UPPER, LOWER, Q, KV, C, OUT, UP, DOWN, MIXED, TOKENS, GAINS = range(12)
START, OWN, ON1, ON2, ON3, ACROSS0, ACROSS1, ACROSS2, ACROSS3, END = range(10)
GRAD1, GRAD0, START1, START0, ADD1, ADD0, TURN, HOP = range(10, 18)


def fwd(layer, k):
    return 100 + 20 * layer + k


def bwd(layer, k):
    return 200 + 20 * layer + k


ENTRY, FIRST, TAIL = 0, 1, 2
SEND_RING = 48

X_FIRST = {(Q, 1), (KV, 0), (OUT, 0), (OUT, 1), (DOWN, 0), (DOWN, 1)}
Z_SECOND = set()
GATHER_Z_SECOND = set()
PLAN = {
    ENTRY: (
        (MIXER, 1, OWN),
        (MIXER, 0, START),
        (LOWER, 0, OWN),
        (MIXER, 0, OWN),
        (UPPER, 0, START),
        (UPPER, 1, OWN),
        (MIXER, 0, ON1),
        (MIXER, 0, ON2),
        (MIXER, 0, ON3),
        (UPPER, 0, OWN),
        (LOWER, 0, START),
        (MIXER, 0, ACROSS0),
        (MIXER, 0, ACROSS1),
        (MIXER, 0, ACROSS2),
        (MIXER, 0, ACROSS3),
    ),
    FIRST: (
        (UPPER, 0, ON1),
        (UPPER, 0, ON2),
        (UPPER, 0, ON3),
        (MIXER, 0, END),
    ),
    fwd(0, 1): (
        (MIXER, 1, START),
    ),
    fwd(0, 3): (
        (LOWER, 0, ON1),
        (LOWER, 0, ON2),
        (LOWER, 0, ON3),
    ),
    fwd(0, 4): (
        (UPPER, 0, ACROSS0),
        (UPPER, 0, ACROSS1),
        (UPPER, 0, ACROSS2),
        (UPPER, 0, ACROSS3),
    ),
    fwd(0, 5): (
        (LOWER, 0, ACROSS0),
        (LOWER, 0, ACROSS1),
        (LOWER, 0, ACROSS2),
        (LOWER, 0, ACROSS3),
    ),
    fwd(0, 6): (
        (UPPER, 0, END),
        (UPPER, 1, START),
        (MIXER, 1, ON1),
        (MIXER, 1, ON2),
        (MIXER, 1, ON3),
    ),
    fwd(0, 7): (
        (LOWER, 1, OWN),
        (LOWER, 0, END),
    ),
    fwd(0, 8): (
        (MIXER, 1, ACROSS0),
        (MIXER, 1, ACROSS1),
        (MIXER, 1, ACROSS2),
        (MIXER, 1, ACROSS3),
    ),
    fwd(0, 9): (
        (LOWER, 1, START),
        (UPPER, 1, ON1),
        (UPPER, 1, ON2),
        (UPPER, 1, ON3),
    ),
    fwd(0, 10): (
        (MIXER, 1, END),
    ),
    fwd(1, 3): (
        (LOWER, 1, ON1),
        (LOWER, 1, ON2),
        (LOWER, 1, ON3),
    ),
    fwd(1, 4): (
        (UPPER, 1, ACROSS0),
        (UPPER, 1, ACROSS1),
        (UPPER, 1, ACROSS2),
        (UPPER, 1, ACROSS3),
    ),
    fwd(1, 6): (
        (LOWER, 1, ACROSS0),
        (LOWER, 1, ACROSS1),
        (LOWER, 1, ACROSS2),
        (LOWER, 1, ACROSS3),
    ),
    fwd(1, 7): (
        (LOWER, 1, END),
        (UPPER, 1, END),
    ),
    bwd(1, 0): (
        (MIXED, 0, START),
        (DOWN, 1, GRAD1),
        (DOWN, 1, START1),
    ),
    bwd(1, 1): (
        (UP, 1, GRAD1),
        (UP, 1, START1),
        (DOWN, 1, GRAD0),
    ),
    bwd(1, 3): (
        (UP, 1, START0),
        (DOWN, 1, START0),
    ),
    bwd(1, 4): (
        (OUT, 1, GRAD1),
    ),
    bwd(1, 5): (
        (UP, 1, GRAD0),
    ),
    bwd(1, 6): (
        (UP, 1, ADD1),
        (OUT, 1, START1),
        (OUT, 1, START0),
    ),
    bwd(1, 7): (
        (DOWN, 1, ADD1),
        (DOWN, 1, ADD0),
    ),
    bwd(1, 8): (
        (C, 1, START1),
        (C, 1, START0),
    ),
    bwd(1, 9): (
        (MIXED, 0, HOP),
        (Q, 1, START1),
        (UP, 1, ADD0),
    ),
    bwd(1, 10): (
        (UP, 1, TURN),
        (Q, 1, START0),
        (KV, 1, START1),
    ),
    bwd(0, 0): (
        (DOWN, 0, GRAD1),
    ),
    bwd(0, 1): (
        (DOWN, 0, START1),
        (DOWN, 0, GRAD0),
        (UP, 0, GRAD1),
        (KV, 1, START0),
    ),
    bwd(0, 2): (
        (DOWN, 1, TURN),
        (Q, 1, ADD1),
        (Q, 1, ADD0),
        (OUT, 1, ADD1),
        (UP, 0, START1),
    ),
    bwd(0, 3): (
        (UP, 0, GRAD0),
        (C, 1, ADD1),
        (C, 1, ADD0),
        (KV, 1, ADD1),
    ),
    bwd(0, 4): (
        (UP, 0, START0),
        (OUT, 1, ADD0),
        (KV, 1, ADD0),
        (C, 1, TURN),
    ),
    bwd(0, 5): (
        (DOWN, 0, START0),
        (OUT, 0, GRAD1),
    ),
    bwd(0, 6): (
        (KV, 1, TURN),
        (UP, 0, ADD1),
    ),
    bwd(0, 7): (
        (OUT, 0, START0),
        (OUT, 1, TURN),
    ),
    bwd(0, 8): (
        (UP, 1, END),
        (Q, 1, TURN),
        (DOWN, 0, ADD1),
    ),
    bwd(0, 9): (
        (UP, 0, ADD0),
        (MIXED, 0, END),
        (OUT, 0, START1),
        (UP, 0, TURN),
        (OUT, 1, END),
    ),
    bwd(0, 10): (
        (C, 1, END),
        (KV, 0, START1),
        (OUT, 0, ADD0),
        (C, 0, START1),
        (C, 0, START0),
        (Q, 0, START1),
        (Q, 0, START0),
        (DOWN, 0, ADD0),
    ),
    bwd(0, 11): (
        (DOWN, 0, TURN),
        (OUT, 0, ADD1),
        (KV, 0, START0),
        (Q, 1, END),
        (KV, 0, ADD1),
        (KV, 1, END),
        (DOWN, 1, END),
    ),
    TAIL: (
        (C, 0, ADD1),
        (GAINS, 0, START),
        (OUT, 0, TURN),
        (C, 0, ADD0),
        (Q, 0, ADD1),
        (Q, 0, ADD0),
        (UP, 0, END),
        (C, 0, TURN),
        (TOKENS, 0, START),
        (KV, 0, ADD0),
        (KV, 0, TURN),
        (Q, 0, TURN),
        (GAINS, 0, HOP),
        (TOKENS, 0, HOP),
        (Q, 0, END),
        (C, 0, END),
        (OUT, 0, END),
        (KV, 0, END),
        (TOKENS, 0, END),
        (GAINS, 0, END),
        (DOWN, 0, END),
    ),
}


def kernel(
    n_seq,
    layers,
    tok_hbm,
    cot_hbm,
    len_ref,
    qkv_hbm,
    ctrl_hbm,
    up_hbm,
    down_hbm,
    out_hbm,
    norm_attn_hbm,
    norm_ffn_hbm,
    mixed_hbm,
    gt_hbm,
    gqkv_hbm,
    gctrl_hbm,
    gout_hbm,
    gup_hbm,
    gdown_hbm,
    gn_hbm,
    H,
    MID,
    AB,
    FB,
    QKV,
    WB,
    S2,
    ZS,
    PS,
    XS,
    AST,
    MST,
    OB,
    GU,
    GG,
    KP,
    VP,
    LOC,
    TOKB,
    GBF,
    DOB,
    DU,
    DMID,
    YST,
    DNB,
    DZ,
    DWF,
    WA,
    WF,
    GAIN,
    GROW,
    GFULL,
    ARS,
    ARR,
    SCS,
    SCR1,
    SCR2,
    SCP,
    RQ,
    RKV,
    RC,
    ROUT,
    RUP,
    RDN,
    LQ,
    LKV,
    LC,
    LOUT,
    LUP,
    LDN,
    OQKV,
    OCTRL,
    OOUT,
    OUP,
    ODN,
    GN,
    GNY,
    GNR,
    GNO,
    OUTB,
    send_sems,
    recv_sems,
    local_sems,
):
    T, D = TOKB.shape[1], TOKB.shape[2]
    tiles = T // TILE
    R = D // GROUPS
    stride = n_seq // GROUPS
    s = lax.axis_index("seq")
    m = lax.axis_index("mp")
    y, core = m // 2, m % 2
    g, lo = s // stride, s % stride
    x, z = g % 2, g // 2
    z1, z0 = z // 2, z % 2
    last = layers - 1

    def flip_z(d):
        d1, d0 = d // 2, d % 2
        return 2 * (1 - z1 if d1 else z1) + (1 - z0 if d0 else z0)

    def seq_of(gx, gz):
        return (gz * 2 + gx) * stride + lo

    core_peer = (s, 2 * y + (1 - core))
    y_peer = (s, 2 * (1 - y) + core)
    x_peer = (seq_of(1 - x, z), m)
    z_peer = {d: (seq_of(x, flip_z(d)), m) for d in (1, 2, 3)}
    near = near_size(n_seq)
    blocks = n_seq // near
    low, high = s % near, s // near

    used = [0, 0, 0]
    leaving = {}

    def arrival():
        used[0] += 1
        return recv_sems.at[used[0] - 1]

    def remote(src, dst, peer, leave, arrive):
        return pltpu.make_async_remote_copy(
            src_ref=src,
            dst_ref=dst,
            send_sem=leave,
            recv_sem=arrive,
            device_id=peer,
            device_id_type=MESH,
        )

    def send(src, dst, peer, arrive=None):
        k = used[2] % SEND_RING
        used[2] += 1
        if k in leaving:
            leaving[k].wait_send()
        c = remote(src, dst, peer, send_sems.at[k], arrival() if arrive is None else arrive)
        c.start()
        leaving[k] = c
        return c

    def leave_done(c):
        for k, other in list(leaving.items()):
            if other is c:
                c.wait_send()
                del leaving[k]

    def arrived(region, arrive):
        remote(region, region, core_peer, send_sems.at[0], arrive).wait_recv()

    def local(src, dst):
        k = used[1]
        used[1] += 1
        c = pltpu.make_async_copy(src, dst, local_sems.at[k])
        c.start()
        return c

    barrier = pltpu.get_barrier_semaphore()

    def hello(peer):
        pl.semaphore_signal(barrier, inc=1, device_id=peer, device_id_type=MESH)

    hello(core_peer)
    hello(y_peer)
    count = 2
    for d in range(1, near):
        hello((high * near + lax.rem(low + d, near), m))
        count += 1
    for d in range(1, blocks):
        other = lax.rem(high + d, blocks) * near
        hello((other + low, m))
        count += 1
        if stride == 1:
            hello((other + 1 - low, m))
            count += 1

    rows_in = [local(norm_attn_hbm, GROW.at[0]), local(norm_ffn_hbm, GROW.at[1])]
    own = []
    for l in range(layers):
        for k in range(4):
            src = qkv_hbm.at[l, k] if k < 3 else ctrl_hbm.at[l]
            own.append(local(src, WA.at[l, y, z, x, slice(None), pl.ds(k * 128, 128)]))
        lanes = 0
        for src in (up_hbm, down_hbm, out_hbm):
            at = pl.ds(lanes, src.shape[-1])
            own.append(local(src.at[l], WF.at[l, y, z, x, slice(None), at]))
            lanes += src.shape[-1]
    tok_copy = local(tok_hbm.at[y], TOKB.at[0])
    cot_copy = local(cot_hbm.at[y], TOKB.at[1])
    gain_sub = lax.broadcasted_iota(jnp.int32, (8, R), 0)
    own_gains = jnp.zeros((8, R), F32)
    for c in rows_in:
        c.wait()
    for l in range(layers):
        for k in range(2):
            row = GROW[k].astype(F32)[l : l + 1]
            own_gains = jnp.where(gain_sub == 2 * l + k, row, own_gains)
    GAIN[0, :, pl.ds(0, R)] = jnp.where(x == 0, own_gains, 0.0)
    GAIN[0, :, pl.ds(R, R)] = jnp.where(x == 0, 0.0, own_gains)

    pl.semaphore_wait(barrier, count)

    every = slice(None)

    class Gather:
        def __init__(self, buf, l, low_end, cut, high_end, z_second):
            self.buf, self.l, self.c = buf, l, {}
            self.all = pl.ds(low_end, high_end - low_end)
            self.first, self.second = pl.ds(low_end, cut - low_end), pl.ds(cut, high_end - cut)
            self.z_second = z_second
            self.last = None

        def push(self, key, region, peer, lanes=None):
            src = self.buf.at[(self.l,) + region + (slice(None), lanes or self.all)]
            arrive = None
            if key[0] in (5, 6) and not self.z_second:
                self.last = self.last or {5: arrival(), 6: arrival()}
                arrive = self.last[key[0]]
            self.c[key] = send(src, src, peer, arrive)

        def take(self, *keys):
            for key in keys:
                self.c[key].wait_recv()

        def start(self):
            for d in (1, 2, 3):
                self.push((0, d), (y, z, x), z_peer[d])

        def own(self):
            self.push((1, 0), (y, z, x), x_peer)
            self.push((2, 0), (y, z, x), y_peer)

        def on(self, d):
            if not self.z_second:
                self.take((0, d))
                self.push((1, d), (y, flip_z(d), x), x_peer)
                self.push((2, d), (y, flip_z(d), x), y_peer)
            elif d == 1:
                self.take((1, 0))
                for k in (1, 2, 3):
                    self.push((3, k), (y, z, 1 - x), z_peer[k], self.first)
                self.push((5, 0), (y, z, 1 - x), y_peer, self.first)
            elif d == 2:
                self.take((2, 0))
                for k in (1, 2, 3):
                    self.push((4, k), (1 - y, z, x), z_peer[k], self.second)
                self.push((6, 0), (1 - y, z, x), x_peer, self.second)

        def across(self, d):
            zz = flip_z(d)
            if not self.z_second:
                self.take((1, d))
                self.push((5, d), (y, zz, 1 - x), y_peer, self.first)
                self.take((2, d))
                self.push((6, d), (1 - y, zz, x), x_peer, self.second)
            elif d:
                self.take((0, d), (3, d))
                self.push((5, d), (y, zz, slice(None)), y_peer, self.first)
                self.take((4, d))
                self.push((6, d), (slice(None), zz, x), x_peer, self.second)

        def end(self):
            if self.z_second:
                for d in range(4):
                    self.take((5, d), (6, d))
                return
            far = self.buf.at[self.l, 1 - y, every, 1 - x]
            arrived(far.at[:, :, self.first], self.last[5])
            arrived(far.at[:, :, self.second], self.last[6])

        def parts(self):
            part = {START: self.start, OWN: self.own, END: self.end}
            for d in (1, 2, 3):
                part[ON1 + d - 1] = functools.partial(self.on, d)
            for d in range(4):
                part[ACROSS0 + d] = functools.partial(self.across, d)
            return part

    gains_here = arrival()
    for d in (0, 1, 2, 3):
        for o in (0, 1):
            if (d, o) == (0, 0):
                continue
            peer = (seq_of(1 - x if o else x, flip_z(d)), m)
            send(GAIN.at[0], GAIN.at[d * 2 + o], peer, gains_here)
    for c in own:
        c.wait()
    jobs = {}
    for l in range(layers):
        for name, buf, bounds in (
            (MIXER, WA, (0, 256, 512)),
            (UPPER, WF, (0, 256, 512)),
            (LOWER, WF, (512, 896, 1152)),
        ):
            jobs[name, l] = Gather(buf, l, *bounds, (name, l) in GATHER_Z_SECOND).parts()

    def at(place):
        for name, l, part in PLAN.get(place, ()):
            jobs[name, l][part]()

    at(ENTRY)

    lane = lax.broadcasted_iota(jnp.int32, (TILE, 128), 1)
    first = lane < HEAD
    head_rows = [
        (lax.broadcasted_iota(jnp.int32, (1, 128), 1) < HEAD).astype(F32).astype(BF),
        (lax.broadcasted_iota(jnp.int32, (1, 128), 1) >= HEAD).astype(F32).astype(BF),
    ]
    rr = lax.broadcasted_iota(jnp.int32, (TILE, TILE), 0)
    cc = lax.broadcasted_iota(jnp.int32, (TILE, TILE), 1)
    lower = rr >= cc
    lower_ones = lower.astype(F32).astype(BF)
    upper_ones = (rr <= cc).astype(F32).astype(BF)
    diag = (lax.broadcasted_iota(jnp.int32, (128, 128), 0) < HEAD) == (
        lax.broadcasted_iota(jnp.int32, (128, 128), 1) < HEAD
    )

    def per_head(value):
        a = jnp.sum(jnp.where(first, value, 0.0), axis=-1, keepdims=True)
        b = jnp.sum(jnp.where(first, 0.0, value), axis=-1, keepdims=True)
        return jnp.where(first, a, b)

    def per_head_max(value):
        a = jnp.max(jnp.where(first, value, -jnp.inf), axis=-1, keepdims=True)
        b = jnp.max(jnp.where(first, -jnp.inf, value), axis=-1, keepdims=True)
        return jnp.where(first, a, b)

    def heads(value):
        return value * head_rows[0], value * head_rows[1]

    def tile_rows(i):
        return pl.ds(i * TILE, TILE)

    def weight(buf, l, p, start, width):
        return buf[l, p, :, :, :, pl.ds(start, width)].reshape(D, width)

    def mixer_weight(l, p):
        return weight(WA, l, p, 0, 512)

    def up_weight(l, p):
        return weight(WF, l, p, 0, 512)

    def down_weight(l, p):
        return weight(WF, l, p, 512, 512)

    def out_weight(l, p):
        return weight(WF, l, p, 1024, 128)

    shared = [0]
    share_sems = [[send_sems.at[SEND_RING + k] for k in range(ARS.shape[0])]]
    share_sems.append([arrival() for _ in range(ARR.shape[0])])
    share_prev = {}

    def share_start(value):
        k = shared[0]
        shared[0] += 1
        slot = k % ARS.shape[0]
        if slot in share_prev:
            share_prev[slot].wait_send()
        ARS[slot] = value.astype(BF)
        k = k % ARR.shape[0]
        c = remote(ARS.at[slot], ARR.at[k], core_peer, share_sems[0][slot], share_sems[1][k])
        c.start()
        share_prev[slot] = c
        return c, slot, k

    def share_end(handle):
        c, slot, k = handle
        c.wait_recv()
        return ARS[slot].astype(F32) + ARR[k].astype(F32)

    class Scan:
        def __init__(self, call, forward):
            self.call, self.forward = call, forward

        def pack_normalizer(self, which, part):
            sub = lax.broadcasted_iota(jnp.int32, (16, 128), 0)
            rest = jnp.zeros((16, 128), F32)
            for k in range(3):
                piece = part.astype(BF).astype(F32)
                rest = jnp.where(sub == k, piece, rest)
                part = part - piece
            SCS[which, pl.ds(128, 16)] = rest.astype(BF)

        def start(self, k_state, v_state, z_row):
            which = self.call
            SCS[which, pl.ds(0, 128)] = (k_state + pltpu.roll(v_state, HEAD, 1)).astype(BF)
            self.pack_normalizer(which, z_row)
            self.near = []
            for d in range(1, near):
                peer = (high * near + lax.rem(low + d, near), m)
                self.near.append(send(SCS.at[which], SCR1.at[self.call, d - 1], peer))

        def step(self):
            for c in self.near:
                c.wait_recv()
                leave_done(c)
            which = self.call
            both = SCS[which].astype(F32)
            for d in range(1, near):
                both = both + SCR1[self.call, d - 1].astype(F32)
            SCS[which, pl.ds(0, 128)] = both[:128].astype(BF)
            self.pack_normalizer(which, jnp.sum(both[128:131], axis=0, keepdims=True))
            self.links = []
            for d in range(1, blocks):
                to = high + d if self.forward else high - d
                frm = high - d if self.forward else high + d
                inside = to < blocks if self.forward else to >= 0
                comes = frm >= 0 if self.forward else frm < blocks
                target = jnp.where(inside, to, high)
                leave = send_sems.at[SEND_RING + ARS.shape[0] + (self.call % 2) * (blocks - 1) + d - 1]
                target = (target * near + low, m)
                c = remote(SCS.at[which], SCR2.at[self.call, d - 1], target, leave, arrival())

                @pl.when(inside)
                def _(c=c):
                    c.start()

                self.links.append((c, inside, comes))

        def end(self):
            acc = SCP.at[self.call % 2]
            before = jnp.zeros(acc.shape, F32)
            for d in range(1, near):
                mine = low >= d if self.forward else low < d
                before = before + jnp.where(mine, SCR1[self.call, d - 1].astype(F32), 0.0)
            acc[...] = before
            for d, (c, inside, comes) in enumerate(self.links):

                @pl.when(comes)
                def _(c=c, d=d):
                    c.wait_recv()
                    acc[...] += SCR2[self.call, d].astype(F32)

            for c, inside, comes in self.links:

                @pl.when(inside)
                def _(c=c):
                    c.wait_send()

            block = acc[pl.ds(0, 128)]
            k_state = jnp.where(diag, block, 0.0)
            v_state = pltpu.roll(jnp.where(diag, 0.0, block), HEAD, 1)
            return k_state, v_state, jnp.sum(acc[pl.ds(128, 3)], axis=0, keepdims=True)

    def add_to(buf, at, more):
        buf[at] = (buf[at].astype(F32) + more.astype(F32)).astype(BF)

    class Scatter:
        def __init__(self, buf, land, l, x_first, z_second):
            self.buf, self.land, self.l = buf, land, l
            self.x_first, self.z_second = x_first, z_second
            self.first_peer = x_peer if x_first else y_peer
            self.next_peer = y_peer if x_first else x_peer
            self.c = {}

        def block(self, first_other, next_other, zz=every):
            ox, oy = (first_other, next_other) if self.x_first else (next_other, first_other)
            return (self.l, 1 - y if oy else y, zz, 1 - x if ox else x)

        def start(self, o):
            src = self.buf.at[self.block(1, o)]
            self.c[0, o] = send(src, self.land.at[self.l, pl.ds(4 * o, 4)], self.first_peer)

        def add(self, o):
            self.c[0, o].wait_recv()
            add_to(self.buf, self.block(0, o), self.land[self.l, pl.ds(4 * o, 4)])
            if self.z_second:
                self.c[1, o] = arrival()
                for d in (1, 2, 3):
                    src = self.buf.at[self.block(0, o, flip_z(d))]
                    send(src, self.land.at[self.l, 7 + 3 * o + d], z_peer[d], self.c[1, o])
            elif o:
                src = self.buf.at[self.block(0, o)]
                self.c[1] = send(src, self.land.at[self.l, pl.ds(8, 4)], self.next_peer)

        def turn(self):
            if self.z_second:
                for o in (1, 0):
                    total = self.buf[self.block(0, o, z)].astype(F32)
                    arrived(self.land.at[self.l, pl.ds(8 + 3 * o, 3)], self.c[1, o])
                    for d in (1, 2, 3):
                        total = total + self.land[self.l, 7 + 3 * o + d].astype(F32)
                    self.buf[self.block(0, o, z)] = total.astype(BF)
                    if o:
                        src = self.buf.at[self.block(0, o, z)]
                        self.c[2] = send(src, self.land.at[self.l, 14], self.next_peer)
                return
            self.c[1].wait_recv()
            self.c[2] = arrival()
            for d in (1, 2, 3, 0):
                at_ = self.block(0, 0, flip_z(d))
                add_to(self.buf, at_, self.land[self.l, 8 + flip_z(d)])
                if d:
                    send(self.buf.at[at_], self.land.at[self.l, 11 + d], z_peer[d], self.c[2])

        def end(self):
            total = self.buf[self.block(0, 0, z)].astype(F32)
            if self.z_second:
                self.c[2].wait_recv()
                return total + self.land[self.l, 14].astype(F32)
            arrived(self.land.at[self.l, pl.ds(12, 3)], self.c[2])
            for d in (1, 2, 3):
                total = total + self.land[self.l, 11 + d].astype(F32)
            return total

    finals = []

    def finish(l, name):
        total = scatters[name, l].end()
        if name == UP:
            OUP[l] = total
            finals.append(local(OUP.at[l], gup_hbm.at[l]))
        elif name == DOWN:
            ODN[l] = total
            finals.append(local(ODN.at[l], gdown_hbm.at[l]))
        elif name == OUT:
            OOUT[l] = total
            finals.append(local(OOUT.at[l], gout_hbm.at[l]))
        elif name == Q:
            OQKV[l, 0] = total
            finals.append(local(OQKV.at[l, 0], gqkv_hbm.at[l, 0]))
        elif name == KV:
            OQKV[l, 1] = total[:, :128]
            OQKV[l, 2] = total[:, 128:]
            finals.append(local(OQKV.at[l, pl.ds(1, 2)], gqkv_hbm.at[l, pl.ds(1, 2)]))
        else:
            OCTRL[l] = total
            finals.append(local(OCTRL.at[l], gctrl_hbm.at[l]))

    def split_rows(value):
        return value.astype(BF).reshape(4, 2, R, value.shape[-1])

    def grad_up(l, o):
        yy = 1 - y if o else y
        RUP[l, yy] = split_rows(tn(FB[l], DU[yy]))

    def grad_down(l, o):
        yy = 1 - y if o else y
        RDN[l, yy] = split_rows(tn(GBF[...], GG[l, yy]))

    def grad_out(l):
        grads = tn(GBF[...], OB[l])
        for p in range(2):
            ROUT[l, p] = split_rows(grads[:, p * 128 : (p + 1) * 128])

    scatters = {}
    for l in range(layers):
        for name, buf, land in (
            (Q, RQ, LQ),
            (KV, RKV, LKV),
            (C, RC, LC),
            (OUT, ROUT, LOUT),
            (UP, RUP, LUP),
            (DOWN, RDN, LDN),
        ):
            f = Scatter(buf, land, l, (name, l) in X_FIRST, (name, l) in Z_SECOND)
            scatters[name, l] = f
            jobs[name, l] = {
                START1: functools.partial(f.start, 1),
                START0: functools.partial(f.start, 0),
                ADD1: functools.partial(f.add, 1),
                ADD0: functools.partial(f.add, 0),
                TURN: f.turn,
                END: functools.partial(finish, l, name),
            }
        for name, f in ((UP, grad_up), (DOWN, grad_down)):
            jobs[name, l][GRAD1] = functools.partial(f, l, 1)
            jobs[name, l][GRAD0] = functools.partial(f, l, 0)
        jobs[OUT, l][GRAD1] = functools.partial(grad_out, l)

    tok_copy.wait()
    cot_copy.wait()
    arrived(GAIN.at[pl.ds(1, 7)], gains_here)
    for gz in range(GROUPS // 2):
        total = jnp.zeros((8, 128), F32)
        for d in range(4):
            here = flip_z(d) == gz
            total = total + jnp.where(here, GAIN[2 * d] + GAIN[2 * d + 1], 0.0)
        GFULL[:, pl.ds(gz * 128, 128)] = total

    def gain_row(l, which):
        return GFULL[pl.ds(2 * l + which, 1), :]

    def stream(l, rows):
        return TOKB[0, rows].astype(F32) if l == 0 else H[l - 1, rows]

    def attn_norm(l, i):
        rows = tile_rows(i)
        y_hat, _ = norm_parts(stream(l, rows))
        AB[l, rows] = (y_hat * gain_row(l, 0)).astype(BF)

    for i in range(tiles):
        attn_norm(0, i)

    at(FIRST)

    for l in range(layers):
        more_layers = l + 1 < layers
        at(fwd(l, 0))
        scans = [Scan(2 * l + p, True) for p in range(2)]

        def project_pair(p, l=l):
            out = nn(AB[l], mixer_weight(l, p))
            kv = out[:, 128:384].astype(BF)
            th = jnp.tanh(out[:, 384:] * (1.0 / 16.0))
            w = jnp.exp(16.0 * th).astype(BF)
            sums = [
                (
                    tn(w[j * TILE : (j + 1) * TILE], kv[j * TILE : (j + 1) * TILE]),
                    jnp.sum(w[j * TILE : (j + 1) * TILE].astype(F32), axis=0, keepdims=True),
                )
                for j in range(tiles)
            ]
            ks, vs, zs = 0.0, 0.0, 0.0
            for j, (both, z_j) in enumerate(sums):
                k_j = jnp.where(diag, both[:, :128], 0.0)
                v_j = jnp.where(diag, both[:, 128:], 0.0)
                if j < tiles - 1:
                    LOC[p, j, 0] = k_j
                    LOC[p, j, 1] = v_j
                ks, vs, zs = ks + k_j, vs + v_j, zs + z_j
            QKV[l, p, :, pl.ds(0, 128)] = out[:, :128].astype(BF)
            QKV[l, p, :, pl.ds(128, 256)] = kv
            WB[l, p] = w
            S2[l, p] = (1.0 - th * th).astype(BF)
            return ks, vs, zs

        def inside_block(p, l=l):
            units = range(tiles)
            w = [WB[l, p, tile_rows(j)] for j in units]
            q = [QKV[l, p, tile_rows(j), pl.ds(0, 128)] for j in units]
            k = [QKV[l, p, tile_rows(j), pl.ds(128, 128)] for j in units]
            qs = [heads(q[j]) for j in units]
            a = [[jnp.where(lower, nt(qs[j][h], k[j]), 0.0).astype(BF) for h in (0, 1)] for j in units]
            sums = [nn(lower_ones, w[j]) for j in units]
            ws = [heads(w[j]) for j in units]
            num = [nn(a[j][0], ws[j][0]) + nn(a[j][1], ws[j][1]) for j in units]
            for j in units:
                for h in (0, 1):
                    AST[l, p, j, h] = a[j][h]
                ZS[l, p, tile_rows(j)] = sums[j]
                XS[l, p, tile_rows(j)] = num[j]

        def with_earlier(states, l=l):
            units = [(p, j) for p in range(2) for j in range(tiles)]
            ks, vs, z_before = {}, {}, {}
            for p, j in units:
                if j == 0:
                    k_pre, v_pre, z_pre = states[p]
                else:
                    k_pre = k_pre + LOC[p, j - 1, 0]
                    v_pre = v_pre + LOC[p, j - 1, 1]
                    z_pre = z_pre + jnp.sum(
                        WB[l, p, tile_rows(j - 1)].astype(F32), axis=0, keepdims=True
                    )
                ks[p, j], vs[p, j], z_before[p, j] = k_pre.astype(BF), v_pre.astype(BF), z_pre
            w = {(p, j): WB[l, p, tile_rows(j)] for p, j in units}
            q = {(p, j): QKV[l, p, tile_rows(j), pl.ds(0, 128)] for p, j in units}
            v = {(p, j): QKV[l, p, tile_rows(j), pl.ds(256, 128)] for p, j in units}
            inv = {(p, j): 1.0 / (ZS[l, p, tile_rows(j)] + z_before[p, j]) for p, j in units}
            num = {(p, j): XS[l, p, tile_rows(j)] for p, j in units}
            xs = {u: (num[u] + nt(q[u], ks[u])) * inv[u] * 0.125 for u in units}
            e = {u: jnp.exp(xs[u] - per_head_max(xs[u])) for u in units}
            prob = {u: e[u] / per_head(e[u]) for u in units}
            scaled = {u: (prob[u] * inv[u]).astype(BF) for u in units}
            rs = {u: heads(scaled[u]) for u in units}
            mm = {
                u: [jnp.where(lower, nt(rs[u][h], w[u]), 0.0).astype(BF) for h in (0, 1)]
                for u in units
            }
            vh = {u: heads(v[u]) for u in units}
            out = {
                u: nn(scaled[u], vs[u]) + nn(mm[u][0], vh[u][0]) + nn(mm[u][1], vh[u][1])
                for u in units
            }
            for p, j in units:
                rows = tile_rows(j)
                KP[l, p, j] = ks[p, j]
                VP[l, p, j] = vs[p, j]
                ZS[l, p, rows] = inv[p, j]
                XS[l, p, rows] = xs[p, j]
                PS[l, p, rows] = prob[p, j]
                for h in (0, 1):
                    MST[l, p, j, h] = mm[p, j][h]
                OB[l, rows, pl.ds(p * 128, 128)] = out[p, j].astype(BF)

        for p in range(2):
            scans[p].start(*project_pair(p))
            at(fwd(l, 1 + p))
        for p in range(2):
            inside_block(p)
            at(fwd(l, 3 + 2 * p))
            scans[p].step()
            at(fwd(l, 4 + 2 * p))
        with_earlier([scans[0].end(), scans[1].end()])
        at(fwd(l, 7))

        handles = []
        for i in range(tiles):
            rows = tile_rows(i)
            part = nt(OB[l, rows, pl.ds(0, 128)], out_weight(l, 0))
            part = part + nt(OB[l, rows, pl.ds(128, 128)], out_weight(l, 1))
            handles.append(share_start(part))
        at(fwd(l, 8))
        more = []
        for i in range(tiles):
            rows = tile_rows(i)
            mid = stream(l, rows) + share_end(handles[i])
            y_hat, _ = norm_parts(mid)
            f = (y_hat * gain_row(l, 1)).astype(BF)
            hidden = [nn(f, up_weight(l, p)) for p in range(2)]
            gates = [gate_and_slope(u) for u in hidden]
            low_gates = [gate.astype(BF) for gate, _ in gates]
            part = nt(low_gates[0], down_weight(l, 0)) + nt(low_gates[1], down_weight(l, 1))
            more.append(share_start(part))
            MID[l, rows] = mid
            FB[l, rows] = f
            for p in range(2):
                GG[l, p, rows] = low_gates[p]
                GU[l, p, rows] = gates[p][1].astype(BF)
            at(fwd(l, 9 + i))
        if more_layers:
            for i in range(tiles):
                rows = tile_rows(i)
                H[l, rows] = MID[l, rows] + share_end(more[i])
                attn_norm(l + 1, i)
            at(fwd(l, 11))

    length = len_ref[y]

    def valid_rows(i):
        row = lax.broadcasted_iota(jnp.int32, (TILE, 1), 0)
        return jnp.where(s * T + i * TILE + row < length, 1.0, 0.0)

    half_rows = pl.ds(pl.multiple_of(core * (T // 2), T // 2), T // 2)

    class Spread:
        def __init__(self, k, out):
            self.k, self.out = k, out

        def start(self):
            src = OUTB.at[self.k, y, half_rows]
            self.c = send(src, src, y_peer)

        def hop(self):
            self.c.wait_recv()
            src = OUTB.at[self.k, 1 - y, half_rows]
            self.c = send(src, src, core_peer)

        def end(self):
            self.c.wait_recv()
            finals.append(local(OUTB.at[self.k], self.out))

    for name, f in ((MIXED, Spread(0, mixed_hbm)), (TOKENS, Spread(1, gt_hbm))):
        jobs[name, 0] = {START: f.start, HOP: f.hop, END: f.end}

    for i in range(tiles):
        rows = tile_rows(i)
        out = MID[last, rows] + share_end(more[i])
        keep = valid_rows(i)
        OUTB[0, y, rows] = (out * keep).astype(BF)
        DMID[rows] = TOKB[1, rows].astype(F32) * keep

    grad_norm = [None] * (2 * layers)

    for l in range(last, -1, -1):
        for i in range(tiles):
            GBF[tile_rows(i)] = DMID[tile_rows(i)].astype(BF)
        at(bwd(l, 0))
        handles = []
        for i in range(tiles):
            rows = tile_rows(i)
            gb = GBF[rows]
            du = [
                (nn(gb, down_weight(l, p)) * GU[l, p, rows].astype(F32)).astype(BF)
                for p in range(2)
            ]
            part = nt(du[0], up_weight(l, 0)) + nt(du[1], up_weight(l, 1))
            handles.append(share_start(part))
            for p in range(2):
                DU[p, rows] = du[p]
        at(bwd(l, 1))
        gsum = jnp.zeros((1, D), F32)
        for i in range(tiles):
            rows = tile_rows(i)
            df = share_end(handles[i])
            y_hat, rstd = norm_parts(MID[l, rows])
            gsum = gsum + jnp.sum(df * y_hat, axis=0, keepdims=True)
            df = df * gain_row(l, 1)
            dm = DMID[rows] + (
                df
                - jnp.mean(df, axis=-1, keepdims=True)
                - y_hat * jnp.mean(df * y_hat, axis=-1, keepdims=True)
            ) * rstd
            DMID[rows] = dm
            GBF[rows] = dm.astype(BF)
            for p in range(2):
                DOB[p, rows] = nn(GBF[rows], out_weight(l, p)).astype(BF)
        grad_norm[2 * l + 1] = gsum
        at(bwd(l, 2))

        scans = [Scan(2 * layers + 2 * (last - l) + k, False) for k in range(2)]
        order = (1 - y, y)

        def to_states(l=l):
            units = [(k, j) for k in range(2) for j in range(tiles - 1, -1, -1)]
            rows = {u: tile_rows(u[1]) for u in units}
            w = {(k, j): WB[l, order[k], rows[k, j]] for k, j in units}
            q = {(k, j): QKV[l, order[k], rows[k, j], pl.ds(0, 128)] for k, j in units}
            v = {(k, j): QKV[l, order[k], rows[k, j], pl.ds(256, 128)] for k, j in units}
            do = {(k, j): DOB[order[k], rows[k, j]] for k, j in units}
            inv = {(k, j): ZS[l, order[k], rows[k, j]] for k, j in units}
            prob = {(k, j): PS[l, order[k], rows[k, j]] for k, j in units}
            xs = {(k, j): XS[l, order[k], rows[k, j]] for k, j in units}
            v_pre = {(k, j): VP[l, order[k], j] for k, j in units}
            ws = {u: heads(w[u]) for u in units}
            dos = {u: heads(do[u]) for u in units}
            pair = {
                u: [jnp.where(lower, nt(dos[u][h], v[u]), 0.0).astype(BF) for h in (0, 1)]
                for u in units
            }
            dr = {
                u: nt(do[u], v_pre[u]) + nn(pair[u][0], ws[u][0]) + nn(pair[u][1], ws[u][1])
                for u in units
            }
            dp = {u: dr[u] * inv[u] for u in units}
            dx = {u: prob[u] * (dp[u] - per_head(dp[u] * prob[u])) for u in units}
            dn = {u: (dx[u] * inv[u] * 0.125).astype(BF) for u in units}
            r = {u: (prob[u] * inv[u]).astype(BF) for u in units}
            dz = {
                u: -(r[u].astype(F32) * dp[u]) - 8.0 * dn[u].astype(F32) * xs[u] for u in units
            }
            dk = {u: jnp.where(diag, tn(dn[u], q[u]), 0.0) for u in units}
            dv = {u: jnp.where(diag, tn(r[u], do[u]), 0.0) for u in units}
            totals = []
            for k in range(2):
                total = [0.0, 0.0, 0.0]
                for j in range(tiles):
                    dzs = jnp.sum(dz[k, j], axis=0, keepdims=True)
                    total = [a + b for a, b in zip(total, (dk[k, j], dv[k, j], dzs))]
                totals.append(total)
            for k, j in units:
                p = order[k]
                for h in (0, 1):
                    YST[p, j, h] = pair[k, j][h]
                DNB[p, rows[k, j]] = dn[k, j]
                DZ[p, rows[k, j]] = dz[k, j]
                if j > 0:
                    LOC[p, j - 1, 0] = dk[k, j]
                    LOC[p, j - 1, 1] = dv[k, j]
            return totals

        def within(p, l=l):
            units = range(tiles)
            rows = [tile_rows(j) for j in units]
            w = [WB[l, p, rows[j]] for j in units]
            q = [QKV[l, p, rows[j], pl.ds(0, 128)] for j in units]
            k = [QKV[l, p, rows[j], pl.ds(128, 128)] for j in units]
            do = [DOB[p, rows[j]] for j in units]
            dn = [DNB[p, rows[j]] for j in units]
            r = [(PS[l, p, rows[j]] * ZS[l, p, rows[j]]).astype(BF) for j in units]
            dz = [DZ[p, rows[j]] for j in units]
            k_pre = [KP[l, p, j] for j in units]
            dz_hi = [dz[j].astype(BF) for j in units]
            dz_lo = [(dz[j] - dz_hi[j].astype(F32)).astype(BF) for j in units]
            dns, rs, dos, qs, ks = ([heads(a[j]) for j in units] for a in (dn, r, do, q, k))
            da = [
                [jnp.where(lower, nt(dns[j][h], w[j]), 0.0).astype(BF) for h in (0, 1)]
                for j in units
            ]
            dq = [
                nn(dn[j], k_pre[j]) + nn(da[j][0], ks[j][0]) + nn(da[j][1], ks[j][1]) for j in units
            ]
            dk = [tn(da[j][0], qs[j][0]) + tn(da[j][1], qs[j][1]) for j in units]
            dv = [
                tn(MST[l, p, j, 0], dos[j][0]) + tn(MST[l, p, j, 1], dos[j][1]) for j in units
            ]
            dw = [
                nn(upper_ones, dz_hi[j])
                + nn(upper_ones, dz_lo[j])
                + tn(YST[p, j, 0], rs[j][0])
                + tn(AST[l, p, j, 0], dns[j][0])
                + tn(YST[p, j, 1], rs[j][1])
                + tn(AST[l, p, j, 1], dns[j][1])
                for j in units
            ]
            for j in units:
                DU[p, rows[j], pl.ds(0, 128)] = dq[j].astype(BF)
                DWF[p, rows[j], pl.ds(0, 128)] = dk[j]
                DWF[p, rows[j], pl.ds(128, 128)] = dv[j]
                DWF[p, rows[j], pl.ds(256, 128)] = dw[j]

        def with_later(k, p, l=l):
            k_post, v_post, z_after = scans[k].end()
            for j in range(tiles - 1, -1, -1):
                rows = tile_rows(j)
                if j < tiles - 1:
                    k_post = k_post + LOC[p, j, 0]
                    v_post = v_post + LOC[p, j, 1]
                    z_after = z_after + jnp.sum(DZ[p, tile_rows(j + 1)], axis=0, keepdims=True)
                kb, vb = k_post.astype(BF), v_post.astype(BF)
                w = WB[l, p, rows]
                key = QKV[l, p, rows, pl.ds(128, 128)]
                v = QKV[l, p, rows, pl.ds(256, 128)]
                dk = DWF[p, rows, pl.ds(0, 128)] + nn(w, kb)
                dv = DWF[p, rows, pl.ds(128, 128)] + nn(w, vb)
                dw = DWF[p, rows, pl.ds(256, 128)] + nt(key, kb) + nt(v, vb) + z_after
                dc = dw * w.astype(F32) * S2[l, p, rows].astype(F32)
                DU[p, rows, pl.ds(128, 128)] = dk.astype(BF)
                DU[p, rows, pl.ds(256, 128)] = dv.astype(BF)
                DU[p, rows, pl.ds(384, 128)] = dc.astype(BF)

        totals = to_states()
        for k in range(2):
            scans[k].start(*totals[k])
        at(bwd(l, 3))
        for k in range(2):
            scans[k].step()
            at(bwd(l, 4 + k))
        for k in range(2):
            p = order[k]
            within(p)
            RQ[l, p] = split_rows(tn(AB[l], DU[p, :, pl.ds(0, 128)]))
            at(bwd(l, 6 + k))
        for k in range(2):
            p = order[k]
            with_later(k, p)
            grads = split_rows(tn(AB[l], DU[p, :, pl.ds(128, 384)]))
            RKV[l, p] = grads[..., :256]
            RC[l, p] = grads[..., 256:]
            at(bwd(l, 8 + k))
        handles = []
        for i in range(tiles):
            rows = tile_rows(i)
            part = nt(DU[0, rows], mixer_weight(l, 0))
            part = part + nt(DU[1, rows], mixer_weight(l, 1))
            handles.append(share_start(part))
        at(bwd(l, 10))
        gsum = jnp.zeros((1, D), F32)
        for i in range(tiles):
            rows = tile_rows(i)
            da = share_end(handles[i])
            y_hat, rstd = norm_parts(stream(l, rows))
            gsum = gsum + jnp.sum(da * y_hat, axis=0, keepdims=True)
            da = da * gain_row(l, 0)
            dh = DMID[rows] + (
                da
                - jnp.mean(da, axis=-1, keepdims=True)
                - y_hat * jnp.mean(da * y_hat, axis=-1, keepdims=True)
            ) * rstd
            DMID[rows] = dh
            if l == 0:
                OUTB[1, y, rows] = dh.astype(BF)
        grad_norm[2 * l] = gsum
        at(bwd(l, 11))

    class Gains:
        def start(self):
            sub = lax.broadcasted_iota(jnp.int32, (8, D), 0)
            self.rows = jnp.zeros((8, D), F32)
            for k in range(2 * layers):
                self.rows = jnp.where(sub == k, grad_norm[k], self.rows)
            GN[...] = self.rows
            self.c = send(GN, GNY, y_peer)

        def hop(self):
            self.c.wait_recv()
            both = self.rows + GNY[...]
            for gz in range(GROUPS // 2):
                GNR[0, gz] = both[:, gz * 128 : (gz + 1) * 128]
            self.c = arrival()
            for d in range(4):
                for o in range(2):
                    if (d, o) == (0, 0):
                        continue
                    peer = (seq_of(1 - x if o else x, flip_z(d)), m)
                    k = 2 * d + o
                    send(GNR.at[0, flip_z(d)], GNR.at[1, k], peer, self.c)

        def end(self):
            total = GNR[0, z]
            arrived(GNR.at[1, pl.ds(1, 7)], self.c)
            for k in range(1, 8):
                total = total + GNR[1, k]
            GNO[...] = total
            finals.append(local(GNO, gn_hbm))

    f = Gains()
    jobs[GAINS, 0] = {START: f.start, HOP: f.hop, END: f.end}
    at(TAIL)
    for c in finals:
        c.wait()
    for c in (*leaving.values(), *share_prev.values()):
        c.wait_send()
    assert used[0] == recv_sems.shape[0] and used[1] == local_sems.shape[0], used


def lay_out(stride, *refs):
    mixed, tokens, qkv, ctrl, out, up, down, gains = refs[:8]
    mixed_out, tokens_out, attn_out, ffn_out, *weights_out = refs[8:17]
    wide, sems, *held = refs[17:]
    arrays = (tokens, mixed, up, down, qkv, ctrl, out)
    results = (None, mixed_out, weights_out[3], weights_out[4], *weights_out[:3])
    parts = [(k, b) for k in range(len(arrays)) for b in range(2)]
    ins = {
        (k, b): pltpu.make_async_copy(arrays[k].at[b], held[k].at[b], sems.at[0, k, b])
        for k, b in parts
    }
    for c in ins.values():
        c.start()
    x = (lax.axis_index("seq") // stride) % 2
    R = attn_out.shape[1]
    rows = jnp.where(x == 0, gains[:, pl.ds(0, R)], gains[:, pl.ds(R, R)])
    for l in range(attn_out.shape[0]):
        attn_out[pl.ds(l, 1), :] = rows[2 * l : 2 * l + 1]
        ffn_out[pl.ds(l, 1), :] = rows[2 * l + 1 : 2 * l + 2]
    outs = []
    for k, b in parts:
        ins[k, b].wait()
        if k == 0:
            wide[b] = held[0][b].astype(F32)
            c = pltpu.make_async_copy(wide.at[b], tokens_out.at[b], sems.at[1, k, b])
        else:
            c = pltpu.make_async_copy(held[k].at[b], results[k].at[b], sems.at[1, k, b])
        c.start()
        outs.append(c)
    for c in outs:
        c.wait()


def shards(tokens, lengths, norm_attn, norm_ffn, w_qkv, w_ctrl, w_out, w_up, w_down, cotangent):
    layers = w_qkv.shape[0]
    n_seq = lax.axis_size("seq")
    stride = n_seq // GROUPS
    _, T, D = tokens.shape
    rows = w_qkv.shape[1]
    weights = [w_qkv.transpose(0, 2, 1, 3), w_ctrl, w_up, w_down, w_out]
    gains = [norm_attn, norm_ffn]
    blocks = [[k * stride + j for j in range(stride)] for k in range(GROUPS)]
    if stride > 1:

        def fill(a, dim=1):
            return lax.all_gather(a, "seq", axis=dim, tiled=True, axis_index_groups=blocks)

        weights = [fill(a, a.ndim - 2) for a in weights]
        gains = [fill(a) for a in gains]
    R = D // GROUPS
    A = 3 * w_qkv.shape[-1] + w_ctrl.shape[-1]
    U = w_up.shape[-1]
    F = 2 * U + w_out.shape[-1]
    near = near_size(n_seq)
    far = n_seq // near
    tiles = T // TILE
    arrivals = 1 + sum(19 if (n, l) in GATHER_Z_SECOND else 13 for n in range(3) for l in range(layers))
    arrivals += 2 * tiles + 4 * layers * (near + far - 2)
    arrivals += sum(5 if (n, l) in Z_SECOND else 4 for n in range(Q, DOWN + 1) for l in range(layers))
    arrivals += 4 + 2
    bf, f32 = BF, F32
    v = pltpu.VMEM
    scratch = [
        v((max(layers - 1, 1), T, D), f32),
        v((layers, T, D), f32),
        v((layers, T, D), bf),
        v((layers, T, D), bf),
        v((layers, 2, T, 384), bf),
        v((layers, 2, T, 128), bf),
        v((layers, 2, T, 128), bf),
        v((layers, 2, T, 128), f32),
        v((layers, 2, T, 128), f32),
        v((layers, 2, T, 128), f32),
        v((layers, 2, tiles, 2, TILE, TILE), bf),
        v((layers, 2, tiles, 2, TILE, TILE), bf),
        v((layers, T, 256), bf),
        v((layers, 2, T, U), bf),
        v((layers, 2, T, U), bf),
        v((layers, 2, tiles, 128, 128), bf),
        v((layers, 2, tiles, 128, 128), bf),
        v((2, max(tiles - 1, 1), 2, 128, 128), f32),
        v((2, T, D), bf),
        v((T, D), bf),
        v((2, T, 128), bf),
        v((2, T, U), bf),
        v((T, D), f32),
        v((2, tiles, 2, TILE, TILE), bf),
        v((2, T, 128), bf),
        v((2, T, 128), f32),
        v((2, T, 384), f32),
        v((layers, 2, 4, 2, R, A), bf),
        v((layers, 2, 4, 2, R, F), bf),
        v((8, 8, 128), f32),
        v((2, layers, R), bf),
        v((8, D), f32),
        v((tiles, TILE, D), bf),
        v((2 * tiles, TILE, D), bf),
        v((4 * layers, 144, 128), bf),
        v((4 * layers, near - 1, 144, 128), bf),
        v((4 * layers, far - 1, 144, 128), bf),
        v((2, 144, 128), f32),
        v((layers, 2, 4, 2, R, 128), bf),
        v((layers, 2, 4, 2, R, 256), bf),
        v((layers, 2, 4, 2, R, 128), bf),
        v((layers, 2, 4, 2, R, 128), bf),
        v((layers, 2, 4, 2, R, U), bf),
        v((layers, 2, 4, 2, R, U), bf),
        v((layers, 15, R, 128), bf),
        v((layers, 15, R, 256), bf),
        v((layers, 15, R, 128), bf),
        v((layers, 15, R, 128), bf),
        v((layers, 15, R, U), bf),
        v((layers, 15, R, U), bf),
        v((layers, 3, R, 128), f32),
        v((layers, R, 128), f32),
        v((layers, R, 128), f32),
        v((layers, R, U), f32),
        v((layers, R, U), f32),
        v((8, D), f32),
        v((8, D), f32),
        v((2, 8, 8, 128), f32),
        v((8, 128), f32),
        v((2, 2, T, D), bf),
        pltpu.SemaphoreType.DMA((SEND_RING + tiles + 2 * (far - 1),)),
        pltpu.SemaphoreType.DMA((arrivals,)),
        pltpu.SemaphoreType.DMA((7 + 13 * layers,)),
    ]
    any_spec = pl.BlockSpec(memory_space=pl.ANY)
    out_shape = (
        jax.ShapeDtypeStruct((2, T, D), bf),
        jax.ShapeDtypeStruct((2, T, D), bf),
        jax.ShapeDtypeStruct((layers, 3, R, 128), f32),
        jax.ShapeDtypeStruct((layers, R, 128), f32),
        jax.ShapeDtypeStruct((layers, R, 128), f32),
        jax.ShapeDtypeStruct((layers, R, U), f32),
        jax.ShapeDtypeStruct((layers, R, U), f32),
        jax.ShapeDtypeStruct((8, 128), f32),
    )
    mixed, grad_tokens, *grads, gn = pl.pallas_call(
        functools.partial(kernel, n_seq, layers),
        out_shape=out_shape,
        in_specs=[
            any_spec,
            any_spec,
            pl.BlockSpec(memory_space=pltpu.SMEM),
            *[any_spec] * 7,
        ],
        out_specs=(any_spec,) * len(out_shape),
        scratch_shapes=scratch,
        compiler_params=pltpu.CompilerParams(
            collective_id=0, has_side_effects=True, vmem_limit_bytes=VMEM_BYTES
        ),
    )(tokens, cotangent, lengths, *weights, *gains)
    out_shape = (
        jax.ShapeDtypeStruct((2, T, D), bf),
        jax.ShapeDtypeStruct((2, T, D), f32),
        jax.ShapeDtypeStruct((layers, R), f32),
        jax.ShapeDtypeStruct((layers, R), f32),
        *[jax.ShapeDtypeStruct(a.shape, f32) for a in grads],
    )
    vmem_spec = pl.BlockSpec(memory_space=pltpu.VMEM)
    mixed, grad_tokens, *grads = pl.pallas_call(
        functools.partial(lay_out, stride),
        out_shape=out_shape,
        in_specs=[any_spec] * 7 + [vmem_spec],
        out_specs=(any_spec, any_spec, vmem_spec, vmem_spec) + (any_spec,) * 5,
        scratch_shapes=[
            v((2, T, D), f32),
            pltpu.SemaphoreType.DMA((2, 7, 2)),
            *[v(a.shape, a.dtype) for a in (grad_tokens, mixed, *grads[3:], *grads[:3])],
        ],
        compiler_params=pltpu.CompilerParams(vmem_limit_bytes=VMEM_BYTES),
    )(mixed, grad_tokens, *grads, gn)
    if stride > 1:

        def empty(a):
            return lax.psum_scatter(
                a, "seq", scatter_dimension=max(a.ndim - 2, 1), tiled=True, axis_index_groups=blocks
            )

        grads = [empty(a) for a in grads]
    grads[2] = grads[2].transpose(0, 2, 1, 3)
    return (mixed, grad_tokens, *grads)


VMEM_BYTES = 62 << 20


def solution(mesh):
    in_specs = (
        P(None, "seq", None),
        P(),
        P(None, "seq"),
        P(None, "seq"),
        P(None, "seq", None, "mp"),
        P(None, "seq", "mp"),
        P(None, "seq", "mp"),
        P(None, "seq", "mp"),
        P(None, "seq", "mp"),
        P(None, "seq", None),
    )
    out_specs = (
        P(None, "seq", None),
        P(None, "seq", None),
        P(None, "seq"),
        P(None, "seq"),
        P(None, "seq", None, "mp"),
        P(None, "seq", "mp"),
        P(None, "seq", "mp"),
        P(None, "seq", "mp"),
        P(None, "seq", "mp"),
    )
    return jax.shard_map(shards, mesh=mesh, in_specs=in_specs, out_specs=out_specs, check_vma=False)
```

```python
import functools

import jax
import jax.numpy as jnp
from jax import lax
from jax.experimental import pallas as pl
from jax.experimental.pallas import tpu as pltpu
from jax.sharding import PartitionSpec as P

F32 = jnp.float32
BF = jnp.bfloat16
MESH = pl.DeviceIdType.MESH
GROUPS = 8
HEAD = 64
EPS = 1e-05
TILE = 256


def nn(a, b):
    return lax.dot_general(a, b, (((1,), (0,)), ((), ())), preferred_element_type=F32)


def nt(a, b):
    return lax.dot_general(a, b, (((1,), (1,)), ((), ())), preferred_element_type=F32)


def tn(a, b):
    return lax.dot_general(a, b, (((0,), (0,)), ((), ())), preferred_element_type=F32)


def near_size(n_seq):
    return 1 << ((n_seq.bit_length() - 1) // 2)


def norm_parts(x):
    center = x - jnp.mean(x, axis=-1, keepdims=True)
    spread = jnp.mean(center * center, axis=-1, keepdims=True)
    rstd = lax.rsqrt(spread + EPS)
    return center * rstd, rstd


def gate_and_slope(u):
    u2 = u * u
    t = jnp.tanh(u * (0.7978845608 + (0.7978845608 * 0.044715) * u2))
    half = 0.5 + 0.5 * t
    gate = u * half
    slope = half + gate * (1.0 - half) * (1.5957691216 + (1.5957691216 * 0.134145) * u2)
    return gate, slope


MIXER, UPPER, LOWER, Q, KV, C, OUT, UP, DOWN, MIXED, TOKENS, GAINS = range(12)
START, OWN, ON1, ON2, ON3, ACROSS0, ACROSS1, ACROSS2, ACROSS3, END = range(10)
GRAD1, GRAD0, START1, START0, ADD1, ADD0, TURN, HOP, RELAY = range(10, 19)


def fwd(layer, k):
    return 100 + 20 * layer + k


def bwd(layer, k):
    return 200 + 20 * layer + k


ENTRY, FIRST, TAIL = 0, 1, 2
SEND_RING = 48

X_FIRST = {(Q, 1), (C, 1), (OUT, 0), (OUT, 1), (DOWN, 0), (DOWN, 1)}
Z_SECOND = {(C, 1), (DOWN, 1)}
GATHER_Z_SECOND = {(UPPER, 0), (LOWER, 1)}
PLAN = {
    ENTRY: (
        (MIXER, 0, START),
        (UPPER, 0, OWN),
        (MIXER, 0, OWN),
        (LOWER, 0, START),
        (LOWER, 0, OWN),
        (MIXER, 0, ON1),
        (MIXER, 0, ACROSS0),
        (MIXER, 0, ON2),
        (UPPER, 0, ON2),
        (UPPER, 0, ON3),
        (UPPER, 0, ON1),
        (MIXER, 1, START),
        (MIXER, 0, ACROSS1),
        (MIXER, 0, ON3),
        (UPPER, 0, START),
        (LOWER, 0, ON1),
        (MIXER, 0, ACROSS2),
        (MIXER, 0, ACROSS3),
        (MIXER, 1, ON1),
    ),
    FIRST: (
        (LOWER, 0, ON2),
        (UPPER, 0, ACROSS0),
        (MIXER, 0, END),
    ),
    fwd(0, 0): (
        (LOWER, 0, ON3),
    ),
    fwd(0, 2): (
        (LOWER, 1, OWN),
        (LOWER, 0, ACROSS0),
        (LOWER, 0, ACROSS1),
    ),
    fwd(0, 3): (
        (UPPER, 0, ACROSS2),
    ),
    fwd(0, 4): (
        (MIXER, 1, OWN),
    ),
    fwd(0, 5): (
        (MIXER, 1, ACROSS1),
        (LOWER, 0, ACROSS2),
        (LOWER, 0, ACROSS3),
    ),
    fwd(0, 6): (
        (UPPER, 0, ACROSS3),
        (UPPER, 1, START),
        (MIXER, 1, ON2),
        (UPPER, 0, ACROSS1),
        (LOWER, 1, START),
        (LOWER, 0, END),
    ),
    fwd(0, 7): (
        (MIXER, 1, ON3),
    ),
    fwd(0, 8): (
        (MIXER, 1, ACROSS0),
        (UPPER, 0, END),
        (MIXER, 1, ACROSS2),
        (LOWER, 1, ON2),
        (LOWER, 1, ON1),
    ),
    fwd(0, 9): (
        (MIXER, 1, ACROSS3),
        (LOWER, 1, ON3),
        (UPPER, 1, ON2),
    ),
    fwd(0, 10): (
        (MIXER, 1, END),
        (UPPER, 1, ON1),
    ),
    fwd(1, 1): (
        (UPPER, 1, ON3),
    ),
    fwd(1, 2): (
        (LOWER, 1, ACROSS1),
        (LOWER, 1, ACROSS2),
    ),
    fwd(1, 3): (
        (UPPER, 1, ACROSS1),
        (LOWER, 1, ACROSS0),
        (UPPER, 1, ACROSS2),
    ),
    fwd(1, 5): (
        (UPPER, 1, OWN),
        (LOWER, 1, ACROSS3),
    ),
    fwd(1, 6): (
        (UPPER, 1, ACROSS0),
        (UPPER, 1, ACROSS3),
    ),
    fwd(1, 7): (
        (LOWER, 1, END),
    ),
    fwd(1, 8): (
        (UPPER, 1, END),
    ),
    bwd(1, 0): (
        (DOWN, 1, GRAD1),
        (DOWN, 1, START1),
    ),
    bwd(1, 1): (
        (UP, 1, GRAD1),
        (UP, 1, START1),
        (DOWN, 1, GRAD0),
    ),
    bwd(1, 2): (
        (OUT, 1, GRAD1),
    ),
    bwd(1, 3): (
        (DOWN, 1, START0),
        (UP, 1, START0),
    ),
    bwd(1, 4): (
        (OUT, 1, START1),
        (OUT, 1, START0),
    ),
    bwd(1, 5): (
        (UP, 1, GRAD0),
    ),
    bwd(1, 6): (
        (MIXED, 0, START),
    ),
    bwd(1, 7): (
        (UP, 1, ADD1),
        (UP, 1, ADD0),
    ),
    bwd(1, 8): (
        (DOWN, 1, ADD1),
        (DOWN, 1, ADD0),
        (KV, 1, START1),
        (Q, 1, START0),
        (Q, 1, START1),
    ),
    bwd(1, 9): (
        (C, 1, START0),
    ),
    bwd(1, 10): (
        (MIXED, 0, HOP),
        (C, 1, START1),
        (KV, 1, START0),
    ),
    bwd(0, 0): (
        (OUT, 1, ADD1),
        (DOWN, 0, GRAD1),
    ),
    bwd(0, 1): (
        (UP, 0, GRAD1),
        (DOWN, 1, RELAY),
        (MIXED, 0, END),
        (DOWN, 0, GRAD0),
    ),
    bwd(0, 2): (
        (UP, 0, START1),
        (UP, 0, GRAD0),
    ),
    bwd(0, 3): (
        (DOWN, 0, START1),
        (KV, 1, ADD1),
        (KV, 1, ADD0),
        (UP, 1, TURN),
    ),
    bwd(0, 4): (
        (Q, 1, ADD1),
        (C, 1, ADD0),
    ),
    bwd(0, 5): (
        (UP, 0, START0),
        (UP, 1, RELAY),
        (OUT, 1, ADD0),
        (Q, 1, ADD0),
        (OUT, 0, GRAD1),
    ),
    bwd(0, 6): (
        (C, 1, ADD1),
        (DOWN, 0, START0),
        (OUT, 1, TURN),
    ),
    bwd(0, 7): (
        (DOWN, 0, ADD1),
        (Q, 0, START0),
        (Q, 0, START1),
        (UP, 0, ADD1),
        (Q, 1, TURN),
        (KV, 1, TURN),
    ),
    bwd(0, 8): (
        (C, 0, START1),
        (UP, 0, ADD0),
        (DOWN, 0, ADD0),
        (OUT, 1, RELAY),
        (KV, 0, START1),
        (DOWN, 0, TURN),
        (C, 1, RELAY),
        (UP, 1, END),
    ),
    bwd(0, 9): (
        (Q, 1, RELAY),
        (KV, 1, RELAY),
        (OUT, 0, START1),
        (OUT, 0, START0),
        (Q, 0, ADD1),
        (C, 0, START0),
        (OUT, 1, END),
        (KV, 0, START0),
    ),
    bwd(0, 10): (
        (DOWN, 0, RELAY),
        (UP, 0, TURN),
        (Q, 0, ADD0),
        (OUT, 0, ADD1),
        (C, 0, ADD1),
        (KV, 0, ADD1),
    ),
    bwd(0, 11): (
        (C, 1, TURN),
        (C, 0, ADD0),
        (UP, 0, RELAY),
    ),
    TAIL: (
        (OUT, 0, ADD0),
        (GAINS, 0, START),
        (TOKENS, 0, START),
        (Q, 0, TURN),
        (KV, 0, ADD0),
        (Q, 1, END),
        (DOWN, 1, TURN),
        (C, 0, TURN),
        (Q, 0, RELAY),
        (OUT, 0, TURN),
        (C, 1, END),
        (C, 0, RELAY),
        (KV, 0, TURN),
        (DOWN, 0, END),
        (UP, 0, END),
        (KV, 1, END),
        (GAINS, 0, HOP),
        (OUT, 0, RELAY),
        (Q, 0, END),
        (KV, 0, RELAY),
        (C, 0, END),
        (TOKENS, 0, HOP),
        (OUT, 0, END),
        (DOWN, 1, END),
        (GAINS, 0, END),
        (KV, 0, END),
        (TOKENS, 0, END),
    ),
}


def kernel(
    n_seq,
    layers,
    tok_hbm,
    cot_hbm,
    len_ref,
    qkv_hbm,
    ctrl_hbm,
    up_hbm,
    down_hbm,
    out_hbm,
    norm_attn_hbm,
    norm_ffn_hbm,
    mixed_hbm,
    gt_hbm,
    gqkv_hbm,
    gctrl_hbm,
    gout_hbm,
    gup_hbm,
    gdown_hbm,
    gn_hbm,
    H,
    MID,
    AB,
    FB,
    QKV,
    WB,
    S2,
    ZS,
    PS,
    XS,
    AST,
    MST,
    OB,
    GU,
    GG,
    KP,
    VP,
    LOC,
    TOKB,
    GBF,
    DOB,
    DU,
    DMID,
    YST,
    DNB,
    DZ,
    DWF,
    WA,
    WF,
    GAIN,
    GROW,
    GFULL,
    ARS,
    ARR,
    SCS,
    SCR1,
    SCR2,
    SCP,
    RQ,
    RKV,
    RC,
    ROUT,
    RUP,
    RDN,
    LQ,
    LKV,
    LC,
    LOUT,
    LUP,
    LDN,
    OQKV,
    OCTRL,
    OOUT,
    OUP,
    ODN,
    GN,
    GNY,
    GNR,
    GNO,
    OUTB,
    send_sems,
    inner_sems,
    recv_sems,
    local_sems,
):
    T, D = TOKB.shape[1], TOKB.shape[2]
    tiles = T // TILE
    R = D // GROUPS
    stride = n_seq // GROUPS
    s = lax.axis_index("seq")
    m = lax.axis_index("mp")
    y, core = m // 2, m % 2
    g, lo = s // stride, s % stride
    x, z = g % 2, g // 2
    z1, z0 = z // 2, z % 2
    inner = z1 != z0
    last = layers - 1

    def flip_z(d):
        d1, d0 = d // 2, d % 2
        return 2 * (1 - z1 if d1 else z1) + (1 - z0 if d0 else z0)

    def seq_of(gx, gz):
        return (gz * 2 + gx) * stride + lo

    core_peer = (s, 2 * y + (1 - core))
    y_peer = (s, 2 * (1 - y) + core)
    x_peer = (seq_of(1 - x, z), m)
    z_peer = {d: (seq_of(x, flip_z(d)), m) for d in (1, 2, 3)}
    near = near_size(n_seq)
    blocks = n_seq // near
    low, high = s % near, s // near

    used = [0, 0, 0]
    leaving = {}

    def arrival():
        used[0] += 1
        return recv_sems.at[used[0] - 1]

    def remote(src, dst, peer, leave, arrive):
        return pltpu.make_async_remote_copy(
            src_ref=src,
            dst_ref=dst,
            send_sem=leave,
            recv_sem=arrive,
            device_id=peer,
            device_id_type=MESH,
        )

    def send(src, dst, peer, arrive=None):
        k = used[2] % SEND_RING
        used[2] += 1
        if k in leaving:
            leaving[k].wait_send()
        c = remote(src, dst, peer, send_sems.at[k], arrival() if arrive is None else arrive)
        c.start()
        leaving[k] = c
        return c

    def send_if_inner(src, dst, peer, arrive, leave):
        c = remote(src, dst, peer, leave, arrive)

        @pl.when(inner)
        def _():
            c.start()

        return c

    def leave_done(c):
        for k, other in list(leaving.items()):
            if other is c:
                c.wait_send()
                del leaving[k]

    def arrived(region, arrive):
        remote(region, region, core_peer, send_sems.at[0], arrive).wait_recv()

    def local(src, dst):
        k = used[1]
        used[1] += 1
        c = pltpu.make_async_copy(src, dst, local_sems.at[k])
        c.start()
        return c

    barrier = pltpu.get_barrier_semaphore()

    def hello(peer):
        pl.semaphore_signal(barrier, inc=1, device_id=peer, device_id_type=MESH)

    hello(core_peer)
    hello(y_peer)
    count = 2
    for d in range(1, near):
        hello((high * near + lax.rem(low + d, near), m))
        count += 1
    for d in range(1, blocks):
        other = lax.rem(high + d, blocks) * near
        hello((other + low, m))
        count += 1
        if stride == 1:
            hello((other + 1 - low, m))
            count += 1

    rows_in = [local(norm_attn_hbm, GROW.at[0]), local(norm_ffn_hbm, GROW.at[1])]
    own = []
    for l in range(layers):
        for k in range(4):
            src = qkv_hbm.at[l, k] if k < 3 else ctrl_hbm.at[l]
            own.append(local(src, WA.at[l, y, z, x, slice(None), pl.ds(k * 128, 128)]))
        lanes = 0
        for src in (up_hbm, down_hbm, out_hbm):
            at = pl.ds(lanes, src.shape[-1])
            own.append(local(src.at[l], WF.at[l, y, z, x, slice(None), at]))
            lanes += src.shape[-1]
    tok_copy = local(tok_hbm.at[y], TOKB.at[0])
    cot_copy = local(cot_hbm.at[y], TOKB.at[1])
    gain_sub = lax.broadcasted_iota(jnp.int32, (8, R), 0)
    own_gains = jnp.zeros((8, R), F32)
    for c in rows_in:
        c.wait()
    for l in range(layers):
        for k in range(2):
            row = GROW[k].astype(F32)[l : l + 1]
            own_gains = jnp.where(gain_sub == 2 * l + k, row, own_gains)
    GAIN[0, :, pl.ds(0, R)] = jnp.where(x == 0, own_gains, 0.0)
    GAIN[0, :, pl.ds(R, R)] = jnp.where(x == 0, 0.0, own_gains)

    pl.semaphore_wait(barrier, count)

    every = slice(None)

    inner_used = [0]
    inner_last = []

    def inner_leave():
        inner_used[0] += 1
        return inner_sems.at[inner_used[0] - 1]

    class Gather:
        def __init__(self, buf, l, low_end, cut, high_end, z_second):
            self.buf, self.l, self.c = buf, l, {}
            self.all = pl.ds(low_end, high_end - low_end)
            self.first, self.second = pl.ds(low_end, cut - low_end), pl.ds(cut, high_end - cut)
            self.z_second = z_second
            self.last = None
            self.inner = {}

        def along_z(self, kind, region, lanes=None):
            for d in (1, 2):
                self.push((kind, d), region, z_peer[d], lanes)
            src = self.buf.at[(self.l,) + region + (slice(None), lanes or self.all)]
            arrive, leave = arrival(), inner_leave()
            self.c[kind, 3] = send_if_inner(src, src, z_peer[3], arrive, leave)
            self.inner[kind] = (self.c[kind, 3], arrive, leave)

        def pass_on(self, kind, region, lanes=None):
            before, arrive, leave = self.inner[kind]

            @pl.when(inner)
            def _():
                before.wait_send()

            src = self.buf.at[(self.l,) + region + (slice(None), lanes or self.all)]
            inner_last.append(send_if_inner(src, src, z_peer[1], arrive, leave))

        def push(self, key, region, peer, lanes=None):
            src = self.buf.at[(self.l,) + region + (slice(None), lanes or self.all)]
            arrive = None
            if key[0] in (5, 6) and not self.z_second:
                self.last = self.last or {5: arrival(), 6: arrival()}
                arrive = self.last[key[0]]
            self.c[key] = send(src, src, peer, arrive)

        def take(self, *keys):
            for key in keys:
                self.c[key].wait_recv()

        def start(self):
            self.along_z(0, (y, z, x))

        def own(self):
            self.push((1, 0), (y, z, x), x_peer)
            self.push((2, 0), (y, z, x), y_peer)

        def on(self, d):
            if not self.z_second:
                self.take((0, d))
                if d == 2:
                    self.pass_on(0, (y, flip_z(d), x))
                self.push((1, d), (y, flip_z(d), x), x_peer)
                self.push((2, d), (y, flip_z(d), x), y_peer)
            elif d == 1:
                self.take((1, 0))
                self.along_z(3, (y, z, 1 - x), self.first)
                self.push((5, 0), (y, z, 1 - x), y_peer, self.first)
            elif d == 2:
                self.take((2, 0))
                self.along_z(4, (1 - y, z, x), self.second)
                self.push((6, 0), (1 - y, z, x), x_peer, self.second)

        def across(self, d):
            zz = flip_z(d)
            if not self.z_second:
                self.take((1, d))
                self.push((5, d), (y, zz, 1 - x), y_peer, self.first)
                self.take((2, d))
                self.push((6, d), (1 - y, zz, x), x_peer, self.second)
            elif d:
                self.take((0, d), (3, d))
                if d == 2:
                    self.pass_on(0, (y, zz, x))
                    self.pass_on(3, (y, zz, 1 - x), self.first)
                self.push((5, d), (y, zz, slice(None)), y_peer, self.first)
                self.take((4, d))
                if d == 2:
                    self.pass_on(4, (1 - y, zz, x), self.second)
                self.push((6, d), (slice(None), zz, x), x_peer, self.second)

        def end(self):
            if self.z_second:
                for d in range(4):
                    self.take((5, d), (6, d))
                return
            far = self.buf.at[self.l, 1 - y, every, 1 - x]
            arrived(far.at[:, :, self.first], self.last[5])
            arrived(far.at[:, :, self.second], self.last[6])

        def parts(self):
            part = {START: self.start, OWN: self.own, END: self.end}
            for d in (1, 2, 3):
                part[ON1 + d - 1] = functools.partial(self.on, d)
            for d in range(4):
                part[ACROSS0 + d] = functools.partial(self.across, d)
            return part

    gains_here = arrival()
    for d in (0, 1, 2, 3):
        for o in (0, 1):
            if (d, o) == (0, 0):
                continue
            peer = (seq_of(1 - x if o else x, flip_z(d)), m)
            send(GAIN.at[0], GAIN.at[d * 2 + o], peer, gains_here)
    for c in own:
        c.wait()
    jobs = {}
    for l in range(layers):
        for name, buf, bounds in (
            (MIXER, WA, (0, 256, 512)),
            (UPPER, WF, (0, 256, 512)),
            (LOWER, WF, (512, 896, 1152)),
        ):
            jobs[name, l] = Gather(buf, l, *bounds, (name, l) in GATHER_Z_SECOND).parts()

    def at(place):
        for name, l, part in PLAN.get(place, ()):
            jobs[name, l][part]()

    at(ENTRY)

    lane = lax.broadcasted_iota(jnp.int32, (TILE, 128), 1)
    first = lane < HEAD
    head_rows = [
        (lax.broadcasted_iota(jnp.int32, (1, 128), 1) < HEAD).astype(F32).astype(BF),
        (lax.broadcasted_iota(jnp.int32, (1, 128), 1) >= HEAD).astype(F32).astype(BF),
    ]
    rr = lax.broadcasted_iota(jnp.int32, (TILE, TILE), 0)
    cc = lax.broadcasted_iota(jnp.int32, (TILE, TILE), 1)
    lower = rr >= cc
    lower_ones = lower.astype(F32).astype(BF)
    upper_ones = (rr <= cc).astype(F32).astype(BF)
    diag = (lax.broadcasted_iota(jnp.int32, (128, 128), 0) < HEAD) == (
        lax.broadcasted_iota(jnp.int32, (128, 128), 1) < HEAD
    )

    def per_head(value):
        a = jnp.sum(jnp.where(first, value, 0.0), axis=-1, keepdims=True)
        b = jnp.sum(jnp.where(first, 0.0, value), axis=-1, keepdims=True)
        return jnp.where(first, a, b)

    def per_head_max(value):
        a = jnp.max(jnp.where(first, value, -jnp.inf), axis=-1, keepdims=True)
        b = jnp.max(jnp.where(first, -jnp.inf, value), axis=-1, keepdims=True)
        return jnp.where(first, a, b)

    def heads(value):
        return value * head_rows[0], value * head_rows[1]

    def tile_rows(i):
        return pl.ds(i * TILE, TILE)

    def weight(buf, l, p, start, width):
        return buf[l, p, :, :, :, pl.ds(start, width)].reshape(D, width)

    def mixer_weight(l, p):
        return weight(WA, l, p, 0, 512)

    def up_weight(l, p):
        return weight(WF, l, p, 0, 512)

    def down_weight(l, p):
        return weight(WF, l, p, 512, 512)

    def out_weight(l, p):
        return weight(WF, l, p, 1024, 128)

    shared = [0]
    share_sems = [[send_sems.at[SEND_RING + k] for k in range(ARS.shape[0])]]
    share_sems.append([arrival() for _ in range(ARR.shape[0])])
    share_prev = {}

    def share_start(value):
        k = shared[0]
        shared[0] += 1
        slot = k % ARS.shape[0]
        if slot in share_prev:
            share_prev[slot].wait_send()
        ARS[slot] = value.astype(BF)
        k = k % ARR.shape[0]
        c = remote(ARS.at[slot], ARR.at[k], core_peer, share_sems[0][slot], share_sems[1][k])
        c.start()
        share_prev[slot] = c
        return c, slot, k

    def share_end(handle):
        c, slot, k = handle
        c.wait_recv()
        return ARS[slot].astype(F32) + ARR[k].astype(F32)

    class Scan:
        def __init__(self, call, forward):
            self.call, self.forward = call, forward

        def pack_normalizer(self, which, part):
            sub = lax.broadcasted_iota(jnp.int32, (16, 128), 0)
            rest = jnp.zeros((16, 128), F32)
            for k in range(3):
                piece = part.astype(BF).astype(F32)
                rest = jnp.where(sub == k, piece, rest)
                part = part - piece
            SCS[which, pl.ds(128, 16)] = rest.astype(BF)

        def start(self, k_state, v_state, z_row):
            which = self.call
            SCS[which, pl.ds(0, 128)] = (k_state + pltpu.roll(v_state, HEAD, 1)).astype(BF)
            self.pack_normalizer(which, z_row)
            self.near = []
            for d in range(1, near):
                peer = (high * near + lax.rem(low + d, near), m)
                self.near.append(send(SCS.at[which], SCR1.at[self.call, d - 1], peer))

        def step(self):
            for c in self.near:
                c.wait_recv()
                leave_done(c)
            which = self.call
            both = SCS[which].astype(F32)
            for d in range(1, near):
                both = both + SCR1[self.call, d - 1].astype(F32)
            SCS[which, pl.ds(0, 128)] = both[:128].astype(BF)
            self.pack_normalizer(which, jnp.sum(both[128:131], axis=0, keepdims=True))
            self.links = []
            for d in range(1, blocks):
                to = high + d if self.forward else high - d
                frm = high - d if self.forward else high + d
                inside = to < blocks if self.forward else to >= 0
                comes = frm >= 0 if self.forward else frm < blocks
                target = jnp.where(inside, to, high)
                leave = send_sems.at[SEND_RING + ARS.shape[0] + (self.call % 2) * (blocks - 1) + d - 1]
                target = (target * near + low, m)
                c = remote(SCS.at[which], SCR2.at[self.call, d - 1], target, leave, arrival())

                @pl.when(inside)
                def _(c=c):
                    c.start()

                self.links.append((c, inside, comes))

        def end(self):
            acc = SCP.at[self.call % 2]
            before = jnp.zeros(acc.shape, F32)
            for d in range(1, near):
                mine = low >= d if self.forward else low < d
                before = before + jnp.where(mine, SCR1[self.call, d - 1].astype(F32), 0.0)
            acc[...] = before
            for d, (c, inside, comes) in enumerate(self.links):

                @pl.when(comes)
                def _(c=c, d=d):
                    c.wait_recv()
                    acc[...] += SCR2[self.call, d].astype(F32)

            for c, inside, comes in self.links:

                @pl.when(inside)
                def _(c=c):
                    c.wait_send()

            block = acc[pl.ds(0, 128)]
            k_state = jnp.where(diag, block, 0.0)
            v_state = pltpu.roll(jnp.where(diag, 0.0, block), HEAD, 1)
            return k_state, v_state, jnp.sum(acc[pl.ds(128, 3)], axis=0, keepdims=True)

    def add_to(buf, at, more):
        buf[at] = (buf[at].astype(F32) + more.astype(F32)).astype(BF)

    class Scatter:
        def __init__(self, buf, land, l, x_first, z_second):
            self.buf, self.land, self.l = buf, land, l
            self.x_first, self.z_second = x_first, z_second
            self.first_peer = x_peer if x_first else y_peer
            self.next_peer = y_peer if x_first else x_peer
            self.c = {}

        def block(self, first_other, next_other, zz=every):
            ox, oy = (first_other, next_other) if self.x_first else (next_other, first_other)
            return (self.l, 1 - y if oy else y, zz, 1 - x if ox else x)

        def start(self, o):
            src = self.buf.at[self.block(1, o)]
            self.c[0, o] = send(src, self.land.at[self.l, pl.ds(4 * o, 4)], self.first_peer)

        def add(self, o):
            self.c[0, o].wait_recv()
            add_to(self.buf, self.block(0, o), self.land[self.l, pl.ds(4 * o, 4)])
            if self.z_second:
                self.along_z(o, 7 + 3 * o, 15 + o)
            elif o:
                src = self.buf.at[self.block(0, o)]
                self.next = send(src, self.land.at[self.l, pl.ds(8, 4)], self.next_peer)

        def along_z(self, o, base, extra):
            near, far, through = arrival(), arrival(), arrival()
            self.c[1, o] = (near, far, through, base, extra)
            src = self.buf.at[self.block(0, o, flip_z(1))]
            send(src, self.land.at[self.l, base + 1], z_peer[1], near)
            src = self.buf.at[self.block(0, o, flip_z(3))]
            slot = jnp.where(inner, base + 3, extra)
            peer = (jnp.where(inner, z_peer[3][0], z_peer[1][0]), m)
            first = used[0] - 2
            send(src, self.land.at[self.l, slot], peer, recv_sems.at[jnp.where(inner, first, first + 1)])

        def relay_z(self, o):
            near, far, through, base, extra = self.c[1, o]

            @pl.when(inner)
            def _():
                arrived(self.land.at[self.l, extra], through)
                add_to(self.buf, self.block(0, o, flip_z(2)), self.land[self.l, extra])

            src = self.buf.at[self.block(0, o, flip_z(2))]
            send(src, self.land.at[self.l, base + 2], z_peer[2], near)

        def relay(self):
            for o in (1, 0) if self.z_second else (0,):
                self.relay_z(o)

        def sum_z(self, o):
            near, far, through, base, extra = self.c[1, o]
            at_ = self.block(0, o, z)

            @pl.when(inner)
            def _():
                arrived(self.land.at[self.l, base + 3], far)
                add_to(self.buf, at_, self.land[self.l, base + 3])

            arrived(self.land.at[self.l, pl.ds(base + 1, 2)], near)
            total = self.buf[at_].astype(F32) + self.land[self.l, base + 1].astype(F32)
            return total + self.land[self.l, base + 2].astype(F32)

        def turn(self):
            if self.z_second:
                for o in (1, 0):
                    self.buf[self.block(0, o, z)] = self.sum_z(o).astype(BF)
                    if o:
                        src = self.buf.at[self.block(0, o, z)]
                        self.c[2] = send(src, self.land.at[self.l, 14], self.next_peer)
                return
            self.next.wait_recv()
            for d in (1, 3, 2, 0):
                add_to(self.buf, self.block(0, 0, flip_z(d)), self.land[self.l, 8 + flip_z(d)])
                if d == 3:
                    self.along_z(0, 11, 15)

        def end(self):
            if not self.z_second:
                return self.sum_z(0)
            self.c[2].wait_recv()
            return self.buf[self.block(0, 0, z)].astype(F32) + self.land[self.l, 14].astype(F32)

    finals = []

    def finish(l, name):
        total = scatters[name, l].end()
        if name == UP:
            OUP[l] = total
            finals.append(local(OUP.at[l], gup_hbm.at[l]))
        elif name == DOWN:
            ODN[l] = total
            finals.append(local(ODN.at[l], gdown_hbm.at[l]))
        elif name == OUT:
            OOUT[l] = total
            finals.append(local(OOUT.at[l], gout_hbm.at[l]))
        elif name == Q:
            OQKV[l, 0] = total
            finals.append(local(OQKV.at[l, 0], gqkv_hbm.at[l, 0]))
        elif name == KV:
            OQKV[l, 1] = total[:, :128]
            OQKV[l, 2] = total[:, 128:]
            finals.append(local(OQKV.at[l, pl.ds(1, 2)], gqkv_hbm.at[l, pl.ds(1, 2)]))
        else:
            OCTRL[l] = total
            finals.append(local(OCTRL.at[l], gctrl_hbm.at[l]))

    def split_rows(value):
        return value.astype(BF).reshape(4, 2, R, value.shape[-1])

    def grad_up(l, o):
        yy = 1 - y if o else y
        RUP[l, yy] = split_rows(tn(FB[l], DU[yy]))

    def grad_down(l, o):
        yy = 1 - y if o else y
        RDN[l, yy] = split_rows(tn(GBF[...], GG[l, yy]))

    def grad_out(l):
        grads = tn(GBF[...], OB[l])
        for p in range(2):
            ROUT[l, p] = split_rows(grads[:, p * 128 : (p + 1) * 128])

    scatters = {}
    for l in range(layers):
        for name, buf, land in (
            (Q, RQ, LQ),
            (KV, RKV, LKV),
            (C, RC, LC),
            (OUT, ROUT, LOUT),
            (UP, RUP, LUP),
            (DOWN, RDN, LDN),
        ):
            f = Scatter(buf, land, l, (name, l) in X_FIRST, (name, l) in Z_SECOND)
            scatters[name, l] = f
            jobs[name, l] = {
                START1: functools.partial(f.start, 1),
                START0: functools.partial(f.start, 0),
                ADD1: functools.partial(f.add, 1),
                ADD0: functools.partial(f.add, 0),
                TURN: f.turn,
                RELAY: f.relay,
                END: functools.partial(finish, l, name),
            }
        for name, f in ((UP, grad_up), (DOWN, grad_down)):
            jobs[name, l][GRAD1] = functools.partial(f, l, 1)
            jobs[name, l][GRAD0] = functools.partial(f, l, 0)
        jobs[OUT, l][GRAD1] = functools.partial(grad_out, l)

    tok_copy.wait()
    cot_copy.wait()
    arrived(GAIN.at[pl.ds(1, 7)], gains_here)
    for gz in range(GROUPS // 2):
        total = jnp.zeros((8, 128), F32)
        for d in range(4):
            here = flip_z(d) == gz
            total = total + jnp.where(here, GAIN[2 * d] + GAIN[2 * d + 1], 0.0)
        GFULL[:, pl.ds(gz * 128, 128)] = total

    def gain_row(l, which):
        return GFULL[pl.ds(2 * l + which, 1), :]

    def stream(l, rows):
        return TOKB[0, rows].astype(F32) if l == 0 else H[l - 1, rows]

    def attn_norm(l, i):
        rows = tile_rows(i)
        y_hat, _ = norm_parts(stream(l, rows))
        AB[l, rows] = (y_hat * gain_row(l, 0)).astype(BF)

    for i in range(tiles):
        attn_norm(0, i)

    length = len_ref[y]

    def valid_rows(i):
        row = lax.broadcasted_iota(jnp.int32, (TILE, 1), 0)
        return jnp.where(s * T + i * TILE + row < length, 1.0, 0.0)

    for i in range(tiles):
        rows = tile_rows(i)
        dh = TOKB[1, rows].astype(F32) * valid_rows(i)
        DMID[rows] = dh
        GBF[rows] = dh.astype(BF)

    at(FIRST)

    for l in range(layers):
        more_layers = l + 1 < layers
        at(fwd(l, 0))
        scans = [Scan(2 * l + p, True) for p in range(2)]

        def project_pair(p, l=l):
            out = nn(AB[l], mixer_weight(l, p))
            kv = out[:, 128:384].astype(BF)
            th = jnp.tanh(out[:, 384:] * (1.0 / 16.0))
            w = jnp.exp(16.0 * th).astype(BF)
            sums = [
                (
                    tn(w[j * TILE : (j + 1) * TILE], kv[j * TILE : (j + 1) * TILE]),
                    jnp.sum(w[j * TILE : (j + 1) * TILE].astype(F32), axis=0, keepdims=True),
                )
                for j in range(tiles)
            ]
            ks, vs, zs = 0.0, 0.0, 0.0
            for j, (both, z_j) in enumerate(sums):
                k_j = jnp.where(diag, both[:, :128], 0.0)
                v_j = jnp.where(diag, both[:, 128:], 0.0)
                if j < tiles - 1:
                    LOC[p, j, 0] = k_j
                    LOC[p, j, 1] = v_j
                ks, vs, zs = ks + k_j, vs + v_j, zs + z_j
            QKV[l, p, :, pl.ds(0, 128)] = out[:, :128].astype(BF)
            QKV[l, p, :, pl.ds(128, 256)] = kv
            WB[l, p] = w
            S2[l, p] = (1.0 - th * th).astype(BF)
            return ks, vs, zs

        def inside_block(p, l=l):
            units = range(tiles)
            w = [WB[l, p, tile_rows(j)] for j in units]
            q = [QKV[l, p, tile_rows(j), pl.ds(0, 128)] for j in units]
            k = [QKV[l, p, tile_rows(j), pl.ds(128, 128)] for j in units]
            qs = [heads(q[j]) for j in units]
            a = [[jnp.where(lower, nt(qs[j][h], k[j]), 0.0).astype(BF) for h in (0, 1)] for j in units]
            sums = [nn(lower_ones, w[j]) for j in units]
            ws = [heads(w[j]) for j in units]
            num = [nn(a[j][0], ws[j][0]) + nn(a[j][1], ws[j][1]) for j in units]
            for j in units:
                for h in (0, 1):
                    AST[l, p, j, h] = a[j][h]
                ZS[l, p, tile_rows(j)] = sums[j]
                XS[l, p, tile_rows(j)] = num[j]

        def with_earlier(states, l=l):
            units = [(p, j) for p in range(2) for j in range(tiles)]
            ks, vs, z_before = {}, {}, {}
            for p, j in units:
                if j == 0:
                    k_pre, v_pre, z_pre = states[p]
                else:
                    k_pre = k_pre + LOC[p, j - 1, 0]
                    v_pre = v_pre + LOC[p, j - 1, 1]
                    z_pre = z_pre + jnp.sum(
                        WB[l, p, tile_rows(j - 1)].astype(F32), axis=0, keepdims=True
                    )
                ks[p, j], vs[p, j], z_before[p, j] = k_pre.astype(BF), v_pre.astype(BF), z_pre
            w = {(p, j): WB[l, p, tile_rows(j)] for p, j in units}
            q = {(p, j): QKV[l, p, tile_rows(j), pl.ds(0, 128)] for p, j in units}
            v = {(p, j): QKV[l, p, tile_rows(j), pl.ds(256, 128)] for p, j in units}
            inv = {(p, j): 1.0 / (ZS[l, p, tile_rows(j)] + z_before[p, j]) for p, j in units}
            num = {(p, j): XS[l, p, tile_rows(j)] for p, j in units}
            xs = {u: (num[u] + nt(q[u], ks[u])) * inv[u] * 0.125 for u in units}
            e = {u: jnp.exp(xs[u] - per_head_max(xs[u])) for u in units}
            prob = {u: e[u] / per_head(e[u]) for u in units}
            scaled = {u: (prob[u] * inv[u]).astype(BF) for u in units}
            rs = {u: heads(scaled[u]) for u in units}
            mm = {
                u: [jnp.where(lower, nt(rs[u][h], w[u]), 0.0).astype(BF) for h in (0, 1)]
                for u in units
            }
            vh = {u: heads(v[u]) for u in units}
            out = {
                u: nn(scaled[u], vs[u]) + nn(mm[u][0], vh[u][0]) + nn(mm[u][1], vh[u][1])
                for u in units
            }
            for p, j in units:
                rows = tile_rows(j)
                KP[l, p, j] = ks[p, j]
                VP[l, p, j] = vs[p, j]
                ZS[l, p, rows] = inv[p, j]
                XS[l, p, rows] = xs[p, j]
                PS[l, p, rows] = prob[p, j]
                for h in (0, 1):
                    MST[l, p, j, h] = mm[p, j][h]
                OB[l, rows, pl.ds(p * 128, 128)] = out[p, j].astype(BF)

        for p in range(2):
            scans[p].start(*project_pair(p))
            at(fwd(l, 1 + p))
        for p in range(2):
            inside_block(p)
            at(fwd(l, 3 + 2 * p))
            scans[p].step()
            at(fwd(l, 4 + 2 * p))
        with_earlier([scans[0].end(), scans[1].end()])
        at(fwd(l, 7))

        handles = []
        for i in range(tiles):
            rows = tile_rows(i)
            part = nt(OB[l, rows, pl.ds(0, 128)], out_weight(l, 0))
            part = part + nt(OB[l, rows, pl.ds(128, 128)], out_weight(l, 1))
            handles.append(share_start(part))
        at(fwd(l, 8))
        more = []
        for i in range(tiles):
            rows = tile_rows(i)
            mid = stream(l, rows) + share_end(handles[i])
            y_hat, _ = norm_parts(mid)
            f = (y_hat * gain_row(l, 1)).astype(BF)
            hidden = [nn(f, up_weight(l, p)) for p in range(2)]
            gates = [gate_and_slope(u) for u in hidden]
            low_gates = [gate.astype(BF) for gate, _ in gates]
            if more_layers:
                part = nt(low_gates[0], down_weight(l, 0)) + nt(low_gates[1], down_weight(l, 1))
            else:
                gb = GBF[rows]
                du = [(nn(gb, down_weight(l, p)) * gates[p][1]).astype(BF) for p in range(2)]
                part = nt(du[0], up_weight(l, 0)) + nt(du[1], up_weight(l, 1))
            more.append(share_start(part))
            MID[l, rows] = mid
            FB[l, rows] = f
            for p in range(2):
                GG[l, p, rows] = low_gates[p]
                if more_layers:
                    GU[l, p, rows] = gates[p][1].astype(BF)
                else:
                    DU[p, rows] = du[p]
            at(fwd(l, 9 + i))
        if more_layers:
            for i in range(tiles):
                rows = tile_rows(i)
                H[l, rows] = MID[l, rows] + share_end(more[i])
                attn_norm(l + 1, i)
            at(fwd(l, 11))

    half_rows = pl.ds(pl.multiple_of(core * (T // 2), T // 2), T // 2)

    class Spread:
        def __init__(self, k, out):
            self.k, self.out = k, out

        def start(self):
            src = OUTB.at[self.k, y, half_rows]
            self.c = send(src, src, y_peer)

        def hop(self):
            self.c.wait_recv()
            src = OUTB.at[self.k, 1 - y, half_rows]
            self.c = send(src, src, core_peer)

        def end(self):
            self.c.wait_recv()
            finals.append(local(OUTB.at[self.k], self.out))

    for name, f in ((MIXED, Spread(0, mixed_hbm)), (TOKENS, Spread(1, gt_hbm))):
        jobs[name, 0] = {START: f.start, HOP: f.hop, END: f.end}

    grad_norm = [None] * (2 * layers)

    for l in range(last, -1, -1):
        if l == last:
            at(bwd(l, 0))
            handles = more
        else:
            for i in range(tiles):
                GBF[tile_rows(i)] = DMID[tile_rows(i)].astype(BF)
            at(bwd(l, 0))
            handles = []
            for i in range(tiles):
                rows = tile_rows(i)
                gb = GBF[rows]
                du = [
                    (nn(gb, down_weight(l, p)) * GU[l, p, rows].astype(F32)).astype(BF)
                    for p in range(2)
                ]
                part = nt(du[0], up_weight(l, 0)) + nt(du[1], up_weight(l, 1))
                handles.append(share_start(part))
                for p in range(2):
                    DU[p, rows] = du[p]
        at(bwd(l, 1))
        gsum = jnp.zeros((1, D), F32)
        for i in range(tiles):
            rows = tile_rows(i)
            df = share_end(handles[i])
            y_hat, rstd = norm_parts(MID[l, rows])
            gsum = gsum + jnp.sum(df * y_hat, axis=0, keepdims=True)
            df = df * gain_row(l, 1)
            dm = DMID[rows] + (
                df
                - jnp.mean(df, axis=-1, keepdims=True)
                - y_hat * jnp.mean(df * y_hat, axis=-1, keepdims=True)
            ) * rstd
            DMID[rows] = dm
            GBF[rows] = dm.astype(BF)
            for p in range(2):
                DOB[p, rows] = nn(GBF[rows], out_weight(l, p)).astype(BF)
        grad_norm[2 * l + 1] = gsum
        at(bwd(l, 2))

        scans = [Scan(2 * layers + 2 * (last - l) + k, False) for k in range(2)]
        order = (1 - y, y)

        def to_states(l=l):
            units = [(k, j) for k in range(2) for j in range(tiles - 1, -1, -1)]
            rows = {u: tile_rows(u[1]) for u in units}
            w = {(k, j): WB[l, order[k], rows[k, j]] for k, j in units}
            q = {(k, j): QKV[l, order[k], rows[k, j], pl.ds(0, 128)] for k, j in units}
            v = {(k, j): QKV[l, order[k], rows[k, j], pl.ds(256, 128)] for k, j in units}
            do = {(k, j): DOB[order[k], rows[k, j]] for k, j in units}
            inv = {(k, j): ZS[l, order[k], rows[k, j]] for k, j in units}
            prob = {(k, j): PS[l, order[k], rows[k, j]] for k, j in units}
            xs = {(k, j): XS[l, order[k], rows[k, j]] for k, j in units}
            v_pre = {(k, j): VP[l, order[k], j] for k, j in units}
            ws = {u: heads(w[u]) for u in units}
            dos = {u: heads(do[u]) for u in units}
            pair = {
                u: [jnp.where(lower, nt(dos[u][h], v[u]), 0.0).astype(BF) for h in (0, 1)]
                for u in units
            }
            dr = {
                u: nt(do[u], v_pre[u]) + nn(pair[u][0], ws[u][0]) + nn(pair[u][1], ws[u][1])
                for u in units
            }
            dp = {u: dr[u] * inv[u] for u in units}
            dx = {u: prob[u] * (dp[u] - per_head(dp[u] * prob[u])) for u in units}
            dn = {u: (dx[u] * inv[u] * 0.125).astype(BF) for u in units}
            r = {u: (prob[u] * inv[u]).astype(BF) for u in units}
            dz = {
                u: -(r[u].astype(F32) * dp[u]) - 8.0 * dn[u].astype(F32) * xs[u] for u in units
            }
            dk = {u: jnp.where(diag, tn(dn[u], q[u]), 0.0) for u in units}
            dv = {u: jnp.where(diag, tn(r[u], do[u]), 0.0) for u in units}
            totals = []
            for k in range(2):
                total = [0.0, 0.0, 0.0]
                for j in range(tiles):
                    dzs = jnp.sum(dz[k, j], axis=0, keepdims=True)
                    total = [a + b for a, b in zip(total, (dk[k, j], dv[k, j], dzs))]
                totals.append(total)
            for k, j in units:
                p = order[k]
                for h in (0, 1):
                    YST[p, j, h] = pair[k, j][h]
                DNB[p, rows[k, j]] = dn[k, j]
                DZ[p, rows[k, j]] = dz[k, j]
                if j > 0:
                    LOC[p, j - 1, 0] = dk[k, j]
                    LOC[p, j - 1, 1] = dv[k, j]
            return totals

        def within(p, l=l):
            units = range(tiles)
            rows = [tile_rows(j) for j in units]
            w = [WB[l, p, rows[j]] for j in units]
            q = [QKV[l, p, rows[j], pl.ds(0, 128)] for j in units]
            k = [QKV[l, p, rows[j], pl.ds(128, 128)] for j in units]
            do = [DOB[p, rows[j]] for j in units]
            dn = [DNB[p, rows[j]] for j in units]
            r = [(PS[l, p, rows[j]] * ZS[l, p, rows[j]]).astype(BF) for j in units]
            dz = [DZ[p, rows[j]] for j in units]
            k_pre = [KP[l, p, j] for j in units]
            dz_hi = [dz[j].astype(BF) for j in units]
            dz_lo = [(dz[j] - dz_hi[j].astype(F32)).astype(BF) for j in units]
            dns, rs, dos, qs, ks = ([heads(a[j]) for j in units] for a in (dn, r, do, q, k))
            da = [
                [jnp.where(lower, nt(dns[j][h], w[j]), 0.0).astype(BF) for h in (0, 1)]
                for j in units
            ]
            dq = [
                nn(dn[j], k_pre[j]) + nn(da[j][0], ks[j][0]) + nn(da[j][1], ks[j][1]) for j in units
            ]
            dk = [tn(da[j][0], qs[j][0]) + tn(da[j][1], qs[j][1]) for j in units]
            dv = [
                tn(MST[l, p, j, 0], dos[j][0]) + tn(MST[l, p, j, 1], dos[j][1]) for j in units
            ]
            dw = [
                nn(upper_ones, dz_hi[j])
                + nn(upper_ones, dz_lo[j])
                + tn(YST[p, j, 0], rs[j][0])
                + tn(AST[l, p, j, 0], dns[j][0])
                + tn(YST[p, j, 1], rs[j][1])
                + tn(AST[l, p, j, 1], dns[j][1])
                for j in units
            ]
            for j in units:
                DU[p, rows[j], pl.ds(0, 128)] = dq[j].astype(BF)
                DWF[p, rows[j], pl.ds(0, 128)] = dk[j]
                DWF[p, rows[j], pl.ds(128, 128)] = dv[j]
                DWF[p, rows[j], pl.ds(256, 128)] = dw[j]

        def with_later(k, p, l=l):
            k_post, v_post, z_after = scans[k].end()
            for j in range(tiles - 1, -1, -1):
                rows = tile_rows(j)
                if j < tiles - 1:
                    k_post = k_post + LOC[p, j, 0]
                    v_post = v_post + LOC[p, j, 1]
                    z_after = z_after + jnp.sum(DZ[p, tile_rows(j + 1)], axis=0, keepdims=True)
                kb, vb = k_post.astype(BF), v_post.astype(BF)
                w = WB[l, p, rows]
                key = QKV[l, p, rows, pl.ds(128, 128)]
                v = QKV[l, p, rows, pl.ds(256, 128)]
                dk = DWF[p, rows, pl.ds(0, 128)] + nn(w, kb)
                dv = DWF[p, rows, pl.ds(128, 128)] + nn(w, vb)
                dw = DWF[p, rows, pl.ds(256, 128)] + nt(key, kb) + nt(v, vb) + z_after
                dc = dw * w.astype(F32) * S2[l, p, rows].astype(F32)
                DU[p, rows, pl.ds(128, 128)] = dk.astype(BF)
                DU[p, rows, pl.ds(256, 128)] = dv.astype(BF)
                DU[p, rows, pl.ds(384, 128)] = dc.astype(BF)

        totals = to_states()
        for k in range(2):
            scans[k].start(*totals[k])
        if l == last:
            outs = []
            for i in range(tiles):
                rows = tile_rows(i)
                part = nt(GG[l, 0, rows], down_weight(l, 0)) + nt(GG[l, 1, rows], down_weight(l, 1))
                outs.append(share_start(part))
        at(bwd(l, 3))
        for k in range(2):
            scans[k].step()
            at(bwd(l, 4 + k))
        for k in range(2):
            p = order[k]
            within(p)
            RQ[l, p] = split_rows(tn(AB[l], DU[p, :, pl.ds(0, 128)]))
            if l == last and k == 0:
                for i in range(tiles):
                    rows = tile_rows(i)
                    out = MID[l, rows] + share_end(outs[i])
                    OUTB[0, y, rows] = (out * valid_rows(i)).astype(BF)
            at(bwd(l, 6 + k))
        for k in range(2):
            p = order[k]
            with_later(k, p)
            grads = split_rows(tn(AB[l], DU[p, :, pl.ds(128, 384)]))
            RKV[l, p] = grads[..., :256]
            RC[l, p] = grads[..., 256:]
            at(bwd(l, 8 + k))
        handles = []
        for i in range(tiles):
            rows = tile_rows(i)
            part = nt(DU[0, rows], mixer_weight(l, 0))
            part = part + nt(DU[1, rows], mixer_weight(l, 1))
            handles.append(share_start(part))
        at(bwd(l, 10))
        gsum = jnp.zeros((1, D), F32)
        for i in range(tiles):
            rows = tile_rows(i)
            da = share_end(handles[i])
            y_hat, rstd = norm_parts(stream(l, rows))
            gsum = gsum + jnp.sum(da * y_hat, axis=0, keepdims=True)
            da = da * gain_row(l, 0)
            dh = DMID[rows] + (
                da
                - jnp.mean(da, axis=-1, keepdims=True)
                - y_hat * jnp.mean(da * y_hat, axis=-1, keepdims=True)
            ) * rstd
            DMID[rows] = dh
            if l == 0:
                OUTB[1, y, rows] = dh.astype(BF)
        grad_norm[2 * l] = gsum
        at(bwd(l, 11))

    class Gains:
        def start(self):
            sub = lax.broadcasted_iota(jnp.int32, (8, D), 0)
            self.rows = jnp.zeros((8, D), F32)
            for k in range(2 * layers):
                self.rows = jnp.where(sub == k, grad_norm[k], self.rows)
            GN[...] = self.rows
            self.c = send(GN, GNY, y_peer)

        def hop(self):
            self.c.wait_recv()
            both = self.rows + GNY[...]
            for gz in range(GROUPS // 2):
                GNR[0, gz] = both[:, gz * 128 : (gz + 1) * 128]
            self.c = arrival()
            for d in range(4):
                for o in range(2):
                    if (d, o) == (0, 0):
                        continue
                    peer = (seq_of(1 - x if o else x, flip_z(d)), m)
                    k = 2 * d + o
                    send(GNR.at[0, flip_z(d)], GNR.at[1, k], peer, self.c)

        def end(self):
            total = GNR[0, z]
            arrived(GNR.at[1, pl.ds(1, 7)], self.c)
            for k in range(1, 8):
                total = total + GNR[1, k]
            GNO[...] = total
            finals.append(local(GNO, gn_hbm))

    f = Gains()
    jobs[GAINS, 0] = {START: f.start, HOP: f.hop, END: f.end}
    at(TAIL)
    for c in finals:
        c.wait()
    for c in (*leaving.values(), *share_prev.values()):
        c.wait_send()
    for c in inner_last:

        @pl.when(inner)
        def _(c=c):
            c.wait_send()

    assert used[0] == recv_sems.shape[0] and used[1] == local_sems.shape[0], used
    assert inner_used[0] == inner_sems.shape[0], inner_used


def lay_out(stride, *refs):
    mixed, tokens, qkv, ctrl, out, up, down, gains = refs[:8]
    mixed_out, tokens_out, attn_out, ffn_out, *weights_out = refs[8:17]
    wide, sems, *held = refs[17:]
    arrays = (tokens, mixed, up, down, qkv, ctrl, out)
    results = (None, mixed_out, weights_out[3], weights_out[4], *weights_out[:3])
    parts = [(k, b) for k in range(len(arrays)) for b in range(2)]
    ins = {
        (k, b): pltpu.make_async_copy(arrays[k].at[b], held[k].at[b], sems.at[0, k, b])
        for k, b in parts
    }
    for c in ins.values():
        c.start()
    x = (lax.axis_index("seq") // stride) % 2
    R = attn_out.shape[1]
    rows = jnp.where(x == 0, gains[:, pl.ds(0, R)], gains[:, pl.ds(R, R)])
    for l in range(attn_out.shape[0]):
        attn_out[pl.ds(l, 1), :] = rows[2 * l : 2 * l + 1]
        ffn_out[pl.ds(l, 1), :] = rows[2 * l + 1 : 2 * l + 2]
    outs = []
    for k, b in parts:
        ins[k, b].wait()
        if k == 0:
            wide[b] = held[0][b].astype(F32)
            c = pltpu.make_async_copy(wide.at[b], tokens_out.at[b], sems.at[1, k, b])
        else:
            c = pltpu.make_async_copy(held[k].at[b], results[k].at[b], sems.at[1, k, b])
        c.start()
        outs.append(c)
    for c in outs:
        c.wait()


def shards(tokens, lengths, norm_attn, norm_ffn, w_qkv, w_ctrl, w_out, w_up, w_down, cotangent):
    layers = w_qkv.shape[0]
    n_seq = lax.axis_size("seq")
    stride = n_seq // GROUPS
    _, T, D = tokens.shape
    rows = w_qkv.shape[1]
    weights = [w_qkv.transpose(0, 2, 1, 3), w_ctrl, w_up, w_down, w_out]
    gains = [norm_attn, norm_ffn]
    blocks = [[k * stride + j for j in range(stride)] for k in range(GROUPS)]
    if stride > 1:

        def fill(a, dim=1):
            return lax.all_gather(a, "seq", axis=dim, tiled=True, axis_index_groups=blocks)

        weights = [fill(a, a.ndim - 2) for a in weights]
        gains = [fill(a) for a in gains]
    R = D // GROUPS
    A = 3 * w_qkv.shape[-1] + w_ctrl.shape[-1]
    U = w_up.shape[-1]
    F = 2 * U + w_out.shape[-1]
    near = near_size(n_seq)
    far = n_seq // near
    tiles = T // TILE
    arrivals = 1 + sum(19 if (n, l) in GATHER_Z_SECOND else 13 for n in range(3) for l in range(layers))
    arrivals += 2 * tiles + 4 * layers * (near + far - 2)
    arrivals += sum(9 if (n, l) in Z_SECOND else 6 for n in range(Q, DOWN + 1) for l in range(layers))
    inner_copies = sum(3 if (n, l) in GATHER_Z_SECOND else 1 for n in range(3) for l in range(layers))
    arrivals += 4 + 2
    bf, f32 = BF, F32
    v = pltpu.VMEM
    scratch = [
        v((max(layers - 1, 1), T, D), f32),
        v((layers, T, D), f32),
        v((layers, T, D), bf),
        v((layers, T, D), bf),
        v((layers, 2, T, 384), bf),
        v((layers, 2, T, 128), bf),
        v((layers, 2, T, 128), bf),
        v((layers, 2, T, 128), f32),
        v((layers, 2, T, 128), f32),
        v((layers, 2, T, 128), f32),
        v((layers, 2, tiles, 2, TILE, TILE), bf),
        v((layers, 2, tiles, 2, TILE, TILE), bf),
        v((layers, T, 256), bf),
        v((max(layers - 1, 1), 2, T, U), bf),
        v((layers, 2, T, U), bf),
        v((layers, 2, tiles, 128, 128), bf),
        v((layers, 2, tiles, 128, 128), bf),
        v((2, max(tiles - 1, 1), 2, 128, 128), f32),
        v((2, T, D), bf),
        v((T, D), bf),
        v((2, T, 128), bf),
        v((2, T, U), bf),
        v((T, D), f32),
        v((2, tiles, 2, TILE, TILE), bf),
        v((2, T, 128), bf),
        v((2, T, 128), f32),
        v((2, T, 384), f32),
        v((layers, 2, 4, 2, R, A), bf),
        v((layers, 2, 4, 2, R, F), bf),
        v((8, 8, 128), f32),
        v((2, layers, R), bf),
        v((8, D), f32),
        v((tiles, TILE, D), bf),
        v((2 * tiles, TILE, D), bf),
        v((4 * layers, 144, 128), bf),
        v((4 * layers, near - 1, 144, 128), bf),
        v((4 * layers, far - 1, 144, 128), bf),
        v((2, 144, 128), f32),
        v((layers, 2, 4, 2, R, 128), bf),
        v((layers, 2, 4, 2, R, 256), bf),
        v((layers, 2, 4, 2, R, 128), bf),
        v((layers, 2, 4, 2, R, 128), bf),
        v((layers, 2, 4, 2, R, U), bf),
        v((layers, 2, 4, 2, R, U), bf),
        v((layers, 17, R, 128), bf),
        v((layers, 17, R, 256), bf),
        v((layers, 17, R, 128), bf),
        v((layers, 17, R, 128), bf),
        v((layers, 17, R, U), bf),
        v((layers, 17, R, U), bf),
        v((layers, 3, R, 128), f32),
        v((layers, R, 128), f32),
        v((layers, R, 128), f32),
        v((layers, R, U), f32),
        v((layers, R, U), f32),
        v((8, D), f32),
        v((8, D), f32),
        v((2, 8, 8, 128), f32),
        v((8, 128), f32),
        v((2, 2, T, D), bf),
        pltpu.SemaphoreType.DMA((SEND_RING + tiles + 2 * (far - 1),)),
        pltpu.SemaphoreType.DMA((inner_copies,)),
        pltpu.SemaphoreType.DMA((arrivals,)),
        pltpu.SemaphoreType.DMA((7 + 13 * layers,)),
    ]
    any_spec = pl.BlockSpec(memory_space=pl.ANY)
    out_shape = (
        jax.ShapeDtypeStruct((2, T, D), bf),
        jax.ShapeDtypeStruct((2, T, D), bf),
        jax.ShapeDtypeStruct((layers, 3, R, 128), f32),
        jax.ShapeDtypeStruct((layers, R, 128), f32),
        jax.ShapeDtypeStruct((layers, R, 128), f32),
        jax.ShapeDtypeStruct((layers, R, U), f32),
        jax.ShapeDtypeStruct((layers, R, U), f32),
        jax.ShapeDtypeStruct((8, 128), f32),
    )
    mixed, grad_tokens, *grads, gn = pl.pallas_call(
        functools.partial(kernel, n_seq, layers),
        out_shape=out_shape,
        in_specs=[
            any_spec,
            any_spec,
            pl.BlockSpec(memory_space=pltpu.SMEM),
            *[any_spec] * 7,
        ],
        out_specs=(any_spec,) * len(out_shape),
        scratch_shapes=scratch,
        compiler_params=pltpu.CompilerParams(
            collective_id=0, has_side_effects=True, vmem_limit_bytes=VMEM_BYTES
        ),
    )(tokens, cotangent, lengths, *weights, *gains)
    out_shape = (
        jax.ShapeDtypeStruct((2, T, D), bf),
        jax.ShapeDtypeStruct((2, T, D), f32),
        jax.ShapeDtypeStruct((layers, R), f32),
        jax.ShapeDtypeStruct((layers, R), f32),
        *[jax.ShapeDtypeStruct(a.shape, f32) for a in grads],
    )
    vmem_spec = pl.BlockSpec(memory_space=pltpu.VMEM)
    mixed, grad_tokens, *grads = pl.pallas_call(
        functools.partial(lay_out, stride),
        out_shape=out_shape,
        in_specs=[any_spec] * 7 + [vmem_spec],
        out_specs=(any_spec, any_spec, vmem_spec, vmem_spec) + (any_spec,) * 5,
        scratch_shapes=[
            v((2, T, D), f32),
            pltpu.SemaphoreType.DMA((2, 7, 2)),
            *[v(a.shape, a.dtype) for a in (grad_tokens, mixed, *grads[3:], *grads[:3])],
        ],
        compiler_params=pltpu.CompilerParams(vmem_limit_bytes=VMEM_BYTES),
    )(mixed, grad_tokens, *grads, gn)
    if stride > 1:

        def empty(a):
            return lax.psum_scatter(
                a, "seq", scatter_dimension=max(a.ndim - 2, 1), tiled=True, axis_index_groups=blocks
            )

        grads = [empty(a) for a in grads]
    grads[2] = grads[2].transpose(0, 2, 1, 3)
    return (mixed, grad_tokens, *grads)


VMEM_BYTES = 62 << 20


def solution(mesh):
    in_specs = (
        P(None, "seq", None),
        P(),
        P(None, "seq"),
        P(None, "seq"),
        P(None, "seq", None, "mp"),
        P(None, "seq", "mp"),
        P(None, "seq", "mp"),
        P(None, "seq", "mp"),
        P(None, "seq", "mp"),
        P(None, "seq", None),
    )
    out_specs = (
        P(None, "seq", None),
        P(None, "seq", None),
        P(None, "seq"),
        P(None, "seq"),
        P(None, "seq", None, "mp"),
        P(None, "seq", "mp"),
        P(None, "seq", "mp"),
        P(None, "seq", "mp"),
        P(None, "seq", "mp"),
    )
    return jax.shard_map(shards, mesh=mesh, in_specs=in_specs, out_specs=out_specs, check_vma=False)
```

```python
import functools

import jax
import jax.numpy as jnp
from jax import lax
from jax.experimental import pallas as pl
from jax.experimental.pallas import tpu as pltpu
from jax.sharding import PartitionSpec as P

F32 = jnp.float32
BF = jnp.bfloat16
MESH = pl.DeviceIdType.MESH
GROUPS = 8
HEAD = 64
EPS = 1e-05
TILE = 256


def nn(a, b):
    return lax.dot_general(a, b, (((1,), (0,)), ((), ())), preferred_element_type=F32)


def nt(a, b):
    return lax.dot_general(a, b, (((1,), (1,)), ((), ())), preferred_element_type=F32)


def tn(a, b):
    return lax.dot_general(a, b, (((0,), (0,)), ((), ())), preferred_element_type=F32)


def near_size(n_seq):
    return 1 << ((n_seq.bit_length() - 1) // 2)


def norm_parts(x):
    center = x - jnp.mean(x, axis=-1, keepdims=True)
    spread = jnp.mean(center * center, axis=-1, keepdims=True)
    rstd = lax.rsqrt(spread + EPS)
    return center * rstd, rstd


def gate_and_slope(u):
    u2 = u * u
    t = jnp.tanh(u * (0.7978845608 + (0.7978845608 * 0.044715) * u2))
    half = 0.5 + 0.5 * t
    gate = u * half
    slope = half + gate * (1.0 - half) * (1.5957691216 + (1.5957691216 * 0.134145) * u2)
    return gate, slope


MIXER, UPPER, LOWER, Q, KV, C, OUT, UP, DOWN, MIXED, TOKENS, GAINS = range(12)
START, OWN, ON1, ON2, ON3, ACROSS0, ACROSS1, ACROSS2, ACROSS3, END = range(10)
GRAD1, GRAD0, START1, START0, ADD1, ADD0, TURN, HOP, RELAY = range(10, 19)


def fwd(layer, k):
    return 100 + 20 * layer + k


def bwd(layer, k):
    return 200 + 20 * layer + k


ENTRY, FIRST, TAIL = 0, 1, 2
SEND_RING = 48

X_FIRST = {(Q, 1), (KV, 0), (C, 0), (OUT, 0), (OUT, 1), (DOWN, 0), (DOWN, 1)}
Z_SECOND = {(KV, 1), (DOWN, 1)}
GATHER_Z_SECOND = {(UPPER, 0), (LOWER, 1)}
PLAN = {
    ENTRY: (
        (MIXER, 1, OWN),
        (LOWER, 0, OWN),
        (MIXER, 0, START),
        (MIXER, 0, OWN),
        (MIXER, 0, ON1),
        (UPPER, 0, START),
        (MIXER, 0, ON2),
        (LOWER, 0, START),
        (UPPER, 0, OWN),
        (MIXER, 0, ACROSS0),
        (MIXER, 0, ON3),
        (MIXER, 0, ACROSS1),
        (UPPER, 0, ON1),
        (UPPER, 0, ON2),
        (MIXER, 0, ACROSS2),
    ),
    FIRST: (
        (LOWER, 1, OWN),
        (MIXER, 0, ACROSS3),
        (LOWER, 0, ON2),
        (MIXER, 0, END),
    ),
    fwd(0, 0): (
        (MIXER, 1, START),
        (LOWER, 0, ON3),
    ),
    fwd(0, 1): (
        (LOWER, 0, ON1),
        (UPPER, 0, ON3),
        (UPPER, 0, ACROSS1),
    ),
    fwd(0, 2): (
        (UPPER, 0, ACROSS0),
    ),
    fwd(0, 3): (
        (UPPER, 0, ACROSS2),
        (LOWER, 0, ACROSS3),
    ),
    fwd(0, 4): (
        (UPPER, 0, ACROSS3),
    ),
    fwd(0, 5): (
        (LOWER, 0, ACROSS2),
        (MIXER, 1, ON1),
    ),
    fwd(0, 6): (
        (LOWER, 0, ACROSS0),
        (LOWER, 0, ACROSS1),
        (LOWER, 1, ON3),
        (UPPER, 1, START),
        (MIXER, 1, ON2),
    ),
    fwd(0, 7): (
        (UPPER, 0, END),
        (LOWER, 1, START),
        (MIXER, 1, ON3),
        (LOWER, 0, END),
        (LOWER, 1, ON1),
        (LOWER, 1, ON2),
    ),
    fwd(0, 8): (
        (MIXER, 1, ACROSS1),
        (MIXER, 1, ACROSS2),
    ),
    fwd(0, 9): (
        (LOWER, 1, ACROSS0),
        (MIXER, 1, ACROSS3),
        (MIXER, 1, ACROSS0),
    ),
    fwd(0, 10): (
        (UPPER, 1, ON1),
        (UPPER, 1, ON2),
    ),
    fwd(0, 11): (
        (MIXER, 1, END),
    ),
    fwd(1, 1): (
        (UPPER, 1, ON3),
    ),
    fwd(1, 3): (
        (UPPER, 1, ACROSS1),
        (LOWER, 1, ACROSS2),
        (LOWER, 1, ACROSS1),
    ),
    fwd(1, 6): (
        (UPPER, 1, OWN),
        (LOWER, 1, ACROSS3),
        (UPPER, 1, ACROSS3),
        (UPPER, 1, ACROSS0),
        (UPPER, 1, ACROSS2),
    ),
    fwd(1, 7): (
        (LOWER, 1, END),
    ),
    fwd(1, 8): (
        (UPPER, 1, END),
    ),
    fwd(1, 10): (
        (DOWN, 1, GRAD1),
        (DOWN, 1, START1),
    ),
    bwd(1, 1): (
        (UP, 1, GRAD1),
        (UP, 1, START1),
        (DOWN, 1, GRAD0),
        (UP, 1, START0),
    ),
    bwd(1, 3): (
        (DOWN, 1, START0),
    ),
    bwd(1, 5): (
        (OUT, 1, GRAD1),
        (UP, 1, GRAD0),
    ),
    bwd(1, 6): (
        (MIXED, 0, START),
        (OUT, 1, START1),
    ),
    bwd(1, 7): (
        (Q, 1, START1),
    ),
    bwd(1, 8): (
        (UP, 1, ADD1),
        (UP, 1, ADD0),
    ),
    bwd(1, 10): (
        (Q, 1, START0),
        (DOWN, 1, ADD0),
        (KV, 1, START1),
        (KV, 1, START0),
    ),
    bwd(1, 11): (
        (Q, 1, ADD1),
        (DOWN, 1, ADD1),
        (C, 1, START0),
    ),
    bwd(0, 0): (
        (OUT, 1, ADD1),
        (DOWN, 0, GRAD1),
        (DOWN, 0, START1),
        (C, 1, START1),
        (DOWN, 0, GRAD0),
    ),
    bwd(0, 1): (
        (UP, 0, GRAD1),
        (UP, 1, TURN),
    ),
    bwd(0, 2): (
        (OUT, 0, GRAD1),
        (UP, 0, GRAD0),
        (DOWN, 1, RELAY),
        (KV, 1, ADD1),
        (KV, 1, ADD0),
        (UP, 0, START1),
        (OUT, 1, START0),
    ),
    bwd(0, 3): (
        (DOWN, 0, ADD1),
        (OUT, 0, START0),
        (C, 1, ADD0),
        (Q, 1, ADD0),
    ),
    bwd(0, 4): (
        (OUT, 1, ADD0),
        (UP, 0, START0),
        (C, 1, ADD1),
        (DOWN, 0, START0),
    ),
    bwd(0, 5): (
        (UP, 1, RELAY),
        (KV, 1, RELAY),
        (OUT, 1, TURN),
    ),
    bwd(0, 6): (
        (Q, 1, TURN),
        (OUT, 0, START1),
    ),
    bwd(0, 7): (
        (Q, 0, START1),
        (UP, 0, ADD1),
        (C, 1, TURN),
        (Q, 0, START0),
    ),
    bwd(0, 8): (
        (DOWN, 0, ADD0),
        (DOWN, 0, TURN),
        (KV, 0, START1),
    ),
    bwd(0, 9): (
        (C, 0, START1),
        (OUT, 1, RELAY),
        (Q, 1, RELAY),
        (DOWN, 0, RELAY),
        (KV, 0, START0),
        (OUT, 0, ADD1),
        (OUT, 0, ADD0),
        (UP, 0, ADD0),
        (MIXED, 0, HOP),
        (UP, 0, TURN),
    ),
    bwd(0, 10): (
        (KV, 0, ADD1),
        (C, 1, RELAY),
        (UP, 1, END),
        (OUT, 0, TURN),
        (C, 0, ADD1),
        (Q, 0, ADD1),
    ),
    bwd(0, 11): (
        (UP, 0, RELAY),
        (KV, 1, TURN),
    ),
    TAIL: (
        (GAINS, 0, START),
        (TOKENS, 0, START),
        (DOWN, 0, END),
        (OUT, 0, RELAY),
        (C, 0, START0),
        (KV, 0, ADD0),
        (Q, 0, ADD0),
        (KV, 0, TURN),
        (Q, 0, TURN),
        (KV, 1, END),
        (MIXED, 0, END),
        (KV, 0, RELAY),
        (Q, 1, END),
        (C, 0, ADD0),
        (C, 0, TURN),
        (GAINS, 0, HOP),
        (DOWN, 1, TURN),
        (Q, 0, RELAY),
        (C, 1, END),
        (UP, 0, END),
        (OUT, 0, END),
        (OUT, 1, END),
        (C, 0, RELAY),
        (TOKENS, 0, HOP),
        (GAINS, 0, END),
        (KV, 0, END),
        (Q, 0, END),
        (DOWN, 1, END),
        (C, 0, END),
        (TOKENS, 0, END),
    ),
}


def kernel(
    n_seq,
    layers,
    tok_hbm,
    cot_hbm,
    len_ref,
    qkv_hbm,
    ctrl_hbm,
    up_hbm,
    down_hbm,
    out_hbm,
    norm_attn_hbm,
    norm_ffn_hbm,
    mixed_hbm,
    gt_hbm,
    gqkv_hbm,
    gctrl_hbm,
    gout_hbm,
    gup_hbm,
    gdown_hbm,
    gn_hbm,
    H,
    MID,
    AB,
    FB,
    QKV,
    WB,
    S2,
    ZS,
    PS,
    XS,
    AST,
    MST,
    OB,
    GU,
    GG,
    KP,
    VP,
    LOC,
    TOKB,
    GBF,
    DOB,
    DU,
    DMID,
    YST,
    DNB,
    DZ,
    DWF,
    WA,
    WF,
    GAIN,
    GROW,
    GFULL,
    ARS,
    ARR,
    SCS,
    SCR1,
    SCR2,
    SCP,
    RQ,
    RKV,
    RC,
    ROUT,
    RUP,
    RDN,
    LQ,
    LKV,
    LC,
    LOUT,
    LUP,
    LDN,
    OQKV,
    OCTRL,
    OOUT,
    OUP,
    ODN,
    GN,
    GNY,
    GNR,
    GNO,
    OUTB,
    send_sems,
    inner_sems,
    recv_sems,
    local_sems,
):
    T, D = TOKB.shape[1], TOKB.shape[2]
    tiles = T // TILE
    R = D // GROUPS
    stride = n_seq // GROUPS
    s = lax.axis_index("seq")
    m = lax.axis_index("mp")
    y, core = m // 2, m % 2
    g, lo = s // stride, s % stride
    x, z = g % 2, g // 2
    z1, z0 = z // 2, z % 2
    inner = z1 != z0
    last = layers - 1

    def flip_z(d):
        d1, d0 = d // 2, d % 2
        return 2 * (1 - z1 if d1 else z1) + (1 - z0 if d0 else z0)

    def seq_of(gx, gz):
        return (gz * 2 + gx) * stride + lo

    core_peer = (s, 2 * y + (1 - core))
    y_peer = (s, 2 * (1 - y) + core)
    x_peer = (seq_of(1 - x, z), m)
    z_peer = {d: (seq_of(x, flip_z(d)), m) for d in (1, 2, 3)}
    near = near_size(n_seq)
    blocks = n_seq // near
    low, high = s % near, s // near

    used = [0, 0, 0]
    leaving = {}

    def arrival():
        used[0] += 1
        return recv_sems.at[used[0] - 1]

    def remote(src, dst, peer, leave, arrive):
        return pltpu.make_async_remote_copy(
            src_ref=src,
            dst_ref=dst,
            send_sem=leave,
            recv_sem=arrive,
            device_id=peer,
            device_id_type=MESH,
        )

    def send(src, dst, peer, arrive=None):
        k = used[2] % SEND_RING
        used[2] += 1
        if k in leaving:
            leaving[k].wait_send()
        c = remote(src, dst, peer, send_sems.at[k], arrival() if arrive is None else arrive)
        c.start()
        leaving[k] = c
        return c

    def send_if_inner(src, dst, peer, arrive, leave):
        c = remote(src, dst, peer, leave, arrive)

        @pl.when(inner)
        def _():
            c.start()

        return c

    def leave_done(c):
        for k, other in list(leaving.items()):
            if other is c:
                c.wait_send()
                del leaving[k]

    def arrived(region, arrive):
        remote(region, region, core_peer, send_sems.at[0], arrive).wait_recv()

    def local(src, dst):
        k = used[1]
        used[1] += 1
        c = pltpu.make_async_copy(src, dst, local_sems.at[k])
        c.start()
        return c

    barrier = pltpu.get_barrier_semaphore()

    def hello(peer):
        pl.semaphore_signal(barrier, inc=1, device_id=peer, device_id_type=MESH)

    hello(core_peer)
    hello(y_peer)
    count = 2
    for d in range(1, near):
        hello((high * near + lax.rem(low + d, near), m))
        count += 1
    for d in range(1, blocks):
        other = lax.rem(high + d, blocks) * near
        hello((other + low, m))
        count += 1
        if stride == 1:
            hello((other + 1 - low, m))
            count += 1

    rows_in = [local(norm_attn_hbm, GROW.at[0]), local(norm_ffn_hbm, GROW.at[1])]
    own = []
    for l in range(layers):
        for k in range(4):
            src = qkv_hbm.at[l, k] if k < 3 else ctrl_hbm.at[l]
            own.append(local(src, WA.at[l, y, z, x, slice(None), pl.ds(k * 128, 128)]))
        lanes = 0
        for src in (up_hbm, down_hbm, out_hbm):
            at = pl.ds(lanes, src.shape[-1])
            own.append(local(src.at[l], WF.at[l, y, z, x, slice(None), at]))
            lanes += src.shape[-1]
    tok_copy = local(tok_hbm.at[y], TOKB.at[0])
    cot_copy = local(cot_hbm.at[y], TOKB.at[1])
    gain_sub = lax.broadcasted_iota(jnp.int32, (8, R), 0)
    own_gains = jnp.zeros((8, R), F32)
    for c in rows_in:
        c.wait()
    for l in range(layers):
        for k in range(2):
            row = GROW[k].astype(F32)[l : l + 1]
            own_gains = jnp.where(gain_sub == 2 * l + k, row, own_gains)
    GAIN[0, :, pl.ds(0, R)] = jnp.where(x == 0, own_gains, 0.0)
    GAIN[0, :, pl.ds(R, R)] = jnp.where(x == 0, 0.0, own_gains)

    pl.semaphore_wait(barrier, count)

    every = slice(None)

    inner_used = [0]
    inner_last = []

    def inner_leave():
        inner_used[0] += 1
        return inner_sems.at[inner_used[0] - 1]

    class Gather:
        def __init__(self, buf, l, low_end, cut, high_end, z_second):
            self.buf, self.l, self.c = buf, l, {}
            self.all = pl.ds(low_end, high_end - low_end)
            self.first, self.second = pl.ds(low_end, cut - low_end), pl.ds(cut, high_end - cut)
            self.z_second = z_second
            self.last = None
            self.inner = {}

        def along_z(self, kind, region, lanes=None):
            for d in (1, 2):
                self.push((kind, d), region, z_peer[d], lanes)
            src = self.buf.at[(self.l,) + region + (slice(None), lanes or self.all)]
            arrive, leave = arrival(), inner_leave()
            self.c[kind, 3] = send_if_inner(src, src, z_peer[3], arrive, leave)
            self.inner[kind] = (self.c[kind, 3], arrive, leave)

        def pass_on(self, kind, region, lanes=None):
            before, arrive, leave = self.inner[kind]

            @pl.when(inner)
            def _():
                before.wait_send()

            src = self.buf.at[(self.l,) + region + (slice(None), lanes or self.all)]
            inner_last.append(send_if_inner(src, src, z_peer[1], arrive, leave))

        def push(self, key, region, peer, lanes=None):
            src = self.buf.at[(self.l,) + region + (slice(None), lanes or self.all)]
            arrive = None
            if key[0] in (5, 6) and not self.z_second:
                self.last = self.last or {5: arrival(), 6: arrival()}
                arrive = self.last[key[0]]
            self.c[key] = send(src, src, peer, arrive)

        def take(self, *keys):
            for key in keys:
                self.c[key].wait_recv()

        def start(self):
            self.along_z(0, (y, z, x))

        def own(self):
            self.push((1, 0), (y, z, x), x_peer)
            self.push((2, 0), (y, z, x), y_peer)

        def on(self, d):
            if not self.z_second:
                self.take((0, d))
                if d == 2:
                    self.pass_on(0, (y, flip_z(d), x))
                self.push((1, d), (y, flip_z(d), x), x_peer)
                self.push((2, d), (y, flip_z(d), x), y_peer)
            elif d == 1:
                self.take((1, 0))
                self.along_z(3, (y, z, 1 - x), self.first)
                self.push((5, 0), (y, z, 1 - x), y_peer, self.first)
            elif d == 2:
                self.take((2, 0))
                self.along_z(4, (1 - y, z, x), self.second)
                self.push((6, 0), (1 - y, z, x), x_peer, self.second)

        def across(self, d):
            zz = flip_z(d)
            if not self.z_second:
                self.take((1, d))
                self.push((5, d), (y, zz, 1 - x), y_peer, self.first)
                self.take((2, d))
                self.push((6, d), (1 - y, zz, x), x_peer, self.second)
            elif d:
                self.take((0, d), (3, d))
                if d == 2:
                    self.pass_on(0, (y, zz, x))
                    self.pass_on(3, (y, zz, 1 - x), self.first)
                self.push((5, d), (y, zz, slice(None)), y_peer, self.first)
                self.take((4, d))
                if d == 2:
                    self.pass_on(4, (1 - y, zz, x), self.second)
                self.push((6, d), (slice(None), zz, x), x_peer, self.second)

        def end(self):
            if self.z_second:
                for d in range(4):
                    self.take((5, d), (6, d))
                return
            far = self.buf.at[self.l, 1 - y, every, 1 - x]
            arrived(far.at[:, :, self.first], self.last[5])
            arrived(far.at[:, :, self.second], self.last[6])

        def parts(self):
            part = {START: self.start, OWN: self.own, END: self.end}
            for d in (1, 2, 3):
                part[ON1 + d - 1] = functools.partial(self.on, d)
            for d in range(4):
                part[ACROSS0 + d] = functools.partial(self.across, d)
            return part

    gains_here = arrival()
    for d in (0, 1, 2, 3):
        for o in (0, 1):
            if (d, o) == (0, 0):
                continue
            peer = (seq_of(1 - x if o else x, flip_z(d)), m)
            send(GAIN.at[0], GAIN.at[d * 2 + o], peer, gains_here)
    for c in own:
        c.wait()
    jobs = {}
    for l in range(layers):
        for name, buf, bounds in (
            (MIXER, WA, (0, 256, 512)),
            (UPPER, WF, (0, 256, 512)),
            (LOWER, WF, (512, 896, 1152)),
        ):
            jobs[name, l] = Gather(buf, l, *bounds, (name, l) in GATHER_Z_SECOND).parts()

    def at(place):
        for name, l, part in PLAN.get(place, ()):
            jobs[name, l][part]()

    at(ENTRY)

    lane = lax.broadcasted_iota(jnp.int32, (TILE, 128), 1)
    first = lane < HEAD
    head_rows = [
        (lax.broadcasted_iota(jnp.int32, (1, 128), 1) < HEAD).astype(F32).astype(BF),
        (lax.broadcasted_iota(jnp.int32, (1, 128), 1) >= HEAD).astype(F32).astype(BF),
    ]
    rr = lax.broadcasted_iota(jnp.int32, (TILE, TILE), 0)
    cc = lax.broadcasted_iota(jnp.int32, (TILE, TILE), 1)
    lower = rr >= cc
    lower_ones = lower.astype(F32).astype(BF)
    upper_ones = (rr <= cc).astype(F32).astype(BF)
    diag = (lax.broadcasted_iota(jnp.int32, (128, 128), 0) < HEAD) == (
        lax.broadcasted_iota(jnp.int32, (128, 128), 1) < HEAD
    )

    def per_head(value):
        a = jnp.sum(jnp.where(first, value, 0.0), axis=-1, keepdims=True)
        b = jnp.sum(jnp.where(first, 0.0, value), axis=-1, keepdims=True)
        return jnp.where(first, a, b)

    def per_head_max(value):
        a = jnp.max(jnp.where(first, value, -jnp.inf), axis=-1, keepdims=True)
        b = jnp.max(jnp.where(first, -jnp.inf, value), axis=-1, keepdims=True)
        return jnp.where(first, a, b)

    def heads(value):
        return value * head_rows[0], value * head_rows[1]

    def tile_rows(i):
        return pl.ds(i * TILE, TILE)

    def weight(buf, l, p, start, width):
        return buf[l, p, :, :, :, pl.ds(start, width)].reshape(D, width)

    def mixer_weight(l, p):
        return weight(WA, l, p, 0, 512)

    def up_weight(l, p):
        return weight(WF, l, p, 0, 512)

    def down_weight(l, p):
        return weight(WF, l, p, 512, 512)

    def out_weight(l, p):
        return weight(WF, l, p, 1024, 128)

    shared = [0]
    share_sems = [[send_sems.at[SEND_RING + k] for k in range(ARS.shape[0])]]
    share_sems.append([arrival() for _ in range(ARR.shape[0])])
    share_prev = {}

    def share_start(value):
        k = shared[0]
        shared[0] += 1
        slot = k % ARS.shape[0]
        if slot in share_prev:
            share_prev[slot].wait_send()
        ARS[slot] = value.astype(BF)
        k = k % ARR.shape[0]
        c = remote(ARS.at[slot], ARR.at[k], core_peer, share_sems[0][slot], share_sems[1][k])
        c.start()
        share_prev[slot] = c
        return c, slot, k

    def share_end(handle):
        c, slot, k = handle
        c.wait_recv()
        return ARS[slot].astype(F32) + ARR[k].astype(F32)

    class Scan:
        def __init__(self, call, forward):
            self.call, self.forward = call, forward

        def pack_normalizer(self, which, part):
            sub = lax.broadcasted_iota(jnp.int32, (16, 128), 0)
            rest = jnp.zeros((16, 128), F32)
            for k in range(3):
                piece = part.astype(BF).astype(F32)
                rest = jnp.where(sub == k, piece, rest)
                part = part - piece
            SCS[which, pl.ds(128, 16)] = rest.astype(BF)

        def start(self, k_state, v_state, z_row):
            which = self.call
            SCS[which, pl.ds(0, 128)] = (k_state + pltpu.roll(v_state, HEAD, 1)).astype(BF)
            self.pack_normalizer(which, z_row)
            self.near = []
            for d in range(1, near):
                peer = (high * near + lax.rem(low + d, near), m)
                self.near.append(send(SCS.at[which], SCR1.at[self.call, d - 1], peer))

        def step(self):
            for c in self.near:
                c.wait_recv()
                leave_done(c)
            which = self.call
            both = SCS[which].astype(F32)
            for d in range(1, near):
                both = both + SCR1[self.call, d - 1].astype(F32)
            SCS[which, pl.ds(0, 128)] = both[:128].astype(BF)
            self.pack_normalizer(which, jnp.sum(both[128:131], axis=0, keepdims=True))
            self.links = []
            for d in range(1, blocks):
                to = high + d if self.forward else high - d
                frm = high - d if self.forward else high + d
                inside = to < blocks if self.forward else to >= 0
                comes = frm >= 0 if self.forward else frm < blocks
                target = jnp.where(inside, to, high)
                leave = send_sems.at[SEND_RING + ARS.shape[0] + (self.call % 2) * (blocks - 1) + d - 1]
                target = (target * near + low, m)
                c = remote(SCS.at[which], SCR2.at[self.call, d - 1], target, leave, arrival())

                @pl.when(inside)
                def _(c=c):
                    c.start()

                self.links.append((c, inside, comes))

        def end(self):
            acc = SCP.at[self.call % 2]
            before = jnp.zeros(acc.shape, F32)
            for d in range(1, near):
                mine = low >= d if self.forward else low < d
                before = before + jnp.where(mine, SCR1[self.call, d - 1].astype(F32), 0.0)
            acc[...] = before
            for d, (c, inside, comes) in enumerate(self.links):

                @pl.when(comes)
                def _(c=c, d=d):
                    c.wait_recv()
                    acc[...] += SCR2[self.call, d].astype(F32)

            for c, inside, comes in self.links:

                @pl.when(inside)
                def _(c=c):
                    c.wait_send()

            block = acc[pl.ds(0, 128)]
            k_state = jnp.where(diag, block, 0.0)
            v_state = pltpu.roll(jnp.where(diag, 0.0, block), HEAD, 1)
            return k_state, v_state, jnp.sum(acc[pl.ds(128, 3)], axis=0, keepdims=True)

    def add_to(buf, at, more):
        buf[at] = (buf[at].astype(F32) + more.astype(F32)).astype(BF)

    class Scatter:
        def __init__(self, buf, land, l, x_first, z_second):
            self.buf, self.land, self.l = buf, land, l
            self.x_first, self.z_second = x_first, z_second
            self.first_peer = x_peer if x_first else y_peer
            self.next_peer = y_peer if x_first else x_peer
            self.c = {}

        def block(self, first_other, next_other, zz=every):
            ox, oy = (first_other, next_other) if self.x_first else (next_other, first_other)
            return (self.l, 1 - y if oy else y, zz, 1 - x if ox else x)

        def start(self, o):
            src = self.buf.at[self.block(1, o)]
            self.c[0, o] = send(src, self.land.at[self.l, pl.ds(4 * o, 4)], self.first_peer)

        def add(self, o):
            self.c[0, o].wait_recv()
            add_to(self.buf, self.block(0, o), self.land[self.l, pl.ds(4 * o, 4)])
            if self.z_second:
                self.along_z(o, 7 + 3 * o, 15 + o)
            elif o:
                src = self.buf.at[self.block(0, o)]
                self.next = send(src, self.land.at[self.l, pl.ds(8, 4)], self.next_peer)

        def along_z(self, o, base, extra):
            near, far, through = arrival(), arrival(), arrival()
            self.c[1, o] = (near, far, through, base, extra)
            src = self.buf.at[self.block(0, o, flip_z(1))]
            send(src, self.land.at[self.l, base + 1], z_peer[1], near)
            src = self.buf.at[self.block(0, o, flip_z(3))]
            slot = jnp.where(inner, base + 3, extra)
            peer = (jnp.where(inner, z_peer[3][0], z_peer[1][0]), m)
            first = used[0] - 2
            send(src, self.land.at[self.l, slot], peer, recv_sems.at[jnp.where(inner, first, first + 1)])

        def relay_z(self, o):
            near, far, through, base, extra = self.c[1, o]

            @pl.when(inner)
            def _():
                arrived(self.land.at[self.l, extra], through)
                add_to(self.buf, self.block(0, o, flip_z(2)), self.land[self.l, extra])

            src = self.buf.at[self.block(0, o, flip_z(2))]
            send(src, self.land.at[self.l, base + 2], z_peer[2], near)

        def relay(self):
            for o in (1, 0) if self.z_second else (0,):
                self.relay_z(o)

        def sum_z(self, o):
            near, far, through, base, extra = self.c[1, o]
            at_ = self.block(0, o, z)

            @pl.when(inner)
            def _():
                arrived(self.land.at[self.l, base + 3], far)
                add_to(self.buf, at_, self.land[self.l, base + 3])

            arrived(self.land.at[self.l, pl.ds(base + 1, 2)], near)
            total = self.buf[at_].astype(F32) + self.land[self.l, base + 1].astype(F32)
            return total + self.land[self.l, base + 2].astype(F32)

        def turn(self):
            if self.z_second:
                for o in (1, 0):
                    self.buf[self.block(0, o, z)] = self.sum_z(o).astype(BF)
                    if o:
                        src = self.buf.at[self.block(0, o, z)]
                        self.c[2] = send(src, self.land.at[self.l, 14], self.next_peer)
                return
            self.next.wait_recv()
            for d in (1, 3, 2, 0):
                add_to(self.buf, self.block(0, 0, flip_z(d)), self.land[self.l, 8 + flip_z(d)])
                if d == 3:
                    self.along_z(0, 11, 15)

        def end(self):
            if not self.z_second:
                return self.sum_z(0)
            self.c[2].wait_recv()
            return self.buf[self.block(0, 0, z)].astype(F32) + self.land[self.l, 14].astype(F32)

    finals = []

    def finish(l, name):
        total = scatters[name, l].end()
        if name == UP:
            OUP[l] = total
            finals.append(local(OUP.at[l], gup_hbm.at[l]))
        elif name == DOWN:
            ODN[l] = total
            finals.append(local(ODN.at[l], gdown_hbm.at[l]))
        elif name == OUT:
            OOUT[l] = total
            finals.append(local(OOUT.at[l], gout_hbm.at[l]))
        elif name == Q:
            OQKV[l, 0] = total
            finals.append(local(OQKV.at[l, 0], gqkv_hbm.at[l, 0]))
        elif name == KV:
            OQKV[l, 1] = total[:, :128]
            OQKV[l, 2] = total[:, 128:]
            finals.append(local(OQKV.at[l, pl.ds(1, 2)], gqkv_hbm.at[l, pl.ds(1, 2)]))
        else:
            OCTRL[l] = total
            finals.append(local(OCTRL.at[l], gctrl_hbm.at[l]))

    def split_rows(value):
        return value.astype(BF).reshape(4, 2, R, value.shape[-1])

    def grad_up(l, o):
        yy = 1 - y if o else y
        RUP[l, yy] = split_rows(tn(FB[l], DU[yy]))

    def grad_down(l, o):
        yy = 1 - y if o else y
        RDN[l, yy] = split_rows(tn(GBF[...], GG[l, yy]))

    def grad_out(l):
        grads = tn(GBF[...], OB[l])
        for p in range(2):
            ROUT[l, p] = split_rows(grads[:, p * 128 : (p + 1) * 128])

    scatters = {}
    for l in range(layers):
        for name, buf, land in (
            (Q, RQ, LQ),
            (KV, RKV, LKV),
            (C, RC, LC),
            (OUT, ROUT, LOUT),
            (UP, RUP, LUP),
            (DOWN, RDN, LDN),
        ):
            f = Scatter(buf, land, l, (name, l) in X_FIRST, (name, l) in Z_SECOND)
            scatters[name, l] = f
            jobs[name, l] = {
                START1: functools.partial(f.start, 1),
                START0: functools.partial(f.start, 0),
                ADD1: functools.partial(f.add, 1),
                ADD0: functools.partial(f.add, 0),
                TURN: f.turn,
                RELAY: f.relay,
                END: functools.partial(finish, l, name),
            }
        for name, f in ((UP, grad_up), (DOWN, grad_down)):
            jobs[name, l][GRAD1] = functools.partial(f, l, 1)
            jobs[name, l][GRAD0] = functools.partial(f, l, 0)
        jobs[OUT, l][GRAD1] = functools.partial(grad_out, l)

    tok_copy.wait()
    cot_copy.wait()
    arrived(GAIN.at[pl.ds(1, 7)], gains_here)
    for gz in range(GROUPS // 2):
        total = jnp.zeros((8, 128), F32)
        for d in range(4):
            here = flip_z(d) == gz
            total = total + jnp.where(here, GAIN[2 * d] + GAIN[2 * d + 1], 0.0)
        GFULL[:, pl.ds(gz * 128, 128)] = total

    def gain_row(l, which):
        return GFULL[pl.ds(2 * l + which, 1), :]

    def stream(l, rows):
        return TOKB[0, rows].astype(F32) if l == 0 else H[l - 1, rows]

    def attn_norm(l, i):
        rows = tile_rows(i)
        y_hat, _ = norm_parts(stream(l, rows))
        AB[l, rows] = (y_hat * gain_row(l, 0)).astype(BF)

    for i in range(tiles):
        attn_norm(0, i)

    length = len_ref[y]

    def valid_rows(i):
        row = lax.broadcasted_iota(jnp.int32, (TILE, 1), 0)
        return jnp.where(s * T + i * TILE + row < length, 1.0, 0.0)

    for i in range(tiles):
        rows = tile_rows(i)
        dh = TOKB[1, rows].astype(F32) * valid_rows(i)
        DMID[rows] = dh
        GBF[rows] = dh.astype(BF)

    at(FIRST)

    for l in range(layers):
        more_layers = l + 1 < layers
        at(fwd(l, 0))
        scans = [Scan(2 * l + p, True) for p in range(2)]

        def project_pair(p, l=l):
            out = nn(AB[l], mixer_weight(l, p))
            kv = out[:, 128:384].astype(BF)
            th = jnp.tanh(out[:, 384:] * (1.0 / 16.0))
            w = jnp.exp(16.0 * th).astype(BF)
            sums = [
                (
                    tn(w[j * TILE : (j + 1) * TILE], kv[j * TILE : (j + 1) * TILE]),
                    jnp.sum(w[j * TILE : (j + 1) * TILE].astype(F32), axis=0, keepdims=True),
                )
                for j in range(tiles)
            ]
            ks, vs, zs = 0.0, 0.0, 0.0
            for j, (both, z_j) in enumerate(sums):
                k_j = jnp.where(diag, both[:, :128], 0.0)
                v_j = jnp.where(diag, both[:, 128:], 0.0)
                if j < tiles - 1:
                    LOC[p, j, 0] = k_j
                    LOC[p, j, 1] = v_j
                ks, vs, zs = ks + k_j, vs + v_j, zs + z_j
            QKV[l, p, :, pl.ds(0, 128)] = out[:, :128].astype(BF)
            QKV[l, p, :, pl.ds(128, 256)] = kv
            WB[l, p] = w
            S2[l, p] = (1.0 - th * th).astype(BF)
            return ks, vs, zs

        def inside_block(p, l=l):
            units = range(tiles)
            w = [WB[l, p, tile_rows(j)] for j in units]
            q = [QKV[l, p, tile_rows(j), pl.ds(0, 128)] for j in units]
            k = [QKV[l, p, tile_rows(j), pl.ds(128, 128)] for j in units]
            qs = [heads(q[j]) for j in units]
            a = [[jnp.where(lower, nt(qs[j][h], k[j]), 0.0).astype(BF) for h in (0, 1)] for j in units]
            sums = [nn(lower_ones, w[j]) for j in units]
            ws = [heads(w[j]) for j in units]
            num = [nn(a[j][0], ws[j][0]) + nn(a[j][1], ws[j][1]) for j in units]
            for j in units:
                for h in (0, 1):
                    AST[l, p, j, h] = a[j][h]
                ZS[l, p, tile_rows(j)] = sums[j]
                XS[l, p, tile_rows(j)] = num[j]

        def with_earlier(states, l=l):
            units = [(p, j) for p in range(2) for j in range(tiles)]
            ks, vs, z_before = {}, {}, {}
            for p, j in units:
                if j == 0:
                    k_pre, v_pre, z_pre = states[p]
                else:
                    k_pre = k_pre + LOC[p, j - 1, 0]
                    v_pre = v_pre + LOC[p, j - 1, 1]
                    z_pre = z_pre + jnp.sum(
                        WB[l, p, tile_rows(j - 1)].astype(F32), axis=0, keepdims=True
                    )
                ks[p, j], vs[p, j], z_before[p, j] = k_pre.astype(BF), v_pre.astype(BF), z_pre
            w = {(p, j): WB[l, p, tile_rows(j)] for p, j in units}
            q = {(p, j): QKV[l, p, tile_rows(j), pl.ds(0, 128)] for p, j in units}
            v = {(p, j): QKV[l, p, tile_rows(j), pl.ds(256, 128)] for p, j in units}
            inv = {(p, j): 1.0 / (ZS[l, p, tile_rows(j)] + z_before[p, j]) for p, j in units}
            num = {(p, j): XS[l, p, tile_rows(j)] for p, j in units}
            xs = {u: (num[u] + nt(q[u], ks[u])) * inv[u] * 0.125 for u in units}
            e = {u: jnp.exp(xs[u] - per_head_max(xs[u])) for u in units}
            prob = {u: e[u] / per_head(e[u]) for u in units}
            scaled = {u: (prob[u] * inv[u]).astype(BF) for u in units}
            rs = {u: heads(scaled[u]) for u in units}
            mm = {
                u: [jnp.where(lower, nt(rs[u][h], w[u]), 0.0).astype(BF) for h in (0, 1)]
                for u in units
            }
            vh = {u: heads(v[u]) for u in units}
            out = {
                u: nn(scaled[u], vs[u]) + nn(mm[u][0], vh[u][0]) + nn(mm[u][1], vh[u][1])
                for u in units
            }
            for p, j in units:
                rows = tile_rows(j)
                KP[l, p, j] = ks[p, j]
                VP[l, p, j] = vs[p, j]
                ZS[l, p, rows] = inv[p, j]
                XS[l, p, rows] = xs[p, j]
                PS[l, p, rows] = prob[p, j]
                for h in (0, 1):
                    MST[l, p, j, h] = mm[p, j][h]
                OB[l, rows, pl.ds(p * 128, 128)] = out[p, j].astype(BF)

        for p in range(2):
            scans[p].start(*project_pair(p))
            at(fwd(l, 1 + p))
        for p in range(2):
            inside_block(p)
            at(fwd(l, 3 + 2 * p))
            scans[p].step()
            at(fwd(l, 4 + 2 * p))
        with_earlier([scans[0].end(), scans[1].end()])
        at(fwd(l, 7))

        handles = []
        for i in range(tiles):
            rows = tile_rows(i)
            part = nt(OB[l, rows, pl.ds(0, 128)], out_weight(l, 0))
            part = part + nt(OB[l, rows, pl.ds(128, 128)], out_weight(l, 1))
            handles.append(share_start(part))
        at(fwd(l, 8))
        more = []
        for i in range(tiles):
            rows = tile_rows(i)
            mid = stream(l, rows) + share_end(handles[i])
            y_hat, _ = norm_parts(mid)
            f = (y_hat * gain_row(l, 1)).astype(BF)
            hidden = [nn(f, up_weight(l, p)) for p in range(2)]
            gates = [gate_and_slope(u) for u in hidden]
            low_gates = [gate.astype(BF) for gate, _ in gates]
            if more_layers:
                part = nt(low_gates[0], down_weight(l, 0)) + nt(low_gates[1], down_weight(l, 1))
                more.append(share_start(part))
            MID[l, rows] = mid
            FB[l, rows] = f
            slopes = GU.at[l] if more_layers else DU
            for p in range(2):
                GG[l, p, rows] = low_gates[p]
                slopes[p, rows] = gates[p][1].astype(BF)
            at(fwd(l, 9 + i))
        if not more_layers:
            for i in range(tiles):
                rows = tile_rows(i)
                gb = GBF[rows]
                du = [
                    (nn(gb, down_weight(l, p)) * DU[p, rows].astype(F32)).astype(BF)
                    for p in range(2)
                ]
                part = nt(du[0], up_weight(l, 0)) + nt(du[1], up_weight(l, 1))
                more.append(share_start(part))
                for p in range(2):
                    DU[p, rows] = du[p]
        if more_layers:
            for i in range(tiles):
                rows = tile_rows(i)
                H[l, rows] = MID[l, rows] + share_end(more[i])
                attn_norm(l + 1, i)
            at(fwd(l, 11))

    half_rows = pl.ds(pl.multiple_of(core * (T // 2), T // 2), T // 2)

    class Spread:
        def __init__(self, k, out):
            self.k, self.out = k, out

        def start(self):
            src = OUTB.at[self.k, y, half_rows]
            self.c = send(src, src, y_peer)

        def hop(self):
            self.c.wait_recv()
            src = OUTB.at[self.k, 1 - y, half_rows]
            self.c = send(src, src, core_peer)

        def end(self):
            self.c.wait_recv()
            finals.append(local(OUTB.at[self.k], self.out))

    for name, f in ((MIXED, Spread(0, mixed_hbm)), (TOKENS, Spread(1, gt_hbm))):
        jobs[name, 0] = {START: f.start, HOP: f.hop, END: f.end}

    grad_norm = [None] * (2 * layers)

    for l in range(last, -1, -1):
        if l == last:
            at(bwd(l, 0))
            handles = more
        else:
            for i in range(tiles):
                GBF[tile_rows(i)] = DMID[tile_rows(i)].astype(BF)
            at(bwd(l, 0))
            handles = []
            for i in range(tiles):
                rows = tile_rows(i)
                gb = GBF[rows]
                du = [
                    (nn(gb, down_weight(l, p)) * GU[l, p, rows].astype(F32)).astype(BF)
                    for p in range(2)
                ]
                part = nt(du[0], up_weight(l, 0)) + nt(du[1], up_weight(l, 1))
                handles.append(share_start(part))
                for p in range(2):
                    DU[p, rows] = du[p]
        at(bwd(l, 1))
        gsum = jnp.zeros((1, D), F32)
        for i in range(tiles):
            rows = tile_rows(i)
            df = share_end(handles[i])
            y_hat, rstd = norm_parts(MID[l, rows])
            gsum = gsum + jnp.sum(df * y_hat, axis=0, keepdims=True)
            df = df * gain_row(l, 1)
            dm = DMID[rows] + (
                df
                - jnp.mean(df, axis=-1, keepdims=True)
                - y_hat * jnp.mean(df * y_hat, axis=-1, keepdims=True)
            ) * rstd
            DMID[rows] = dm
            GBF[rows] = dm.astype(BF)
            for p in range(2):
                DOB[p, rows] = nn(GBF[rows], out_weight(l, p)).astype(BF)
        grad_norm[2 * l + 1] = gsum
        at(bwd(l, 2))

        scans = [Scan(2 * layers + 2 * (last - l) + k, False) for k in range(2)]
        order = (1 - y, y)

        def to_states(l=l):
            units = [(k, j) for k in range(2) for j in range(tiles - 1, -1, -1)]
            rows = {u: tile_rows(u[1]) for u in units}
            w = {(k, j): WB[l, order[k], rows[k, j]] for k, j in units}
            q = {(k, j): QKV[l, order[k], rows[k, j], pl.ds(0, 128)] for k, j in units}
            v = {(k, j): QKV[l, order[k], rows[k, j], pl.ds(256, 128)] for k, j in units}
            do = {(k, j): DOB[order[k], rows[k, j]] for k, j in units}
            inv = {(k, j): ZS[l, order[k], rows[k, j]] for k, j in units}
            prob = {(k, j): PS[l, order[k], rows[k, j]] for k, j in units}
            xs = {(k, j): XS[l, order[k], rows[k, j]] for k, j in units}
            v_pre = {(k, j): VP[l, order[k], j] for k, j in units}
            ws = {u: heads(w[u]) for u in units}
            dos = {u: heads(do[u]) for u in units}
            pair = {
                u: [jnp.where(lower, nt(dos[u][h], v[u]), 0.0).astype(BF) for h in (0, 1)]
                for u in units
            }
            dr = {
                u: nt(do[u], v_pre[u]) + nn(pair[u][0], ws[u][0]) + nn(pair[u][1], ws[u][1])
                for u in units
            }
            dp = {u: dr[u] * inv[u] for u in units}
            dx = {u: prob[u] * (dp[u] - per_head(dp[u] * prob[u])) for u in units}
            dn = {u: (dx[u] * inv[u] * 0.125).astype(BF) for u in units}
            r = {u: (prob[u] * inv[u]).astype(BF) for u in units}
            dz = {
                u: -(r[u].astype(F32) * dp[u]) - 8.0 * dn[u].astype(F32) * xs[u] for u in units
            }
            dk = {u: jnp.where(diag, tn(dn[u], q[u]), 0.0) for u in units}
            dv = {u: jnp.where(diag, tn(r[u], do[u]), 0.0) for u in units}
            totals = []
            for k in range(2):
                total = [0.0, 0.0, 0.0]
                for j in range(tiles):
                    dzs = jnp.sum(dz[k, j], axis=0, keepdims=True)
                    total = [a + b for a, b in zip(total, (dk[k, j], dv[k, j], dzs))]
                totals.append(total)
            for k, j in units:
                p = order[k]
                for h in (0, 1):
                    YST[p, j, h] = pair[k, j][h]
                DNB[p, rows[k, j]] = dn[k, j]
                DZ[p, rows[k, j]] = dz[k, j]
                if j > 0:
                    LOC[p, j - 1, 0] = dk[k, j]
                    LOC[p, j - 1, 1] = dv[k, j]
            return totals

        def within(p, l=l):
            units = range(tiles)
            rows = [tile_rows(j) for j in units]
            w = [WB[l, p, rows[j]] for j in units]
            q = [QKV[l, p, rows[j], pl.ds(0, 128)] for j in units]
            k = [QKV[l, p, rows[j], pl.ds(128, 128)] for j in units]
            do = [DOB[p, rows[j]] for j in units]
            dn = [DNB[p, rows[j]] for j in units]
            r = [(PS[l, p, rows[j]] * ZS[l, p, rows[j]]).astype(BF) for j in units]
            dz = [DZ[p, rows[j]] for j in units]
            k_pre = [KP[l, p, j] for j in units]
            dz_hi = [dz[j].astype(BF) for j in units]
            dz_lo = [(dz[j] - dz_hi[j].astype(F32)).astype(BF) for j in units]
            dns, rs, dos, qs, ks = ([heads(a[j]) for j in units] for a in (dn, r, do, q, k))
            da = [
                [jnp.where(lower, nt(dns[j][h], w[j]), 0.0).astype(BF) for h in (0, 1)]
                for j in units
            ]
            dq = [
                nn(dn[j], k_pre[j]) + nn(da[j][0], ks[j][0]) + nn(da[j][1], ks[j][1]) for j in units
            ]
            dk = [tn(da[j][0], qs[j][0]) + tn(da[j][1], qs[j][1]) for j in units]
            dv = [
                tn(MST[l, p, j, 0], dos[j][0]) + tn(MST[l, p, j, 1], dos[j][1]) for j in units
            ]
            dw = [
                nn(upper_ones, dz_hi[j])
                + nn(upper_ones, dz_lo[j])
                + tn(YST[p, j, 0], rs[j][0])
                + tn(AST[l, p, j, 0], dns[j][0])
                + tn(YST[p, j, 1], rs[j][1])
                + tn(AST[l, p, j, 1], dns[j][1])
                for j in units
            ]
            for j in units:
                DU[p, rows[j], pl.ds(0, 128)] = dq[j].astype(BF)
                DWF[p, rows[j], pl.ds(0, 128)] = dk[j]
                DWF[p, rows[j], pl.ds(128, 128)] = dv[j]
                DWF[p, rows[j], pl.ds(256, 128)] = dw[j]

        def with_later(k, p, l=l):
            k_post, v_post, z_after = scans[k].end()
            for j in range(tiles - 1, -1, -1):
                rows = tile_rows(j)
                if j < tiles - 1:
                    k_post = k_post + LOC[p, j, 0]
                    v_post = v_post + LOC[p, j, 1]
                    z_after = z_after + jnp.sum(DZ[p, tile_rows(j + 1)], axis=0, keepdims=True)
                kb, vb = k_post.astype(BF), v_post.astype(BF)
                w = WB[l, p, rows]
                key = QKV[l, p, rows, pl.ds(128, 128)]
                v = QKV[l, p, rows, pl.ds(256, 128)]
                dk = DWF[p, rows, pl.ds(0, 128)] + nn(w, kb)
                dv = DWF[p, rows, pl.ds(128, 128)] + nn(w, vb)
                dw = DWF[p, rows, pl.ds(256, 128)] + nt(key, kb) + nt(v, vb) + z_after
                dc = dw * w.astype(F32) * S2[l, p, rows].astype(F32)
                DU[p, rows, pl.ds(128, 128)] = dk.astype(BF)
                DU[p, rows, pl.ds(256, 128)] = dv.astype(BF)
                DU[p, rows, pl.ds(384, 128)] = dc.astype(BF)

        totals = to_states()
        for k in range(2):
            scans[k].start(*totals[k])
        if l == last:
            outs = []
            for i in range(tiles):
                rows = tile_rows(i)
                part = nt(GG[l, 0, rows], down_weight(l, 0)) + nt(GG[l, 1, rows], down_weight(l, 1))
                outs.append(share_start(part))
        at(bwd(l, 3))
        for k in range(2):
            scans[k].step()
            at(bwd(l, 4 + k))
        for k in range(2):
            p = order[k]
            within(p)
            RQ[l, p] = split_rows(tn(AB[l], DU[p, :, pl.ds(0, 128)]))
            if l == last and k == 0:
                for i in range(tiles):
                    rows = tile_rows(i)
                    out = MID[l, rows] + share_end(outs[i])
                    OUTB[0, y, rows] = (out * valid_rows(i)).astype(BF)
            at(bwd(l, 6 + k))
        for k in range(2):
            p = order[k]
            with_later(k, p)
            grads = split_rows(tn(AB[l], DU[p, :, pl.ds(128, 384)]))
            RKV[l, p] = grads[..., :256]
            RC[l, p] = grads[..., 256:]
            at(bwd(l, 8 + k))
        handles = []
        for i in range(tiles):
            rows = tile_rows(i)
            part = nt(DU[0, rows], mixer_weight(l, 0))
            part = part + nt(DU[1, rows], mixer_weight(l, 1))
            handles.append(share_start(part))
        at(bwd(l, 10))
        gsum = jnp.zeros((1, D), F32)
        for i in range(tiles):
            rows = tile_rows(i)
            da = share_end(handles[i])
            y_hat, rstd = norm_parts(stream(l, rows))
            gsum = gsum + jnp.sum(da * y_hat, axis=0, keepdims=True)
            da = da * gain_row(l, 0)
            dh = DMID[rows] + (
                da
                - jnp.mean(da, axis=-1, keepdims=True)
                - y_hat * jnp.mean(da * y_hat, axis=-1, keepdims=True)
            ) * rstd
            DMID[rows] = dh
            if l == 0:
                OUTB[1, y, rows] = dh.astype(BF)
        grad_norm[2 * l] = gsum
        at(bwd(l, 11))

    class Gains:
        def start(self):
            sub = lax.broadcasted_iota(jnp.int32, (8, D), 0)
            self.rows = jnp.zeros((8, D), F32)
            for k in range(2 * layers):
                self.rows = jnp.where(sub == k, grad_norm[k], self.rows)
            GN[...] = self.rows
            self.c = send(GN, GNY, y_peer)

        def hop(self):
            self.c.wait_recv()
            both = self.rows + GNY[...]
            for gz in range(GROUPS // 2):
                GNR[0, gz] = both[:, gz * 128 : (gz + 1) * 128]
            self.c = arrival()
            for d in range(4):
                for o in range(2):
                    if (d, o) == (0, 0):
                        continue
                    peer = (seq_of(1 - x if o else x, flip_z(d)), m)
                    k = 2 * d + o
                    send(GNR.at[0, flip_z(d)], GNR.at[1, k], peer, self.c)

        def end(self):
            total = GNR[0, z]
            arrived(GNR.at[1, pl.ds(1, 7)], self.c)
            for k in range(1, 8):
                total = total + GNR[1, k]
            GNO[...] = total
            finals.append(local(GNO, gn_hbm))

    f = Gains()
    jobs[GAINS, 0] = {START: f.start, HOP: f.hop, END: f.end}
    at(TAIL)
    for c in finals:
        c.wait()
    for c in (*leaving.values(), *share_prev.values()):
        c.wait_send()
    for c in inner_last:

        @pl.when(inner)
        def _(c=c):
            c.wait_send()

    assert used[0] == recv_sems.shape[0] and used[1] == local_sems.shape[0], used
    assert inner_used[0] == inner_sems.shape[0], inner_used


def lay_out(stride, *refs):
    mixed, tokens, qkv, ctrl, out, up, down, gains = refs[:8]
    mixed_out, tokens_out, attn_out, ffn_out, *weights_out = refs[8:17]
    wide, sems, *held = refs[17:]
    arrays = (tokens, mixed, up, down, qkv, ctrl, out)
    results = (None, mixed_out, weights_out[3], weights_out[4], *weights_out[:3])
    parts = [(k, b) for k in range(len(arrays)) for b in range(2)]
    ins = {
        (k, b): pltpu.make_async_copy(arrays[k].at[b], held[k].at[b], sems.at[0, k, b])
        for k, b in parts
    }
    for c in ins.values():
        c.start()
    x = (lax.axis_index("seq") // stride) % 2
    R = attn_out.shape[1]
    rows = jnp.where(x == 0, gains[:, pl.ds(0, R)], gains[:, pl.ds(R, R)])
    for l in range(attn_out.shape[0]):
        attn_out[pl.ds(l, 1), :] = rows[2 * l : 2 * l + 1]
        ffn_out[pl.ds(l, 1), :] = rows[2 * l + 1 : 2 * l + 2]
    outs = []
    for k, b in parts:
        ins[k, b].wait()
        if k == 0:
            wide[b] = held[0][b].astype(F32)
            c = pltpu.make_async_copy(wide.at[b], tokens_out.at[b], sems.at[1, k, b])
        else:
            c = pltpu.make_async_copy(held[k].at[b], results[k].at[b], sems.at[1, k, b])
        c.start()
        outs.append(c)
    for c in outs:
        c.wait()


def shards(tokens, lengths, norm_attn, norm_ffn, w_qkv, w_ctrl, w_out, w_up, w_down, cotangent):
    layers = w_qkv.shape[0]
    n_seq = lax.axis_size("seq")
    stride = n_seq // GROUPS
    _, T, D = tokens.shape
    rows = w_qkv.shape[1]
    weights = [w_qkv.transpose(0, 2, 1, 3), w_ctrl, w_up, w_down, w_out]
    gains = [norm_attn, norm_ffn]
    blocks = [[k * stride + j for j in range(stride)] for k in range(GROUPS)]
    if stride > 1:

        def fill(a, dim=1):
            return lax.all_gather(a, "seq", axis=dim, tiled=True, axis_index_groups=blocks)

        weights = [fill(a, a.ndim - 2) for a in weights]
        gains = [fill(a) for a in gains]
    R = D // GROUPS
    A = 3 * w_qkv.shape[-1] + w_ctrl.shape[-1]
    U = w_up.shape[-1]
    F = 2 * U + w_out.shape[-1]
    near = near_size(n_seq)
    far = n_seq // near
    tiles = T // TILE
    arrivals = 1 + sum(19 if (n, l) in GATHER_Z_SECOND else 13 for n in range(3) for l in range(layers))
    arrivals += 2 * tiles + 4 * layers * (near + far - 2)
    arrivals += sum(9 if (n, l) in Z_SECOND else 6 for n in range(Q, DOWN + 1) for l in range(layers))
    inner_copies = sum(3 if (n, l) in GATHER_Z_SECOND else 1 for n in range(3) for l in range(layers))
    arrivals += 4 + 2
    bf, f32 = BF, F32
    v = pltpu.VMEM
    scratch = [
        v((max(layers - 1, 1), T, D), f32),
        v((layers, T, D), f32),
        v((layers, T, D), bf),
        v((layers, T, D), bf),
        v((layers, 2, T, 384), bf),
        v((layers, 2, T, 128), bf),
        v((layers, 2, T, 128), bf),
        v((layers, 2, T, 128), f32),
        v((layers, 2, T, 128), f32),
        v((layers, 2, T, 128), f32),
        v((layers, 2, tiles, 2, TILE, TILE), bf),
        v((layers, 2, tiles, 2, TILE, TILE), bf),
        v((layers, T, 256), bf),
        v((max(layers - 1, 1), 2, T, U), bf),
        v((layers, 2, T, U), bf),
        v((layers, 2, tiles, 128, 128), bf),
        v((layers, 2, tiles, 128, 128), bf),
        v((2, max(tiles - 1, 1), 2, 128, 128), f32),
        v((2, T, D), bf),
        v((T, D), bf),
        v((2, T, 128), bf),
        v((2, T, U), bf),
        v((T, D), f32),
        v((2, tiles, 2, TILE, TILE), bf),
        v((2, T, 128), bf),
        v((2, T, 128), f32),
        v((2, T, 384), f32),
        v((layers, 2, 4, 2, R, A), bf),
        v((layers, 2, 4, 2, R, F), bf),
        v((8, 8, 128), f32),
        v((2, layers, R), bf),
        v((8, D), f32),
        v((tiles, TILE, D), bf),
        v((2 * tiles, TILE, D), bf),
        v((4 * layers, 144, 128), bf),
        v((4 * layers, near - 1, 144, 128), bf),
        v((4 * layers, far - 1, 144, 128), bf),
        v((2, 144, 128), f32),
        v((layers, 2, 4, 2, R, 128), bf),
        v((layers, 2, 4, 2, R, 256), bf),
        v((layers, 2, 4, 2, R, 128), bf),
        v((layers, 2, 4, 2, R, 128), bf),
        v((layers, 2, 4, 2, R, U), bf),
        v((layers, 2, 4, 2, R, U), bf),
        v((layers, 17, R, 128), bf),
        v((layers, 17, R, 256), bf),
        v((layers, 17, R, 128), bf),
        v((layers, 17, R, 128), bf),
        v((layers, 17, R, U), bf),
        v((layers, 17, R, U), bf),
        v((layers, 3, R, 128), f32),
        v((layers, R, 128), f32),
        v((layers, R, 128), f32),
        v((layers, R, U), f32),
        v((layers, R, U), f32),
        v((8, D), f32),
        v((8, D), f32),
        v((2, 8, 8, 128), f32),
        v((8, 128), f32),
        v((2, 2, T, D), bf),
        pltpu.SemaphoreType.DMA((SEND_RING + tiles + 2 * (far - 1),)),
        pltpu.SemaphoreType.DMA((inner_copies,)),
        pltpu.SemaphoreType.DMA((arrivals,)),
        pltpu.SemaphoreType.DMA((7 + 13 * layers,)),
    ]
    any_spec = pl.BlockSpec(memory_space=pl.ANY)
    out_shape = (
        jax.ShapeDtypeStruct((2, T, D), bf),
        jax.ShapeDtypeStruct((2, T, D), bf),
        jax.ShapeDtypeStruct((layers, 3, R, 128), f32),
        jax.ShapeDtypeStruct((layers, R, 128), f32),
        jax.ShapeDtypeStruct((layers, R, 128), f32),
        jax.ShapeDtypeStruct((layers, R, U), f32),
        jax.ShapeDtypeStruct((layers, R, U), f32),
        jax.ShapeDtypeStruct((8, 128), f32),
    )
    mixed, grad_tokens, *grads, gn = pl.pallas_call(
        functools.partial(kernel, n_seq, layers),
        out_shape=out_shape,
        in_specs=[
            any_spec,
            any_spec,
            pl.BlockSpec(memory_space=pltpu.SMEM),
            *[any_spec] * 7,
        ],
        out_specs=(any_spec,) * len(out_shape),
        scratch_shapes=scratch,
        compiler_params=pltpu.CompilerParams(
            collective_id=0, has_side_effects=True, vmem_limit_bytes=VMEM_BYTES
        ),
    )(tokens, cotangent, lengths, *weights, *gains)
    out_shape = (
        jax.ShapeDtypeStruct((2, T, D), bf),
        jax.ShapeDtypeStruct((2, T, D), f32),
        jax.ShapeDtypeStruct((layers, R), f32),
        jax.ShapeDtypeStruct((layers, R), f32),
        *[jax.ShapeDtypeStruct(a.shape, f32) for a in grads],
    )
    vmem_spec = pl.BlockSpec(memory_space=pltpu.VMEM)
    mixed, grad_tokens, *grads = pl.pallas_call(
        functools.partial(lay_out, stride),
        out_shape=out_shape,
        in_specs=[any_spec] * 7 + [vmem_spec],
        out_specs=(any_spec, any_spec, vmem_spec, vmem_spec) + (any_spec,) * 5,
        scratch_shapes=[
            v((2, T, D), f32),
            pltpu.SemaphoreType.DMA((2, 7, 2)),
            *[v(a.shape, a.dtype) for a in (grad_tokens, mixed, *grads[3:], *grads[:3])],
        ],
        compiler_params=pltpu.CompilerParams(vmem_limit_bytes=VMEM_BYTES),
    )(mixed, grad_tokens, *grads, gn)
    if stride > 1:

        def empty(a):
            return lax.psum_scatter(
                a, "seq", scatter_dimension=max(a.ndim - 2, 1), tiled=True, axis_index_groups=blocks
            )

        grads = [empty(a) for a in grads]
    grads[2] = grads[2].transpose(0, 2, 1, 3)
    return (mixed, grad_tokens, *grads)


VMEM_BYTES = 62 << 20


def solution(mesh):
    in_specs = (
        P(None, "seq", None),
        P(),
        P(None, "seq"),
        P(None, "seq"),
        P(None, "seq", None, "mp"),
        P(None, "seq", "mp"),
        P(None, "seq", "mp"),
        P(None, "seq", "mp"),
        P(None, "seq", "mp"),
        P(None, "seq", None),
    )
    out_specs = (
        P(None, "seq", None),
        P(None, "seq", None),
        P(None, "seq"),
        P(None, "seq"),
        P(None, "seq", None, "mp"),
        P(None, "seq", "mp"),
        P(None, "seq", "mp"),
        P(None, "seq", "mp"),
        P(None, "seq", "mp"),
    )
    return jax.shard_map(shards, mesh=mesh, in_specs=in_specs, out_specs=out_specs, check_vma=False)
```

```python
import functools

import jax
import jax.numpy as jnp
from jax import lax
from jax.experimental import pallas as pl
from jax.experimental.pallas import tpu as pltpu
from jax.sharding import PartitionSpec as P

F32 = jnp.float32
BF = jnp.bfloat16
MESH = pl.DeviceIdType.MESH
GROUPS = 8
HEAD = 64
EPS = 1e-05
TILE = 256


def nn(a, b):
    return lax.dot_general(a, b, (((1,), (0,)), ((), ())), preferred_element_type=F32)


def nt(a, b):
    return lax.dot_general(a, b, (((1,), (1,)), ((), ())), preferred_element_type=F32)


def tn(a, b):
    return lax.dot_general(a, b, (((0,), (0,)), ((), ())), preferred_element_type=F32)


def near_size(n_seq):
    return 1 << ((n_seq.bit_length() - 1) // 2)


def norm_parts(x):
    center = x - jnp.mean(x, axis=-1, keepdims=True)
    spread = jnp.mean(center * center, axis=-1, keepdims=True)
    rstd = lax.rsqrt(spread + EPS)
    return center * rstd, rstd


def gate_and_slope(u):
    u2 = u * u
    t = jnp.tanh(u * (0.7978845608 + (0.7978845608 * 0.044715) * u2))
    half = 0.5 + 0.5 * t
    gate = u * half
    slope = half + gate * (1.0 - half) * (1.5957691216 + (1.5957691216 * 0.134145) * u2)
    return gate, slope


MIXER, UPPER, LOWER, Q, KV, C, OUT, UP, DOWN, MIXED, TOKENS, GAINS = range(12)
START, OWN, ON1, ON2, ON3, ACROSS0, ACROSS1, ACROSS2, ACROSS3, END = range(10)
GRAD1, GRAD0, START1, START0, ADD1, ADD0, TURN, HOP, RELAY = range(10, 19)


def fwd(layer, k):
    return 100 + 20 * layer + k


def bwd(layer, k):
    return 200 + 20 * layer + k


ENTRY, FIRST, TAIL = 0, 1, 2
SEND_RING = 28

X_FIRST = {(Q, 1), (KV, 0), (C, 0), (OUT, 0), (OUT, 1), (DOWN, 0), (DOWN, 1)}
Z_SECOND = {(KV, 1), (DOWN, 1)}
GATHER_Z_SECOND = {(UPPER, 0), (LOWER, 1)}
PLAN = {
    ENTRY: (
        (MIXER, 1, OWN),
        (LOWER, 0, OWN),
        (MIXER, 0, START),
        (MIXER, 0, OWN),
        (MIXER, 0, ON1),
        (UPPER, 0, START),
        (MIXER, 0, ON2),
        (LOWER, 0, START),
        (UPPER, 0, OWN),
        (MIXER, 0, ACROSS0),
        (MIXER, 0, ON3),
        (MIXER, 0, ACROSS1),
        (UPPER, 0, ON1),
        (UPPER, 0, ON2),
        (MIXER, 0, ACROSS2),
    ),
    FIRST: (
        (LOWER, 1, OWN),
        (MIXER, 0, ACROSS3),
        (LOWER, 0, ON2),
        (MIXER, 0, END),
    ),
    fwd(0, 0): (
        (MIXER, 1, START),
        (LOWER, 0, ON3),
    ),
    fwd(0, 1): (
        (LOWER, 0, ON1),
        (UPPER, 0, ON3),
        (UPPER, 0, ACROSS1),
    ),
    fwd(0, 2): (
        (UPPER, 0, ACROSS0),
    ),
    fwd(0, 3): (
        (UPPER, 0, ACROSS2),
        (LOWER, 0, ACROSS3),
    ),
    fwd(0, 4): (
        (UPPER, 0, ACROSS3),
    ),
    fwd(0, 5): (
        (LOWER, 0, ACROSS2),
        (MIXER, 1, ON1),
    ),
    fwd(0, 6): (
        (LOWER, 0, ACROSS0),
        (LOWER, 0, ACROSS1),
        (LOWER, 1, ON3),
        (UPPER, 1, START),
        (MIXER, 1, ON2),
    ),
    fwd(0, 7): (
        (UPPER, 0, END),
        (LOWER, 1, START),
        (MIXER, 1, ON3),
        (LOWER, 0, END),
        (LOWER, 1, ON1),
        (LOWER, 1, ON2),
    ),
    fwd(0, 8): (
        (MIXER, 1, ACROSS1),
        (MIXER, 1, ACROSS2),
    ),
    fwd(0, 9): (
        (LOWER, 1, ACROSS0),
        (MIXER, 1, ACROSS3),
        (MIXER, 1, ACROSS0),
    ),
    fwd(0, 10): (
        (UPPER, 1, ON1),
        (UPPER, 1, ON2),
    ),
    fwd(0, 11): (
        (MIXER, 1, END),
    ),
    fwd(1, 1): (
        (UPPER, 1, ON3),
    ),
    fwd(1, 3): (
        (UPPER, 1, ACROSS1),
        (LOWER, 1, ACROSS2),
        (LOWER, 1, ACROSS1),
    ),
    fwd(1, 6): (
        (UPPER, 1, OWN),
        (LOWER, 1, ACROSS3),
        (UPPER, 1, ACROSS3),
        (UPPER, 1, ACROSS0),
        (UPPER, 1, ACROSS2),
    ),
    fwd(1, 7): (
        (LOWER, 1, END),
    ),
    fwd(1, 8): (
        (UPPER, 1, END),
    ),
    fwd(1, 10): (
        (DOWN, 1, GRAD1),
        (DOWN, 1, START1),
    ),
    bwd(1, 1): (
        (UP, 1, GRAD1),
        (UP, 1, START1),
        (DOWN, 1, GRAD0),
        (UP, 1, START0),
    ),
    bwd(1, 3): (
        (DOWN, 1, START0),
    ),
    bwd(1, 5): (
        (OUT, 1, GRAD1),
        (UP, 1, GRAD0),
    ),
    bwd(1, 6): (
        (MIXED, 0, START),
        (OUT, 1, START1),
    ),
    bwd(1, 7): (
        (Q, 1, START1),
    ),
    bwd(1, 8): (
        (UP, 1, ADD1),
        (UP, 1, ADD0),
    ),
    bwd(1, 10): (
        (Q, 1, START0),
        (DOWN, 1, ADD0),
        (KV, 1, START1),
        (KV, 1, START0),
    ),
    bwd(1, 11): (
        (Q, 1, ADD1),
        (DOWN, 1, ADD1),
        (C, 1, START0),
    ),
    bwd(0, 0): (
        (OUT, 1, ADD1),
        (DOWN, 0, GRAD1),
        (DOWN, 0, START1),
        (C, 1, START1),
        (DOWN, 0, GRAD0),
    ),
    bwd(0, 1): (
        (UP, 0, GRAD1),
        (UP, 1, TURN),
    ),
    bwd(0, 2): (
        (OUT, 0, GRAD1),
        (UP, 0, GRAD0),
        (DOWN, 1, RELAY),
        (KV, 1, ADD1),
        (KV, 1, ADD0),
        (UP, 0, START1),
        (OUT, 1, START0),
    ),
    bwd(0, 3): (
        (DOWN, 0, ADD1),
        (OUT, 0, START0),
        (C, 1, ADD0),
        (Q, 1, ADD0),
    ),
    bwd(0, 4): (
        (OUT, 1, ADD0),
        (UP, 0, START0),
        (C, 1, ADD1),
        (DOWN, 0, START0),
    ),
    bwd(0, 5): (
        (UP, 1, RELAY),
        (KV, 1, RELAY),
        (OUT, 1, TURN),
    ),
    bwd(0, 6): (
        (Q, 1, TURN),
        (OUT, 0, START1),
    ),
    bwd(0, 7): (
        (Q, 0, START1),
        (UP, 0, ADD1),
        (C, 1, TURN),
        (Q, 0, START0),
    ),
    bwd(0, 8): (
        (DOWN, 0, ADD0),
        (DOWN, 0, TURN),
        (KV, 0, START1),
    ),
    bwd(0, 9): (
        (C, 0, START1),
        (OUT, 1, RELAY),
        (Q, 1, RELAY),
        (DOWN, 0, RELAY),
        (KV, 0, START0),
        (OUT, 0, ADD1),
        (OUT, 0, ADD0),
        (UP, 0, ADD0),
        (MIXED, 0, HOP),
        (UP, 0, TURN),
    ),
    bwd(0, 10): (
        (KV, 0, ADD1),
        (C, 1, RELAY),
        (UP, 1, END),
        (OUT, 0, TURN),
        (C, 0, ADD1),
        (Q, 0, ADD1),
    ),
    bwd(0, 11): (
        (UP, 0, RELAY),
        (KV, 1, TURN),
    ),
    TAIL: (
        (GAINS, 0, START),
        (TOKENS, 0, START),
        (DOWN, 0, END),
        (OUT, 0, RELAY),
        (C, 0, START0),
        (KV, 0, ADD0),
        (Q, 0, ADD0),
        (KV, 0, TURN),
        (Q, 0, TURN),
        (KV, 1, END),
        (MIXED, 0, END),
        (KV, 0, RELAY),
        (Q, 1, END),
        (C, 0, ADD0),
        (C, 0, TURN),
        (GAINS, 0, HOP),
        (DOWN, 1, TURN),
        (Q, 0, RELAY),
        (C, 1, END),
        (UP, 0, END),
        (OUT, 0, END),
        (OUT, 1, END),
        (C, 0, RELAY),
        (TOKENS, 0, HOP),
        (GAINS, 0, END),
        (KV, 0, END),
        (Q, 0, END),
        (DOWN, 1, END),
        (C, 0, END),
        (TOKENS, 0, END),
    ),
}


def kernel(
    n_seq,
    layers,
    tok_hbm,
    cot_hbm,
    len_ref,
    qkv_hbm,
    ctrl_hbm,
    up_hbm,
    down_hbm,
    out_hbm,
    norm_attn_hbm,
    norm_ffn_hbm,
    mixed_hbm,
    gt_hbm,
    gqkv_hbm,
    gctrl_hbm,
    gout_hbm,
    gup_hbm,
    gdown_hbm,
    gn_hbm,
    H,
    MID,
    AB,
    FB,
    QKV,
    WB,
    S2,
    ZS,
    PS,
    XS,
    AST,
    MST,
    OB,
    GU,
    GG,
    KP,
    VP,
    LOC,
    TOKB,
    GBF,
    DOB,
    DU,
    DMID,
    YST,
    DNB,
    DZ,
    DWF,
    WA,
    WF,
    GAIN,
    GROW,
    GFULL,
    ARS,
    ARR,
    SCS,
    SCR1,
    SCR2,
    SCP,
    RQ,
    RKV,
    RC,
    ROUT,
    RUP,
    RDN,
    LQ,
    LKV,
    LC,
    LOUT,
    LUP,
    LDN,
    OQKV,
    OCTRL,
    OOUT,
    OUP,
    ODN,
    GN,
    GNY,
    GNR,
    GNO,
    OUTB,
    send_sems,
    inner_sems,
    recv_sems,
    local_sems,
):
    T, D = TOKB.shape[1], TOKB.shape[2]
    tiles = T // TILE
    R = D // GROUPS
    stride = n_seq // GROUPS
    s = lax.axis_index("seq")
    m = lax.axis_index("mp")
    y, core = m // 2, m % 2
    g, lo = s // stride, s % stride
    x, z = g % 2, g // 2
    z1, z0 = z // 2, z % 2
    inner = z1 != z0
    last = layers - 1

    def flip_z(d):
        d1, d0 = d // 2, d % 2
        return 2 * (1 - z1 if d1 else z1) + (1 - z0 if d0 else z0)

    def seq_of(gx, gz):
        return (gz * 2 + gx) * stride + lo

    core_peer = (s, 2 * y + (1 - core))
    y_peer = (s, 2 * (1 - y) + core)
    x_peer = (seq_of(1 - x, z), m)
    z_peer = {d: (seq_of(x, flip_z(d)), m) for d in (1, 2, 3)}
    near = near_size(n_seq)
    blocks = n_seq // near
    low, high = s % near, s // near

    used = [0, 0, 0]
    leaving = {}

    def arrival():
        used[0] += 1
        return recv_sems.at[used[0] - 1]

    def remote(src, dst, peer, leave, arrive):
        return pltpu.make_async_remote_copy(
            src_ref=src,
            dst_ref=dst,
            send_sem=leave,
            recv_sem=arrive,
            device_id=peer,
            device_id_type=MESH,
        )

    def send(src, dst, peer, arrive=None):
        k = used[2] % SEND_RING
        used[2] += 1
        if k in leaving:
            leaving[k].wait_send()
        c = remote(src, dst, peer, send_sems.at[k], arrival() if arrive is None else arrive)
        c.start()
        leaving[k] = c
        return c

    def send_if_inner(src, dst, peer, arrive, leave):
        c = remote(src, dst, peer, leave, arrive)

        @pl.when(inner)
        def _():
            c.start()

        return c

    def leave_done(c):
        for k, other in list(leaving.items()):
            if other is c:
                c.wait_send()
                del leaving[k]

    def arrived(region, arrive):
        remote(region, region, core_peer, send_sems.at[0], arrive).wait_recv()

    def local(src, dst):
        k = used[1]
        used[1] += 1
        c = pltpu.make_async_copy(src, dst, local_sems.at[k])
        c.start()
        return c

    barrier = pltpu.get_barrier_semaphore()

    def hello(peer):
        pl.semaphore_signal(barrier, inc=1, device_id=peer, device_id_type=MESH)

    hello(core_peer)
    hello(y_peer)
    count = 2
    for d in range(1, near):
        hello((high * near + lax.rem(low + d, near), m))
        count += 1
    for d in range(1, blocks):
        other = lax.rem(high + d, blocks) * near
        hello((other + low, m))
        count += 1
        if stride == 1:
            hello((other + 1 - low, m))
            count += 1

    rows_in = [local(norm_attn_hbm, GROW.at[0]), local(norm_ffn_hbm, GROW.at[1])]
    own = []
    for l in range(layers):
        for k in range(4):
            src = qkv_hbm.at[l, k] if k < 3 else ctrl_hbm.at[l]
            own.append(local(src, WA.at[l, y, z, x, slice(None), pl.ds(k * 128, 128)]))
        lanes = 0
        for src in (up_hbm, down_hbm, out_hbm):
            at = pl.ds(lanes, src.shape[-1])
            own.append(local(src.at[l], WF.at[l, y, z, x, slice(None), at]))
            lanes += src.shape[-1]
    tok_copy = local(tok_hbm.at[y], TOKB.at[0])
    cot_copy = local(cot_hbm.at[y], TOKB.at[1])
    gain_sub = lax.broadcasted_iota(jnp.int32, (8, R), 0)
    own_gains = jnp.zeros((8, R), F32)
    for c in rows_in:
        c.wait()
    for l in range(layers):
        for k in range(2):
            row = GROW[k].astype(F32)[l : l + 1]
            own_gains = jnp.where(gain_sub == 2 * l + k, row, own_gains)
    GAIN[0, :, pl.ds(0, R)] = jnp.where(x == 0, own_gains, 0.0)
    GAIN[0, :, pl.ds(R, R)] = jnp.where(x == 0, 0.0, own_gains)

    pl.semaphore_wait(barrier, count)

    every = slice(None)

    inner_used = [0]
    inner_last = []

    def inner_leave():
        inner_used[0] += 1
        return inner_sems.at[inner_used[0] - 1]

    class Gather:
        def __init__(self, buf, l, low_end, cut, high_end, z_second):
            self.buf, self.l, self.c = buf, l, {}
            self.all = pl.ds(low_end, high_end - low_end)
            self.first, self.second = pl.ds(low_end, cut - low_end), pl.ds(cut, high_end - cut)
            self.z_second = z_second
            self.last = None
            self.inner = {}

        def along_z(self, kind, region, lanes=None):
            for d in (1, 2):
                self.push((kind, d), region, z_peer[d], lanes)
            src = self.buf.at[(self.l,) + region + (slice(None), lanes or self.all)]
            arrive, leave = arrival(), inner_leave()
            self.c[kind, 3] = send_if_inner(src, src, z_peer[3], arrive, leave)
            self.inner[kind] = (self.c[kind, 3], arrive, leave)

        def pass_on(self, kind, region, lanes=None):
            before, arrive, leave = self.inner[kind]

            @pl.when(inner)
            def _():
                before.wait_send()

            src = self.buf.at[(self.l,) + region + (slice(None), lanes or self.all)]
            inner_last.append(send_if_inner(src, src, z_peer[1], arrive, leave))

        def push(self, key, region, peer, lanes=None):
            src = self.buf.at[(self.l,) + region + (slice(None), lanes or self.all)]
            arrive = None
            if key[0] in (5, 6) and not self.z_second:
                self.last = self.last or {5: arrival(), 6: arrival()}
                arrive = self.last[key[0]]
            self.c[key] = send(src, src, peer, arrive)

        def take(self, *keys):
            for key in keys:
                self.c[key].wait_recv()

        def start(self):
            self.along_z(0, (y, z, x))

        def own(self):
            self.push((1, 0), (y, z, x), x_peer)
            self.push((2, 0), (y, z, x), y_peer)

        def on(self, d):
            if not self.z_second:
                self.take((0, d))
                if d == 2:
                    self.pass_on(0, (y, flip_z(d), x))
                self.push((1, d), (y, flip_z(d), x), x_peer)
                self.push((2, d), (y, flip_z(d), x), y_peer)
            elif d == 1:
                self.take((1, 0))
                self.along_z(3, (y, z, 1 - x), self.first)
                self.push((5, 0), (y, z, 1 - x), y_peer, self.first)
            elif d == 2:
                self.take((2, 0))
                self.along_z(4, (1 - y, z, x), self.second)
                self.push((6, 0), (1 - y, z, x), x_peer, self.second)

        def across(self, d):
            zz = flip_z(d)
            if not self.z_second:
                self.take((1, d))
                self.push((5, d), (y, zz, 1 - x), y_peer, self.first)
                self.take((2, d))
                self.push((6, d), (1 - y, zz, x), x_peer, self.second)
            elif d:
                self.take((0, d), (3, d))
                if d == 2:
                    self.pass_on(0, (y, zz, x))
                    self.pass_on(3, (y, zz, 1 - x), self.first)
                self.push((5, d), (y, zz, slice(None)), y_peer, self.first)
                self.take((4, d))
                if d == 2:
                    self.pass_on(4, (1 - y, zz, x), self.second)
                self.push((6, d), (slice(None), zz, x), x_peer, self.second)

        def end(self):
            if self.z_second:
                for d in range(4):
                    self.take((5, d), (6, d))
                return
            far = self.buf.at[self.l, 1 - y, every, 1 - x]
            arrived(far.at[:, :, self.first], self.last[5])
            arrived(far.at[:, :, self.second], self.last[6])

        def parts(self):
            part = {START: self.start, OWN: self.own, END: self.end}
            for d in (1, 2, 3):
                part[ON1 + d - 1] = functools.partial(self.on, d)
            for d in range(4):
                part[ACROSS0 + d] = functools.partial(self.across, d)
            return part

    gains_here = arrival()
    for d in (0, 1, 2, 3):
        for o in (0, 1):
            if (d, o) == (0, 0):
                continue
            peer = (seq_of(1 - x if o else x, flip_z(d)), m)
            send(GAIN.at[0], GAIN.at[d * 2 + o], peer, gains_here)
    for c in own:
        c.wait()
    jobs = {}
    for l in range(layers):
        for name, buf, bounds in (
            (MIXER, WA, (0, 256, 512)),
            (UPPER, WF, (0, 256, 512)),
            (LOWER, WF, (512, 896, 1152)),
        ):
            jobs[name, l] = Gather(buf, l, *bounds, (name, l) in GATHER_Z_SECOND).parts()

    def at(place):
        for name, l, part in PLAN.get(place, ()):
            jobs[name, l][part]()

    at(ENTRY)

    lane = lax.broadcasted_iota(jnp.int32, (TILE, 128), 1)
    first = lane < HEAD
    head_rows = [
        (lax.broadcasted_iota(jnp.int32, (1, 128), 1) < HEAD).astype(F32).astype(BF),
        (lax.broadcasted_iota(jnp.int32, (1, 128), 1) >= HEAD).astype(F32).astype(BF),
    ]
    rr = lax.broadcasted_iota(jnp.int32, (TILE, TILE), 0)
    cc = lax.broadcasted_iota(jnp.int32, (TILE, TILE), 1)
    lower = rr >= cc
    lower_ones = lower.astype(F32).astype(BF)
    upper_ones = (rr <= cc).astype(F32).astype(BF)
    diag = (lax.broadcasted_iota(jnp.int32, (128, 128), 0) < HEAD) == (
        lax.broadcasted_iota(jnp.int32, (128, 128), 1) < HEAD
    )

    def per_head(value):
        a = jnp.sum(jnp.where(first, value, 0.0), axis=-1, keepdims=True)
        b = jnp.sum(jnp.where(first, 0.0, value), axis=-1, keepdims=True)
        return jnp.where(first, a, b)

    def per_head_max(value):
        a = jnp.max(jnp.where(first, value, -jnp.inf), axis=-1, keepdims=True)
        b = jnp.max(jnp.where(first, -jnp.inf, value), axis=-1, keepdims=True)
        return jnp.where(first, a, b)

    def heads(value):
        return value * head_rows[0], value * head_rows[1]

    def tile_rows(i):
        return pl.ds(i * TILE, TILE)

    def weight(buf, l, p, start, width):
        return buf[l, p, :, :, :, pl.ds(start, width)].reshape(D, width)

    def mixer_weight(l, p):
        return weight(WA, l, p, 0, 512)

    def up_weight(l, p):
        return weight(WF, l, p, 0, 512)

    def down_weight(l, p):
        return weight(WF, l, p, 512, 512)

    def out_weight(l, p):
        return weight(WF, l, p, 1024, 128)

    shared = [0]
    share_sems = [[send_sems.at[SEND_RING + k] for k in range(ARS.shape[0])]]
    share_sems.append([arrival() for _ in range(ARR.shape[0])])
    share_prev = {}

    def share_start(value):
        k = shared[0]
        shared[0] += 1
        slot = k % ARS.shape[0]
        if slot in share_prev:
            share_prev[slot].wait_send()
        ARS[slot] = value.astype(BF)
        k = k % ARR.shape[0]
        c = remote(ARS.at[slot], ARR.at[k], core_peer, share_sems[0][slot], share_sems[1][k])
        c.start()
        share_prev[slot] = c
        return c, slot, k

    def share_end(handle):
        c, slot, k = handle
        c.wait_recv()
        return ARS[slot].astype(F32) + ARR[k].astype(F32)

    class Scan:
        def __init__(self, call, forward):
            self.call, self.forward = call, forward

        def pack_normalizer(self, which, part):
            sub = lax.broadcasted_iota(jnp.int32, (16, 128), 0)
            rest = jnp.zeros((16, 128), F32)
            for k in range(3):
                piece = part.astype(BF).astype(F32)
                rest = jnp.where(sub == k, piece, rest)
                part = part - piece
            SCS[which, pl.ds(128, 16)] = rest.astype(BF)

        def start(self, k_state, v_state, z_row):
            which = self.call
            SCS[which, pl.ds(0, 128)] = (k_state + pltpu.roll(v_state, HEAD, 1)).astype(BF)
            self.pack_normalizer(which, z_row)
            self.near = []
            for d in range(1, near):
                peer = (high * near + lax.rem(low + d, near), m)
                self.near.append(send(SCS.at[which], SCR1.at[self.call, d - 1], peer))

        def step(self):
            for c in self.near:
                c.wait_recv()
                leave_done(c)
            which = self.call
            both = SCS[which].astype(F32)
            for d in range(1, near):
                both = both + SCR1[self.call, d - 1].astype(F32)
            SCS[which, pl.ds(0, 128)] = both[:128].astype(BF)
            self.pack_normalizer(which, jnp.sum(both[128:131], axis=0, keepdims=True))
            self.links = []
            for d in range(1, blocks):
                to = high + d if self.forward else high - d
                frm = high - d if self.forward else high + d
                inside = to < blocks if self.forward else to >= 0
                comes = frm >= 0 if self.forward else frm < blocks
                target = jnp.where(inside, to, high)
                leave = send_sems.at[SEND_RING + ARS.shape[0] + (self.call % 2) * (blocks - 1) + d - 1]
                target = (target * near + low, m)
                c = remote(SCS.at[which], SCR2.at[self.call, d - 1], target, leave, arrival())

                @pl.when(inside)
                def _(c=c):
                    c.start()

                self.links.append((c, inside, comes))

        def end(self):
            acc = SCP.at[self.call % 2]
            before = jnp.zeros(acc.shape, F32)
            for d in range(1, near):
                mine = low >= d if self.forward else low < d
                before = before + jnp.where(mine, SCR1[self.call, d - 1].astype(F32), 0.0)
            acc[...] = before
            for d, (c, inside, comes) in enumerate(self.links):

                @pl.when(comes)
                def _(c=c, d=d):
                    c.wait_recv()
                    acc[...] += SCR2[self.call, d].astype(F32)

            for c, inside, comes in self.links:

                @pl.when(inside)
                def _(c=c):
                    c.wait_send()

            block = acc[pl.ds(0, 128)]
            k_state = jnp.where(diag, block, 0.0)
            v_state = pltpu.roll(jnp.where(diag, 0.0, block), HEAD, 1)
            return k_state, v_state, jnp.sum(acc[pl.ds(128, 3)], axis=0, keepdims=True)

    def add_to(buf, at, more):
        buf[at] = (buf[at].astype(F32) + more.astype(F32)).astype(BF)

    class Scatter:
        def __init__(self, buf, land, l, x_first, z_second):
            self.buf, self.land, self.l = buf, land, l
            self.x_first, self.z_second = x_first, z_second
            self.first_peer = x_peer if x_first else y_peer
            self.next_peer = y_peer if x_first else x_peer
            self.c = {}

        def block(self, first_other, next_other, zz=every):
            ox, oy = (first_other, next_other) if self.x_first else (next_other, first_other)
            return (self.l, 1 - y if oy else y, zz, 1 - x if ox else x)

        def start(self, o):
            src = self.buf.at[self.block(1, o)]
            self.c[0, o] = send(src, self.land.at[self.l, pl.ds(4 * o, 4)], self.first_peer)

        def add(self, o):
            self.c[0, o].wait_recv()
            add_to(self.buf, self.block(0, o), self.land[self.l, pl.ds(4 * o, 4)])
            if self.z_second:
                self.along_z(o, 7 + 3 * o, 15 + o)
            elif o:
                src = self.buf.at[self.block(0, o)]
                self.next = send(src, self.land.at[self.l, pl.ds(8, 4)], self.next_peer)

        def along_z(self, o, base, extra):
            near, far, through = arrival(), arrival(), arrival()
            self.c[1, o] = (near, far, through, base, extra)
            src = self.buf.at[self.block(0, o, flip_z(1))]
            send(src, self.land.at[self.l, base + 1], z_peer[1], near)
            src = self.buf.at[self.block(0, o, flip_z(3))]
            slot = jnp.where(inner, base + 3, extra)
            peer = (jnp.where(inner, z_peer[3][0], z_peer[1][0]), m)
            first = used[0] - 2
            send(src, self.land.at[self.l, slot], peer, recv_sems.at[jnp.where(inner, first, first + 1)])

        def relay_z(self, o):
            near, far, through, base, extra = self.c[1, o]

            @pl.when(inner)
            def _():
                arrived(self.land.at[self.l, extra], through)
                add_to(self.buf, self.block(0, o, flip_z(2)), self.land[self.l, extra])

            src = self.buf.at[self.block(0, o, flip_z(2))]
            send(src, self.land.at[self.l, base + 2], z_peer[2], near)

        def relay(self):
            for o in (1, 0) if self.z_second else (0,):
                self.relay_z(o)

        def sum_z(self, o):
            near, far, through, base, extra = self.c[1, o]
            at_ = self.block(0, o, z)

            @pl.when(inner)
            def _():
                arrived(self.land.at[self.l, base + 3], far)
                add_to(self.buf, at_, self.land[self.l, base + 3])

            arrived(self.land.at[self.l, pl.ds(base + 1, 2)], near)
            total = self.buf[at_].astype(F32) + self.land[self.l, base + 1].astype(F32)
            return total + self.land[self.l, base + 2].astype(F32)

        def turn(self):
            if self.z_second:
                for o in (1, 0):
                    self.buf[self.block(0, o, z)] = self.sum_z(o).astype(BF)
                    if o:
                        src = self.buf.at[self.block(0, o, z)]
                        self.c[2] = send(src, self.land.at[self.l, 14], self.next_peer)
                return
            self.next.wait_recv()
            for d in (1, 3, 2, 0):
                add_to(self.buf, self.block(0, 0, flip_z(d)), self.land[self.l, 8 + flip_z(d)])
                if d == 3:
                    self.along_z(0, 11, 15)

        def end(self):
            if not self.z_second:
                return self.sum_z(0)
            self.c[2].wait_recv()
            return self.buf[self.block(0, 0, z)].astype(F32) + self.land[self.l, 14].astype(F32)

    finals = []

    def finish(l, name):
        total = scatters[name, l].end()
        if name == UP:
            OUP[l] = total
            finals.append(local(OUP.at[l], gup_hbm.at[l]))
        elif name == DOWN:
            ODN[l] = total
            finals.append(local(ODN.at[l], gdown_hbm.at[l]))
        elif name == OUT:
            OOUT[l] = total
            finals.append(local(OOUT.at[l], gout_hbm.at[l]))
        elif name == Q:
            OQKV[l, 0] = total
            finals.append(local(OQKV.at[l, 0], gqkv_hbm.at[l, 0]))
        elif name == KV:
            OQKV[l, 1] = total[:, :128]
            OQKV[l, 2] = total[:, 128:]
            finals.append(local(OQKV.at[l, pl.ds(1, 2)], gqkv_hbm.at[l, pl.ds(1, 2)]))
        else:
            OCTRL[l] = total
            finals.append(local(OCTRL.at[l], gctrl_hbm.at[l]))

    def split_rows(value):
        return value.astype(BF).reshape(4, 2, R, value.shape[-1])

    def grad_up(l, o):
        yy = 1 - y if o else y
        RUP[l, yy] = split_rows(tn(FB[l], DU[yy]))

    def grad_down(l, o):
        yy = 1 - y if o else y
        RDN[l, yy] = split_rows(tn(GBF[...], GG[l, yy]))

    def grad_out(l):
        grads = tn(GBF[...], OB[l])
        for p in range(2):
            ROUT[l, p] = split_rows(grads[:, p * 128 : (p + 1) * 128])

    scatters = {}
    for l in range(layers):
        for name, buf, land in (
            (Q, RQ, LQ),
            (KV, RKV, LKV),
            (C, RC, LC),
            (OUT, ROUT, LOUT),
            (UP, RUP, LUP),
            (DOWN, RDN, LDN),
        ):
            f = Scatter(buf, land, l, (name, l) in X_FIRST, (name, l) in Z_SECOND)
            scatters[name, l] = f
            jobs[name, l] = {
                START1: functools.partial(f.start, 1),
                START0: functools.partial(f.start, 0),
                ADD1: functools.partial(f.add, 1),
                ADD0: functools.partial(f.add, 0),
                TURN: f.turn,
                RELAY: f.relay,
                END: functools.partial(finish, l, name),
            }
        for name, f in ((UP, grad_up), (DOWN, grad_down)):
            jobs[name, l][GRAD1] = functools.partial(f, l, 1)
            jobs[name, l][GRAD0] = functools.partial(f, l, 0)
        jobs[OUT, l][GRAD1] = functools.partial(grad_out, l)

    tok_copy.wait()
    cot_copy.wait()
    arrived(GAIN.at[pl.ds(1, 7)], gains_here)
    for gz in range(GROUPS // 2):
        total = jnp.zeros((8, 128), F32)
        for d in range(4):
            here = flip_z(d) == gz
            total = total + jnp.where(here, GAIN[2 * d] + GAIN[2 * d + 1], 0.0)
        GFULL[:, pl.ds(gz * 128, 128)] = total

    def gain_row(l, which):
        return GFULL[pl.ds(2 * l + which, 1), :]

    def stream(l, rows):
        return TOKB[0, rows].astype(F32) if l == 0 else H[l - 1, rows]

    def attn_norm(l, i):
        rows = tile_rows(i)
        y_hat, _ = norm_parts(stream(l, rows))
        AB[l, rows] = (y_hat * gain_row(l, 0)).astype(BF)

    for i in range(tiles):
        attn_norm(0, i)

    length = len_ref[y]

    def valid_rows(i):
        row = lax.broadcasted_iota(jnp.int32, (TILE, 1), 0)
        return jnp.where(s * T + i * TILE + row < length, 1.0, 0.0)

    for i in range(tiles):
        rows = tile_rows(i)
        dh = TOKB[1, rows].astype(F32) * valid_rows(i)
        DMID[rows] = dh
        GBF[rows] = dh.astype(BF)

    at(FIRST)

    for l in range(layers):
        more_layers = l + 1 < layers
        at(fwd(l, 0))
        scans = [Scan(2 * l + p, True) for p in range(2)]

        def project_pair(p, l=l):
            out = nn(AB[l], mixer_weight(l, p))
            kv = out[:, 128:384].astype(BF)
            th = jnp.tanh(out[:, 384:] * (1.0 / 16.0))
            w = jnp.exp(16.0 * th).astype(BF)
            sums = [
                (
                    tn(w[j * TILE : (j + 1) * TILE], kv[j * TILE : (j + 1) * TILE]),
                    jnp.sum(w[j * TILE : (j + 1) * TILE].astype(F32), axis=0, keepdims=True),
                )
                for j in range(tiles)
            ]
            ks, vs, zs = 0.0, 0.0, 0.0
            for j, (both, z_j) in enumerate(sums):
                k_j = jnp.where(diag, both[:, :128], 0.0)
                v_j = jnp.where(diag, both[:, 128:], 0.0)
                if j < tiles - 1:
                    LOC[p, j, 0] = k_j
                    LOC[p, j, 1] = v_j
                ks, vs, zs = ks + k_j, vs + v_j, zs + z_j
            QKV[l, p, :, pl.ds(0, 128)] = out[:, :128].astype(BF)
            QKV[l, p, :, pl.ds(128, 256)] = kv
            WB[l, p] = w
            S2[l, p] = (1.0 - th * th).astype(BF)
            return ks, vs, zs

        def inside_block(p, l=l):
            units = range(tiles)
            w = [WB[l, p, tile_rows(j)] for j in units]
            q = [QKV[l, p, tile_rows(j), pl.ds(0, 128)] for j in units]
            k = [QKV[l, p, tile_rows(j), pl.ds(128, 128)] for j in units]
            qs = [heads(q[j]) for j in units]
            a = [[jnp.where(lower, nt(qs[j][h], k[j]), 0.0).astype(BF) for h in (0, 1)] for j in units]
            sums = [nn(lower_ones, w[j]) for j in units]
            ws = [heads(w[j]) for j in units]
            num = [nn(a[j][0], ws[j][0]) + nn(a[j][1], ws[j][1]) for j in units]
            for j in units:
                for h in (0, 1):
                    AST[l, p, j, h] = a[j][h]
                ZS[l, p, tile_rows(j)] = sums[j]
                XS[l, p, tile_rows(j)] = num[j]

        def with_earlier(states, l=l):
            units = [(p, j) for p in range(2) for j in range(tiles)]
            ks, vs, z_before = {}, {}, {}
            for p, j in units:
                if j == 0:
                    k_pre, v_pre, z_pre = states[p]
                else:
                    k_pre = k_pre + LOC[p, j - 1, 0]
                    v_pre = v_pre + LOC[p, j - 1, 1]
                    z_pre = z_pre + jnp.sum(
                        WB[l, p, tile_rows(j - 1)].astype(F32), axis=0, keepdims=True
                    )
                ks[p, j], vs[p, j], z_before[p, j] = k_pre.astype(BF), v_pre.astype(BF), z_pre
            w = {(p, j): WB[l, p, tile_rows(j)] for p, j in units}
            q = {(p, j): QKV[l, p, tile_rows(j), pl.ds(0, 128)] for p, j in units}
            v = {(p, j): QKV[l, p, tile_rows(j), pl.ds(256, 128)] for p, j in units}
            inv = {(p, j): 1.0 / (ZS[l, p, tile_rows(j)] + z_before[p, j]) for p, j in units}
            num = {(p, j): XS[l, p, tile_rows(j)] for p, j in units}
            xs = {u: (num[u] + nt(q[u], ks[u])) * inv[u] * 0.125 for u in units}
            e = {u: jnp.exp(xs[u] - per_head_max(xs[u])) for u in units}
            prob = {u: e[u] / per_head(e[u]) for u in units}
            scaled = {u: (prob[u] * inv[u]).astype(BF) for u in units}
            rs = {u: heads(scaled[u]) for u in units}
            mm = {
                u: [jnp.where(lower, nt(rs[u][h], w[u]), 0.0).astype(BF) for h in (0, 1)]
                for u in units
            }
            vh = {u: heads(v[u]) for u in units}
            out = {
                u: nn(scaled[u], vs[u]) + nn(mm[u][0], vh[u][0]) + nn(mm[u][1], vh[u][1])
                for u in units
            }
            for p, j in units:
                rows = tile_rows(j)
                KP[l, p, j] = ks[p, j]
                VP[l, p, j] = vs[p, j]
                ZS[l, p, rows] = inv[p, j]
                XS[l, p, rows] = xs[p, j]
                PS[l, p, rows] = prob[p, j]
                for h in (0, 1):
                    MST[l, p, j, h] = mm[p, j][h]
                OB[l, rows, pl.ds(p * 128, 128)] = out[p, j].astype(BF)

        for p in range(2):
            scans[p].start(*project_pair(p))
            at(fwd(l, 1 + p))
        for p in range(2):
            inside_block(p)
            at(fwd(l, 3 + 2 * p))
            scans[p].step()
            at(fwd(l, 4 + 2 * p))
        with_earlier([scans[0].end(), scans[1].end()])
        at(fwd(l, 7))

        handles = []
        for i in range(tiles):
            rows = tile_rows(i)
            part = nt(OB[l, rows, pl.ds(0, 128)], out_weight(l, 0))
            part = part + nt(OB[l, rows, pl.ds(128, 128)], out_weight(l, 1))
            handles.append(share_start(part))
        at(fwd(l, 8))
        more = []
        for i in range(tiles):
            rows = tile_rows(i)
            mid = stream(l, rows) + share_end(handles[i])
            y_hat, _ = norm_parts(mid)
            f = (y_hat * gain_row(l, 1)).astype(BF)
            hidden = [nn(f, up_weight(l, p)) for p in range(2)]
            gates = [gate_and_slope(u) for u in hidden]
            low_gates = [gate.astype(BF) for gate, _ in gates]
            if more_layers:
                part = nt(low_gates[0], down_weight(l, 0)) + nt(low_gates[1], down_weight(l, 1))
                more.append(share_start(part))
            MID[l, rows] = mid
            FB[l, rows] = f
            slopes = GU.at[l] if more_layers else DU
            for p in range(2):
                GG[l, p, rows] = low_gates[p]
                slopes[p, rows] = gates[p][1].astype(BF)
            at(fwd(l, 9 + i))
        if not more_layers:
            for i in range(tiles):
                rows = tile_rows(i)
                gb = GBF[rows]
                du = [
                    (nn(gb, down_weight(l, p)) * DU[p, rows].astype(F32)).astype(BF)
                    for p in range(2)
                ]
                part = nt(du[0], up_weight(l, 0)) + nt(du[1], up_weight(l, 1))
                more.append(share_start(part))
                for p in range(2):
                    DU[p, rows] = du[p]
        if more_layers:
            for i in range(tiles):
                rows = tile_rows(i)
                H[l, rows] = MID[l, rows] + share_end(more[i])
                attn_norm(l + 1, i)
            at(fwd(l, 11))

    half_rows = pl.ds(pl.multiple_of(core * (T // 2), T // 2), T // 2)

    class Spread:
        def __init__(self, k, out):
            self.k, self.out = k, out

        def start(self):
            src = OUTB.at[self.k, y, half_rows]
            self.c = send(src, src, y_peer)

        def hop(self):
            self.c.wait_recv()
            src = OUTB.at[self.k, 1 - y, half_rows]
            self.c = send(src, src, core_peer)

        def end(self):
            self.c.wait_recv()
            finals.append(local(OUTB.at[self.k], self.out))

    for name, f in ((MIXED, Spread(0, mixed_hbm)), (TOKENS, Spread(1, gt_hbm))):
        jobs[name, 0] = {START: f.start, HOP: f.hop, END: f.end}

    grad_norm = [None] * (2 * layers)

    for l in range(last, -1, -1):
        if l == last:
            at(bwd(l, 0))
            handles = more
        else:
            for i in range(tiles):
                GBF[tile_rows(i)] = DMID[tile_rows(i)].astype(BF)
            at(bwd(l, 0))
            handles = []
            for i in range(tiles):
                rows = tile_rows(i)
                gb = GBF[rows]
                du = [
                    (nn(gb, down_weight(l, p)) * GU[l, p, rows].astype(F32)).astype(BF)
                    for p in range(2)
                ]
                part = nt(du[0], up_weight(l, 0)) + nt(du[1], up_weight(l, 1))
                handles.append(share_start(part))
                for p in range(2):
                    DU[p, rows] = du[p]
        at(bwd(l, 1))
        gsum = jnp.zeros((1, D), F32)
        for i in range(tiles):
            rows = tile_rows(i)
            df = share_end(handles[i])
            y_hat, rstd = norm_parts(MID[l, rows])
            gsum = gsum + jnp.sum(df * y_hat, axis=0, keepdims=True)
            df = df * gain_row(l, 1)
            dm = DMID[rows] + (
                df
                - jnp.mean(df, axis=-1, keepdims=True)
                - y_hat * jnp.mean(df * y_hat, axis=-1, keepdims=True)
            ) * rstd
            DMID[rows] = dm
            GBF[rows] = dm.astype(BF)
            for p in range(2):
                DOB[p, rows] = nn(GBF[rows], out_weight(l, p)).astype(BF)
        grad_norm[2 * l + 1] = gsum
        at(bwd(l, 2))

        scans = [Scan(2 * layers + 2 * (last - l) + k, False) for k in range(2)]
        order = (1 - y, y)

        def to_states(l=l):
            units = [(k, j) for k in range(2) for j in range(tiles - 1, -1, -1)]
            rows = {u: tile_rows(u[1]) for u in units}
            w = {(k, j): WB[l, order[k], rows[k, j]] for k, j in units}
            q = {(k, j): QKV[l, order[k], rows[k, j], pl.ds(0, 128)] for k, j in units}
            v = {(k, j): QKV[l, order[k], rows[k, j], pl.ds(256, 128)] for k, j in units}
            do = {(k, j): DOB[order[k], rows[k, j]] for k, j in units}
            inv = {(k, j): ZS[l, order[k], rows[k, j]] for k, j in units}
            prob = {(k, j): PS[l, order[k], rows[k, j]] for k, j in units}
            xs = {(k, j): XS[l, order[k], rows[k, j]] for k, j in units}
            v_pre = {(k, j): VP[l, order[k], j] for k, j in units}
            ws = {u: heads(w[u]) for u in units}
            dos = {u: heads(do[u]) for u in units}
            pair = {
                u: [jnp.where(lower, nt(dos[u][h], v[u]), 0.0).astype(BF) for h in (0, 1)]
                for u in units
            }
            dr = {
                u: nt(do[u], v_pre[u]) + nn(pair[u][0], ws[u][0]) + nn(pair[u][1], ws[u][1])
                for u in units
            }
            dp = {u: dr[u] * inv[u] for u in units}
            dx = {u: prob[u] * (dp[u] - per_head(dp[u] * prob[u])) for u in units}
            dn = {u: (dx[u] * inv[u] * 0.125).astype(BF) for u in units}
            r = {u: (prob[u] * inv[u]).astype(BF) for u in units}
            dz = {
                u: -(r[u].astype(F32) * dp[u]) - 8.0 * dn[u].astype(F32) * xs[u] for u in units
            }
            dk = {u: jnp.where(diag, tn(dn[u], q[u]), 0.0) for u in units}
            dv = {u: jnp.where(diag, tn(r[u], do[u]), 0.0) for u in units}
            totals = []
            for k in range(2):
                total = [0.0, 0.0, 0.0]
                for j in range(tiles):
                    dzs = jnp.sum(dz[k, j], axis=0, keepdims=True)
                    total = [a + b for a, b in zip(total, (dk[k, j], dv[k, j], dzs))]
                totals.append(total)
            for k, j in units:
                p = order[k]
                for h in (0, 1):
                    YST[p, j, h] = pair[k, j][h]
                DNB[p, rows[k, j]] = dn[k, j]
                DZ[p, rows[k, j]] = dz[k, j]
                if j > 0:
                    LOC[p, j - 1, 0] = dk[k, j]
                    LOC[p, j - 1, 1] = dv[k, j]
            return totals

        def within(p, l=l):
            units = range(tiles)
            rows = [tile_rows(j) for j in units]
            w = [WB[l, p, rows[j]] for j in units]
            q = [QKV[l, p, rows[j], pl.ds(0, 128)] for j in units]
            k = [QKV[l, p, rows[j], pl.ds(128, 128)] for j in units]
            do = [DOB[p, rows[j]] for j in units]
            dn = [DNB[p, rows[j]] for j in units]
            r = [(PS[l, p, rows[j]] * ZS[l, p, rows[j]]).astype(BF) for j in units]
            dz = [DZ[p, rows[j]] for j in units]
            k_pre = [KP[l, p, j] for j in units]
            dz_hi = [dz[j].astype(BF) for j in units]
            dz_lo = [(dz[j] - dz_hi[j].astype(F32)).astype(BF) for j in units]
            dns, rs, dos, qs, ks = ([heads(a[j]) for j in units] for a in (dn, r, do, q, k))
            da = [
                [jnp.where(lower, nt(dns[j][h], w[j]), 0.0).astype(BF) for h in (0, 1)]
                for j in units
            ]
            dq = [
                nn(dn[j], k_pre[j]) + nn(da[j][0], ks[j][0]) + nn(da[j][1], ks[j][1]) for j in units
            ]
            dk = [tn(da[j][0], qs[j][0]) + tn(da[j][1], qs[j][1]) for j in units]
            dv = [
                tn(MST[l, p, j, 0], dos[j][0]) + tn(MST[l, p, j, 1], dos[j][1]) for j in units
            ]
            dw = [
                nn(upper_ones, dz_hi[j])
                + nn(upper_ones, dz_lo[j])
                + tn(YST[p, j, 0], rs[j][0])
                + tn(AST[l, p, j, 0], dns[j][0])
                + tn(YST[p, j, 1], rs[j][1])
                + tn(AST[l, p, j, 1], dns[j][1])
                for j in units
            ]
            for j in units:
                DU[p, rows[j], pl.ds(0, 128)] = dq[j].astype(BF)
                DWF[p, rows[j], pl.ds(0, 128)] = dk[j]
                DWF[p, rows[j], pl.ds(128, 128)] = dv[j]
                DWF[p, rows[j], pl.ds(256, 128)] = dw[j]

        def with_later(k, p, l=l):
            k_post, v_post, z_after = scans[k].end()
            for j in range(tiles - 1, -1, -1):
                rows = tile_rows(j)
                if j < tiles - 1:
                    k_post = k_post + LOC[p, j, 0]
                    v_post = v_post + LOC[p, j, 1]
                    z_after = z_after + jnp.sum(DZ[p, tile_rows(j + 1)], axis=0, keepdims=True)
                kb, vb = k_post.astype(BF), v_post.astype(BF)
                w = WB[l, p, rows]
                key = QKV[l, p, rows, pl.ds(128, 128)]
                v = QKV[l, p, rows, pl.ds(256, 128)]
                dk = DWF[p, rows, pl.ds(0, 128)] + nn(w, kb)
                dv = DWF[p, rows, pl.ds(128, 128)] + nn(w, vb)
                dw = DWF[p, rows, pl.ds(256, 128)] + nt(key, kb) + nt(v, vb) + z_after
                dc = dw * w.astype(F32) * S2[l, p, rows].astype(F32)
                DU[p, rows, pl.ds(128, 128)] = dk.astype(BF)
                DU[p, rows, pl.ds(256, 128)] = dv.astype(BF)
                DU[p, rows, pl.ds(384, 128)] = dc.astype(BF)

        totals = to_states()
        for k in range(2):
            scans[k].start(*totals[k])
        if l == last:
            outs = []
            for i in range(tiles):
                rows = tile_rows(i)
                part = nt(GG[l, 0, rows], down_weight(l, 0)) + nt(GG[l, 1, rows], down_weight(l, 1))
                outs.append(share_start(part))
        at(bwd(l, 3))
        for k in range(2):
            scans[k].step()
            at(bwd(l, 4 + k))
        for k in range(2):
            p = order[k]
            within(p)
            RQ[l, p] = split_rows(tn(AB[l], DU[p, :, pl.ds(0, 128)]))
            if l == last and k == 0:
                for i in range(tiles):
                    rows = tile_rows(i)
                    out = MID[l, rows] + share_end(outs[i])
                    OUTB[0, y, rows] = (out * valid_rows(i)).astype(BF)
            at(bwd(l, 6 + k))
        for k in range(2):
            p = order[k]
            with_later(k, p)
            grads = split_rows(tn(AB[l], DU[p, :, pl.ds(128, 384)]))
            RKV[l, p] = grads[..., :256]
            RC[l, p] = grads[..., 256:]
            at(bwd(l, 8 + k))
        handles = []
        for i in range(tiles):
            rows = tile_rows(i)
            part = nt(DU[0, rows], mixer_weight(l, 0))
            part = part + nt(DU[1, rows], mixer_weight(l, 1))
            handles.append(share_start(part))
        at(bwd(l, 10))
        gsum = jnp.zeros((1, D), F32)
        for i in range(tiles):
            rows = tile_rows(i)
            da = share_end(handles[i])
            y_hat, rstd = norm_parts(stream(l, rows))
            gsum = gsum + jnp.sum(da * y_hat, axis=0, keepdims=True)
            da = da * gain_row(l, 0)
            dh = DMID[rows] + (
                da
                - jnp.mean(da, axis=-1, keepdims=True)
                - y_hat * jnp.mean(da * y_hat, axis=-1, keepdims=True)
            ) * rstd
            DMID[rows] = dh
            if l == 0:
                OUTB[1, y, rows] = dh.astype(BF)
        grad_norm[2 * l] = gsum
        at(bwd(l, 11))

    class Gains:
        def start(self):
            sub = lax.broadcasted_iota(jnp.int32, (8, D), 0)
            self.rows = jnp.zeros((8, D), F32)
            for k in range(2 * layers):
                self.rows = jnp.where(sub == k, grad_norm[k], self.rows)
            GN[...] = self.rows
            self.c = send(GN, GNY, y_peer)

        def hop(self):
            self.c.wait_recv()
            both = self.rows + GNY[...]
            for gz in range(GROUPS // 2):
                GNR[0, gz] = both[:, gz * 128 : (gz + 1) * 128]
            self.c = arrival()
            for d in range(4):
                for o in range(2):
                    if (d, o) == (0, 0):
                        continue
                    peer = (seq_of(1 - x if o else x, flip_z(d)), m)
                    k = 2 * d + o
                    send(GNR.at[0, flip_z(d)], GNR.at[1, k], peer, self.c)

        def end(self):
            total = GNR[0, z]
            arrived(GNR.at[1, pl.ds(1, 7)], self.c)
            for k in range(1, 8):
                total = total + GNR[1, k]
            GNO[...] = total
            finals.append(local(GNO, gn_hbm))

    f = Gains()
    jobs[GAINS, 0] = {START: f.start, HOP: f.hop, END: f.end}
    at(TAIL)
    for c in finals:
        c.wait()
    for c in (*leaving.values(), *share_prev.values()):
        c.wait_send()
    for c in inner_last:

        @pl.when(inner)
        def _(c=c):
            c.wait_send()

    assert used[0] == recv_sems.shape[0] and used[1] == local_sems.shape[0], used
    assert inner_used[0] == inner_sems.shape[0], inner_used


def lay_out(stride, *refs):
    mixed, tokens, qkv, ctrl, out, up, down, gains = refs[:8]
    mixed_out, tokens_out, attn_out, ffn_out, *weights_out = refs[8:17]
    wide, sems, *held = refs[17:]
    arrays = (tokens, mixed, up, down, qkv, ctrl, out)
    results = (None, mixed_out, weights_out[3], weights_out[4], *weights_out[:3])
    parts = [(k, b) for k in range(2) for b in range(2)] + [(k, None) for k in range(2, len(arrays))]

    def part(ref, b):
        return ref if b is None else ref.at[b]

    ins = {
        (k, b): pltpu.make_async_copy(part(arrays[k], b), part(held[k], b), sems.at[0, j])
        for j, (k, b) in enumerate(parts)
    }
    for c in ins.values():
        c.start()
    x = (lax.axis_index("seq") // stride) % 2
    R = attn_out.shape[1]
    rows = jnp.where(x == 0, gains[:, pl.ds(0, R)], gains[:, pl.ds(R, R)])
    for l in range(attn_out.shape[0]):
        attn_out[pl.ds(l, 1), :] = rows[2 * l : 2 * l + 1]
        ffn_out[pl.ds(l, 1), :] = rows[2 * l + 1 : 2 * l + 2]
    outs = []
    for j, (k, b) in enumerate(parts):
        ins[k, b].wait()
        if k == 0:
            wide[b] = held[0][b].astype(F32)
            c = pltpu.make_async_copy(wide.at[b], tokens_out.at[b], sems.at[1, j])
        else:
            c = pltpu.make_async_copy(part(held[k], b), part(results[k], b), sems.at[1, j])
        c.start()
        outs.append(c)
    for c in outs:
        c.wait()


def shards(tokens, lengths, norm_attn, norm_ffn, w_qkv, w_ctrl, w_out, w_up, w_down, cotangent):
    layers = w_qkv.shape[0]
    n_seq = lax.axis_size("seq")
    stride = n_seq // GROUPS
    _, T, D = tokens.shape
    rows = w_qkv.shape[1]
    weights = [w_qkv.transpose(0, 2, 1, 3), w_ctrl, w_up, w_down, w_out]
    gains = [norm_attn, norm_ffn]
    blocks = [[k * stride + j for j in range(stride)] for k in range(GROUPS)]
    if stride > 1:

        def fill(a, dim=1):
            return lax.all_gather(a, "seq", axis=dim, tiled=True, axis_index_groups=blocks)

        weights = [fill(a, a.ndim - 2) for a in weights]
        gains = [fill(a) for a in gains]
    R = D // GROUPS
    A = 3 * w_qkv.shape[-1] + w_ctrl.shape[-1]
    U = w_up.shape[-1]
    F = 2 * U + w_out.shape[-1]
    near = near_size(n_seq)
    far = n_seq // near
    tiles = T // TILE
    arrivals = 1 + sum(19 if (n, l) in GATHER_Z_SECOND else 13 for n in range(3) for l in range(layers))
    arrivals += 2 * tiles + 4 * layers * (near + far - 2)
    arrivals += sum(9 if (n, l) in Z_SECOND else 6 for n in range(Q, DOWN + 1) for l in range(layers))
    inner_copies = sum(3 if (n, l) in GATHER_Z_SECOND else 1 for n in range(3) for l in range(layers))
    arrivals += 4 + 2
    bf, f32 = BF, F32
    v = pltpu.VMEM
    scratch = [
        v((max(layers - 1, 1), T, D), f32),
        v((layers, T, D), f32),
        v((layers, T, D), bf),
        v((layers, T, D), bf),
        v((layers, 2, T, 384), bf),
        v((layers, 2, T, 128), bf),
        v((layers, 2, T, 128), bf),
        v((layers, 2, T, 128), f32),
        v((layers, 2, T, 128), f32),
        v((layers, 2, T, 128), f32),
        v((layers, 2, tiles, 2, TILE, TILE), bf),
        v((layers, 2, tiles, 2, TILE, TILE), bf),
        v((layers, T, 256), bf),
        v((max(layers - 1, 1), 2, T, U), bf),
        v((layers, 2, T, U), bf),
        v((layers, 2, tiles, 128, 128), bf),
        v((layers, 2, tiles, 128, 128), bf),
        v((2, max(tiles - 1, 1), 2, 128, 128), f32),
        v((2, T, D), bf),
        v((T, D), bf),
        v((2, T, 128), bf),
        v((2, T, U), bf),
        v((T, D), f32),
        v((2, tiles, 2, TILE, TILE), bf),
        v((2, T, 128), bf),
        v((2, T, 128), f32),
        v((2, T, 384), f32),
        v((layers, 2, 4, 2, R, A), bf),
        v((layers, 2, 4, 2, R, F), bf),
        v((8, 8, 128), f32),
        v((2, layers, R), bf),
        v((8, D), f32),
        v((tiles, TILE, D), bf),
        v((2 * tiles, TILE, D), bf),
        v((4 * layers, 144, 128), bf),
        v((4 * layers, near - 1, 144, 128), bf),
        v((4 * layers, far - 1, 144, 128), bf),
        v((2, 144, 128), f32),
        v((layers, 2, 4, 2, R, 128), bf),
        v((layers, 2, 4, 2, R, 256), bf),
        v((layers, 2, 4, 2, R, 128), bf),
        v((layers, 2, 4, 2, R, 128), bf),
        v((layers, 2, 4, 2, R, U), bf),
        v((layers, 2, 4, 2, R, U), bf),
        v((layers, 17, R, 128), bf),
        v((layers, 17, R, 256), bf),
        v((layers, 17, R, 128), bf),
        v((layers, 17, R, 128), bf),
        v((layers, 17, R, U), bf),
        v((layers, 17, R, U), bf),
        v((layers, 3, R, 128), f32),
        v((layers, R, 128), f32),
        v((layers, R, 128), f32),
        v((layers, R, U), f32),
        v((layers, R, U), f32),
        v((8, D), f32),
        v((8, D), f32),
        v((2, 8, 8, 128), f32),
        v((8, 128), f32),
        v((2, 2, T, D), bf),
        pltpu.SemaphoreType.DMA((SEND_RING + tiles + 2 * (far - 1),)),
        pltpu.SemaphoreType.DMA((inner_copies,)),
        pltpu.SemaphoreType.DMA((arrivals,)),
        pltpu.SemaphoreType.DMA((7 + 13 * layers,)),
    ]
    any_spec = pl.BlockSpec(memory_space=pl.ANY)
    out_shape = (
        jax.ShapeDtypeStruct((2, T, D), bf),
        jax.ShapeDtypeStruct((2, T, D), bf),
        jax.ShapeDtypeStruct((layers, 3, R, 128), f32),
        jax.ShapeDtypeStruct((layers, R, 128), f32),
        jax.ShapeDtypeStruct((layers, R, 128), f32),
        jax.ShapeDtypeStruct((layers, R, U), f32),
        jax.ShapeDtypeStruct((layers, R, U), f32),
        jax.ShapeDtypeStruct((8, 128), f32),
    )
    mixed, grad_tokens, *grads, gn = pl.pallas_call(
        functools.partial(kernel, n_seq, layers),
        out_shape=out_shape,
        in_specs=[
            any_spec,
            any_spec,
            pl.BlockSpec(memory_space=pltpu.SMEM),
            *[any_spec] * 7,
        ],
        out_specs=(any_spec,) * len(out_shape),
        scratch_shapes=scratch,
        compiler_params=pltpu.CompilerParams(
            collective_id=0, has_side_effects=True, vmem_limit_bytes=VMEM_BYTES
        ),
    )(tokens, cotangent, lengths, *weights, *gains)
    out_shape = (
        jax.ShapeDtypeStruct((2, T, D), bf),
        jax.ShapeDtypeStruct((2, T, D), f32),
        jax.ShapeDtypeStruct((layers, R), f32),
        jax.ShapeDtypeStruct((layers, R), f32),
        *[jax.ShapeDtypeStruct(a.shape, f32) for a in grads],
    )
    vmem_spec = pl.BlockSpec(memory_space=pltpu.VMEM)
    mixed, grad_tokens, *grads = pl.pallas_call(
        functools.partial(lay_out, stride),
        out_shape=out_shape,
        in_specs=[any_spec] * 7 + [vmem_spec],
        out_specs=(any_spec, any_spec, vmem_spec, vmem_spec) + (any_spec,) * 5,
        scratch_shapes=[
            v((2, T, D), f32),
            pltpu.SemaphoreType.DMA((2, 9)),
            *[v(a.shape, a.dtype) for a in (grad_tokens, mixed, *grads[3:], *grads[:3])],
        ],
        compiler_params=pltpu.CompilerParams(vmem_limit_bytes=VMEM_BYTES),
    )(mixed, grad_tokens, *grads, gn)
    if stride > 1:

        def empty(a):
            return lax.psum_scatter(
                a, "seq", scatter_dimension=max(a.ndim - 2, 1), tiled=True, axis_index_groups=blocks
            )

        grads = [empty(a) for a in grads]
    grads[2] = grads[2].transpose(0, 2, 1, 3)
    return (mixed, grad_tokens, *grads)


VMEM_BYTES = 62 << 20


def solution(mesh):
    in_specs = (
        P(None, "seq", None),
        P(),
        P(None, "seq"),
        P(None, "seq"),
        P(None, "seq", None, "mp"),
        P(None, "seq", "mp"),
        P(None, "seq", "mp"),
        P(None, "seq", "mp"),
        P(None, "seq", "mp"),
        P(None, "seq", None),
    )
    out_specs = (
        P(None, "seq", None),
        P(None, "seq", None),
        P(None, "seq"),
        P(None, "seq"),
        P(None, "seq", None, "mp"),
        P(None, "seq", "mp"),
        P(None, "seq", "mp"),
        P(None, "seq", "mp"),
        P(None, "seq", "mp"),
    )
    return jax.shard_map(shards, mesh=mesh, in_specs=in_specs, out_specs=out_specs, check_vma=False)
```
